32 devices in a mesh: dp: 8 (over z, y), lab: 4 (over x, core).
Axes of the slice: x: 2, y: 2, z: 4, core: 2. Of those that a mesh axis runs over, the one named last changes fastest.
Arguments:
- frames_in: bfloat16 [64, 64, 512], P(('dp', 'lab')), may hold values from -6 to 6
- predictor: bfloat16 [64, 4, 16, 640], P('dp', None, 'lab'), may hold values from -6 to 6
- seg_lengths: int32 [64, 4], P('dp'), may hold values from 1 to 32, 64 in all within a row
- label_counts: int32 [64, 4], P('dp'), may hold values from 1 to 15, 32 in all within a row
- label_ids: int32 [64, 4, 16], P('dp', None, 'lab'), may hold values from 0 to 1023
- gain_ffn: bfloat16 [512], P('dp'), may hold values from 0.5 to 1.5
- w_ffn_in: bfloat16 [512, 2048], P(None, 'dp'), may hold values from -0.25 to 0.25
- w_ffn_out: bfloat16 [2048, 512], P('dp'), may hold values from -0.125 to 0.125
- gain_att: bfloat16 [512], P('dp'), may hold values from 0.5 to 1.5
- w_qkv: bfloat16 [512, 1536], P(None, 'dp'), may hold values from -0.25 to 0.25
- w_att_out: bfloat16 [512, 512], P('dp'), may hold values from -1 to 1
- gain_conv: bfloat16 [512], P('dp'), may hold values from 0.5 to 1.5
- w_point_in: bfloat16 [512, 1024], P(None, 'dp'), may hold values from -0.25 to 0.25
- w_depth: bfloat16 [9, 512], P(None, 'dp'), may hold values from -2 to 2
- gain_depth: bfloat16 [512], P('dp'), may hold values from 0.5 to 1.5
- w_point_out: bfloat16 [512, 512], P('dp'), may hold values from -0.25 to 0.25
- gain_out: bfloat16 [512], P('dp'), may hold values from 0.5 to 1.5
- w_enc: bfloat16 [512, 640], P(None, 'dp'), may hold values from -0.25 to 0.25
- w_pred: bfloat16 [640, 640], P(None, 'dp'), may hold values from -0.25 to 0.25
- bias_joint: bfloat16 [640], P('dp'), may hold values from -3 to 3
- w_joint_out: bfloat16 [640, 1030], P('dp'), may hold values from -0.5 to 0.5
- bias_out: bfloat16 [1030], replicated, may hold values from -5 to 5
Outputs:
- loss_frame: float32 [64, 4], P('dp')
- encoded: bfloat16 [64, 64, 512], P(('dp', 'lab'))
- grad_frames: float32 [64, 64, 512], P(('dp', 'lab'))
- grad_predictor: float32 [64, 4, 16, 640], P('dp', None, 'lab')
- grad_gain_ffn: float32 [512], P('dp')
- grad_w_ffn_in: float32 [512, 2048], P(None, 'dp')
- grad_w_ffn_out: float32 [2048, 512], P('dp')
- grad_gain_att: float32 [512], P('dp')
- grad_w_qkv: float32 [512, 1536], P(None, 'dp')
- grad_w_att_out: float32 [512, 512], P('dp')
- grad_gain_conv: float32 [512], P('dp')
- grad_w_point_in: float32 [512, 1024], P(None, 'dp')
- grad_w_depth: float32 [9, 512], P(None, 'dp')
- grad_gain_depth: float32 [512], P('dp')
- grad_w_point_out: float32 [512, 512], P('dp')
- grad_gain_out: float32 [512], P('dp')
- grad_w_enc: float32 [512, 640], P(None, 'dp')
- grad_w_pred: float32 [640, 640], P(None, 'dp')
- grad_bias_joint: float32 [640], P('dp')
- grad_w_joint_out: float32 [640, 1030], P('dp')
- grad_bias_out: float32 [1030], replicated
The draws below stay inside these ranges and needn't reach their ends.
Inputs may be any that keep to these rules, and one draw needn't show every extreme that they name: `seg_lengths`: the 4 lengths of a row sum to 64; in every row one utterance has 32 frames. `label_counts`: the 4 counts of a row sum to 32; in every row one utterance has 15 labels. `label_ids`: ids past an utterance's label count are drawn too and do not count; the blank never appears.
All inputs are finite; a program needn't handle non-finite values.
Results may differ from the reference program's by a relative error of at most 0.025.
Values may be sent and summed in bfloat16 or wider, within the bound.
A program may use at most 128 MiB of HBM per device.

```python
import math
import jax
import jax.numpy as jnp
import numpy as np
from jax import lax

D = 512
H = 8
HD = 64
FF = 2048
KW = 9
J = 640
V = 1025
OUT = 1030
ROW_FR = 64
SEG_MAX = 32
SEGS = 4
ULAB = 16
LAB_ROW = 32
ROWS = 64


def place_ends(values, stream_key, smallest, high):
    longest = values.shape.index(max(values.shape))
    spots = []
    for shift in (0, 1):
        where = [jax.random.randint(jax.random.fold_in(stream_key, axis), (), 0, length) for axis, length in enumerate(values.shape)]
        where[longest] = (where[longest] + shift) % values.shape[longest]
        spots.append(tuple(where))
    return values.at[spots[0]].set(smallest).at[spots[1]].set(high)


def steps_of(rng, extent, cuts, smallest, high):
    level, own = 1.0, jax.random.fold_in(rng, 6)
    for dim, blocks in cuts:
        draws = jnp.exp(jax.random.uniform(jax.random.fold_in(own, dim), (blocks,), jnp.float32, smallest / len(cuts), high / len(cuts)))
        level = level * jnp.repeat(draws, extent[dim] // blocks).reshape([-1 if axis == dim else 1 for axis in range(len(extent))])
    return level


def split_up(count, total, limit, skew):
    loads = [(1 << 20) // math.isqrt(standing ** skew) + 1 for standing in range(2, count + 1)]
    surplus, holding = total - limit - (count - 1), [1] * (count - 1)
    while surplus > 0:
        candidates = [i for i in range(count - 1) if holding[i] < limit]
        pool, budget = sum([loads[i] for i in candidates]), surplus
        for i in candidates:
            addition = min(limit - holding[i], max(1, budget * loads[i] // pool), surplus)
            holding[i] = holding[i] + addition
            surplus = surplus - addition
    return np.array([limit] + holding)


def uneven_parts(rng, amount, total, reach, skew):
    if amount == 2:
        one = jax.random.randint(rng, (), max(1, total - reach), min(reach, total - 1) + 1)
        return jnp.stack([one, total - one])
    tallies = jnp.asarray(split_up(amount, total, reach, skew), jnp.int32)
    twos = (amount - 1) // 2
    source_of, sink = tallies[1:1 + 2 * twos:2], tallies[2:2 + 2 * twos:2]
    margin = jnp.minimum(source_of - 1, reach - sink)
    moved = jax.random.randint(jax.random.fold_in(rng, 1), (twos,), 0, 1 << 20) % (margin + 1)
    tallies = tallies.at[1:1 + 2 * twos:2].set(source_of - moved).at[2:2 + 2 * twos:2].set(sink + moved)
    return tallies[jax.random.permutation(jax.random.fold_in(rng, 2), amount)]


def normal_values(key, shape, deviation, most, cuts=(), held_as=jnp.bfloat16):
    entries = deviation * jax.random.normal(key, shape, jnp.float32)
    if cuts:
        entries = entries * steps_of(key, shape, cuts, -0.22, 0.18)
    return jnp.clip(entries, -most, most).astype(held_as)


def setup_inputs(seed: int = 0) -> dict:
    key_of = jax.random.split(jax.random.key(seed), 23)
    frames_in = normal_values(key_of[0], (ROWS, ROW_FR, D), 1.0, 6.0, ((0, 32),))
    predictor = normal_values(key_of[1], (ROWS, SEGS, ULAB, J), 1.0, 6.0, ((0, 8), (2, 4)))
    seg_lengths = jax.vmap(lambda own: uneven_parts(own, SEGS, ROW_FR, SEG_MAX, 2))(jax.random.split(key_of[2], ROWS)).reshape((ROWS, SEGS)).astype(jnp.int32)
    label_counts = jax.vmap(lambda own: uneven_parts(own, SEGS, LAB_ROW, ULAB - 1, 1))(jax.random.split(key_of[3], ROWS)).reshape((ROWS, SEGS)).astype(jnp.int32)
    label_ids = place_ends(jax.random.randint(key_of[4], (ROWS, SEGS, ULAB), 0, V - 1), jax.random.fold_in(key_of[4], 1), 0, (V - 1) - 1).astype(jnp.int32)
    gain_ffn = jnp.clip(1.0 + 0.1 * jax.random.normal(key_of[5], (D,), jnp.float32), 0.5, 1.5).astype(jnp.bfloat16)
    w_ffn_in = normal_values(key_of[6], (D, FF), D ** -0.5, 0.25, ((1, 8),))
    w_ffn_out = normal_values(key_of[7], (FF, D), FF ** -0.5, 0.125, ((0, 8),))
    gain_att = jnp.clip(1.0 + 0.1 * jax.random.normal(key_of[8], (D,), jnp.float32), 0.5, 1.5).astype(jnp.bfloat16)
    w_qkv = normal_values(key_of[9], (D, 3 * D), D ** -0.5, 0.25, ((1, 8),))
    w_att_out = normal_values(key_of[10], (D, D), (D // 16) ** -0.5, 1.0, ((0, 8),))
    gain_conv = jnp.clip(1.0 + 0.1 * jax.random.normal(key_of[11], (D,), jnp.float32), 0.5, 1.5).astype(jnp.bfloat16)
    w_point_in = normal_values(key_of[12], (D, 2 * D), D ** -0.5, 0.25, ((1, 8),))
    w_depth = normal_values(key_of[13], (KW, D), KW ** -0.5, 2.0, ((1, 8),))
    gain_depth = jnp.clip(1.0 + 0.1 * jax.random.normal(key_of[14], (D,), jnp.float32), 0.5, 1.5).astype(jnp.bfloat16)
    w_point_out = normal_values(key_of[15], (D, D), D ** -0.5, 0.25, ((0, 8),))
    gain_out = jnp.clip(1.0 + 0.1 * jax.random.normal(key_of[16], (D,), jnp.float32), 0.5, 1.5).astype(jnp.bfloat16)
    w_enc = normal_values(key_of[17], (D, J), D ** -0.5, 0.25, ((1, 8),))
    w_pred = normal_values(key_of[18], (J, J), J ** -0.5, 0.25, ((1, 8),))
    bias_joint = normal_values(key_of[19], (J,), 0.5, 3.0, ((0, 8),))
    w_joint_out = normal_values(key_of[20], (J, OUT), (J // 4) ** -0.5, 0.5, ((0, 8),))
    bias_out = normal_values(key_of[21], (OUT,), 1.0, 5.0)
    return {"frames_in": frames_in, "predictor": predictor, "seg_lengths": seg_lengths, "label_counts": label_counts, "label_ids": label_ids, "gain_ffn": gain_ffn, "w_ffn_in": w_ffn_in, "w_ffn_out": w_ffn_out, "gain_att": gain_att, "w_qkv": w_qkv, "w_att_out": w_att_out, "gain_conv": gain_conv, "w_point_in": w_point_in, "w_depth": w_depth, "gain_depth": gain_depth, "w_point_out": w_point_out, "gain_out": gain_out, "w_enc": w_enc, "w_pred": w_pred, "bias_joint": bias_joint, "w_joint_out": w_joint_out, "bias_out": bias_out}


epsilon = 1e-05
very_low = -100000.0
highest = lax.Precision.HIGHEST

@jax.custom_vjp
def low(v):
    return lax.optimization_barrier(v.astype(jnp.bfloat16)).astype(jnp.float32)

@jax.custom_vjp
def low_back(v):
    return v

def low_keep(v):
    return (low(v), None)

def low_pass(kept, grad):
    return (grad,)

def back_keep(v):
    return (v, None)

def back_low(kept, grad):
    return (low(grad),)
low.defvjp(low_keep, low_pass)
low_back.defvjp(back_keep, back_low)

def matmul(first_op, second_op):
    return jnp.dot(first_op, second_op, precision=highest, preferred_element_type=jnp.float32)

def log_total(values, along):
    largest = lax.optimization_barrier(jnp.max(values, axis=along, keepdims=True))
    return jnp.squeeze(largest, along) + jnp.log(lax.optimization_barrier(jnp.sum(jnp.exp(values - largest), axis=along)))

def layer_norm(inputs, gain_vec):
    centre = inputs - lax.optimization_barrier(jnp.mean(inputs, axis=-1, keepdims=True))
    spread = lax.optimization_barrier(jnp.mean(centre * centre, axis=-1, keepdims=True))
    return centre * lax.rsqrt(spread + epsilon) * gain_vec

def softmax(scores):
    largest = lax.optimization_barrier(jnp.max(scores, axis=-1, keepdims=True))
    weights = jnp.exp(scores - largest)
    return weights / lax.optimization_barrier(jnp.sum(weights, axis=-1, keepdims=True))

def segments(lengths, frames):
    seg_ends = jnp.cumsum(lengths, axis=-1).astype(jnp.int32)
    starts = (seg_ends - lengths).astype(jnp.int32)
    position = jnp.arange(frames, dtype=jnp.int32)
    passed = position[:, None] >= seg_ends[..., None, :]
    seg_index = lax.optimization_barrier(jnp.sum(passed.astype(jnp.int32), axis=-1)).astype(jnp.int32)
    member = seg_index[..., None] == jnp.arange(lengths.shape[-1], dtype=jnp.int32)
    seg_start = lax.optimization_barrier(jnp.sum(jnp.where(member, starts[..., None, :], 0), axis=-1)).astype(jnp.int32)
    seg_stop = lax.optimization_barrier(jnp.sum(jnp.where(member, seg_ends[..., None, :], 0), axis=-1)).astype(jnp.int32)
    return (seg_index, member, position - seg_start, seg_stop - position)

def conv_piece(conv_pre, w_depth, gain_depth, seg_index):
    width_in = w_depth.shape[1]
    frames = conv_pre.shape[0]
    half_taps = w_depth.shape[0] // 2
    gated = conv_pre[:, :width_in] * jax.nn.sigmoid(conv_pre[:, width_in:])
    padded = jnp.pad(gated, ((half_taps, half_taps), (0, 0)))
    seg_pad = jnp.pad(seg_index, (half_taps, half_taps), constant_values=-1)
    summed = jnp.zeros_like(gated)
    for tap_index in range(w_depth.shape[0]):
        same_seg = (seg_pad[tap_index:tap_index + frames] == seg_index).astype(gated.dtype)
        summed = summed + w_depth[tap_index] * padded[tap_index:tap_index + frames] * same_seg[:, None]
    return jax.nn.silu(layer_norm(summed, gain_depth))

def conformer(inputs, seg_index, params):
    gain_ffn, w_ffn_in, w_ffn_out, gain_att, w_qkv, w_att_out, gain_conv, w_point_in, w_depth, gain_depth, w_point_out, gain_out = params[:12]
    frames = inputs.shape[0]
    ffn_in = low(layer_norm(inputs, gain_ffn))
    ffn_pre = low_back(matmul(ffn_in, w_ffn_in))
    ffn_act = low(jax.nn.silu(ffn_pre))
    after_ffn = inputs + 0.5 * low_back(matmul(ffn_act, w_ffn_out))
    att_in = low(layer_norm(after_ffn, gain_att))
    qkv_all = low(low_back(matmul(att_in, w_qkv))).reshape(frames, 3, H, HD)
    queries, keys, values = (qkv_all[:, 0], qkv_all[:, 1], qkv_all[:, 2])
    scores = low_back(jnp.einsum('thd,shd->hts', queries, keys, precision=highest) * HD ** (-0.5))
    same_seg = seg_index[:, None] == seg_index[None, :]
    probs = low(softmax(jnp.where(same_seg[None], scores, very_low)))
    context = low(low_back(jnp.einsum('hts,shd->thd', probs, values, precision=highest))).reshape(frames, H * HD)
    after_att = after_ffn + low_back(matmul(context, w_att_out))
    conv_in = low(layer_norm(after_att, gain_conv))
    conv_pre = low_back(matmul(conv_in, w_point_in))
    conv_act = low(conv_piece(conv_pre, w_depth, gain_depth, seg_index))
    after_conv = after_att + low_back(matmul(conv_act, w_point_out))
    return layer_norm(after_conv, gain_out)

def joint_terms(encoded, pred_rows, member, frame_labels, params):
    w_enc, w_pred, bias_joint, w_joint_out, bias_out = params[12:]
    joint_width = pred_rows.shape[-1]
    enc_proj = low(low_back(matmul(low(encoded), w_enc)))
    pred_proj = low_back(matmul(pred_rows.reshape(-1, joint_width), w_pred) + bias_joint).reshape(pred_rows.shape)
    per_frame = jnp.einsum('ts,suj->tuj', member.astype(jnp.float32), pred_proj, precision=highest)
    hidden = low(jnp.tanh(enc_proj[:, None, :] + per_frame))
    logits = low_back(jnp.einsum('tuj,jo->tuo', hidden, w_joint_out, precision=highest) + bias_out)
    tokens = logits[..., :V]
    durations = logits[..., V:]
    tok_lp = tokens - log_total(tokens, -1)[..., None]
    dur_lp = durations - log_total(durations, -1)[..., None]
    label_lp = jnp.take_along_axis(tok_lp, frame_labels[..., None], axis=-1)[..., 0]
    return (label_lp[..., None] + dur_lp, tok_lp[..., V - 1:V] + dur_lp[..., 1:])

def lattice(emit_lp, blank_lp, offset, remain, target, member):
    row_count, frames, label_width, dur_count = emit_lp.shape
    label_index = jnp.arange(label_width, dtype=jnp.int32)
    first_col = jnp.where(label_index == 0, 0.0, very_low).astype(emit_lp.dtype)

    def advance(incoming, pieces):
        emit_now, blank_now, offset_now, remain_now = pieces
        arrived = jnp.where((offset_now == 0)[:, None], first_col[None, :], incoming[0])
        columns = [arrived[:, 0]]
        for label_pos in range(1, label_width):
            columns.append(jnp.logaddexp(arrived[:, label_pos], columns[-1] + emit_now[:, label_pos - 1, 0]))
        alpha_now = jnp.stack(columns, axis=1)
        filler = jnp.full((row_count, 1), very_low, emit_lp.dtype)
        pending = []
        for duration in range(1, dur_count):
            emitted = jnp.concatenate([filler, alpha_now[:, :-1] + emit_now[:, :-1, duration]], axis=1)
            pushed = jnp.logaddexp(emitted, alpha_now + blank_now[:, :, duration - 1])
            pushed = jnp.where((duration <= remain_now - 1)[:, None], pushed, very_low)
            arriving = incoming[duration] if duration < dur_count - 1 else jnp.full_like(pushed, very_low)
            pending.append(jnp.logaddexp(arriving, pushed))
        return (jnp.stack(pending), alpha_now)
    initial = jnp.full((dur_count - 1, row_count, label_width), very_low, emit_lp.dtype)
    pieces = (emit_lp.transpose(1, 0, 2, 3), blank_lp.transpose(1, 0, 2, 3), offset.T, remain.T)
    _, alphas = lax.scan(advance, initial, pieces)
    alphas = alphas.transpose(1, 0, 2)
    choose = jnp.arange(1, dur_count, dtype=jnp.int32) == remain[..., None]
    end_lp = lax.optimization_barrier(jnp.sum(jnp.where(choose[..., None, :], blank_lp, 0.0), axis=-1))
    finish = (label_index == target[..., None]) & (remain <= dur_count - 1)[..., None]
    closing = jnp.where(finish, alphas + end_lp, very_low)
    frame_total = log_total(closing, -1)
    return log_total(jnp.where(member, frame_total[..., None], very_low), 1)

def reference(frames_in, predictor, seg_lengths, label_counts, label_ids, gain_ffn, w_ffn_in, w_ffn_out, gain_att, w_qkv, w_att_out, gain_conv, w_point_in, w_depth, gain_depth, w_point_out, gain_out, w_enc, w_pred, bias_joint, w_joint_out, bias_out):
    params = tuple((array_in.astype(jnp.float32) for array_in in (gain_ffn, w_ffn_in, w_ffn_out, gain_att, w_qkv, w_att_out, gain_conv, w_point_in, w_depth, gain_depth, w_point_out, gain_out, w_enc, w_pred, bias_joint, w_joint_out, bias_out)))
    seg_index, member, offset, remain = segments(seg_lengths, ROW_FR)
    frame_labels = lax.optimization_barrier(jnp.sum(jnp.where(member[..., None], label_ids[:, None, :, :], 0), axis=2)).astype(jnp.int32)
    target = lax.optimization_barrier(jnp.sum(jnp.where(member, label_counts[:, None, :], 0), axis=-1)).astype(jnp.int32)

    def objective(frames_f, pred_f, *weights):

        def one_row(pieces):
            frames_row, pred_row, seg_row, member_row, labels_row = pieces
            encoded_row = conformer(frames_row, seg_row, weights)
            emit_row, blank_row = joint_terms(encoded_row, pred_row, member_row, labels_row, weights)
            return (encoded_row, emit_row, blank_row)
        encoded_all, emit_lp, blank_lp = lax.map(jax.checkpoint(one_row), (frames_f, pred_f, seg_index, member, frame_labels))
        log_norm = lattice(emit_lp, blank_lp, offset, remain, target, member)
        return (-jnp.sum(log_norm), (encoded_all, log_norm))
    total_loss, backward, aux_out = jax.vjp(objective, frames_in.astype(jnp.float32), predictor.astype(jnp.float32), *params, has_aux=True)
    encoded_all, log_norm = aux_out
    grad_all = backward(jnp.ones_like(total_loss))
    loss_frame = -log_norm / seg_lengths.astype(jnp.float32)
    return (loss_frame, encoded_all.astype(jnp.bfloat16), grad_all[0], grad_all[1], grad_all[2], grad_all[3], grad_all[4], grad_all[5], grad_all[6], grad_all[7], grad_all[8], grad_all[9], grad_all[10], grad_all[11], grad_all[12], grad_all[13], grad_all[14], grad_all[15], grad_all[16], grad_all[17], grad_all[18])
```

```python
import functools

import jax
import jax.numpy as jnp
from jax import lax
from jax.experimental import pallas as pl
from jax.experimental.pallas import tpu as pltpu
from jax.sharding import PartitionSpec as P


MESH = pl.DeviceIdType.MESH
F32 = jnp.float32
BF = jnp.bfloat16
TILE = 16


def ring_place(dp, n):
    odd = dp % 2
    return (1 - odd) * (dp // 2) + odd * (n - 1 - dp // 2)


def ring_device(place, n):
    place = (place + 2 * n) % n
    high = place // (n // 2)
    return (1 - high) * (2 * place) + high * (2 * (n - 1 - place) + 1)


def x_rows(rows, share):
    tiles = rows // TILE
    return min(tiles // 2, int(tiles * share + 0.5)) * TILE


class Where:
    def __init__(self, n):
        self.n = n
        self.dp = lax.axis_index("dp")
        self.lab = lax.axis_index("lab")
        self.core = self.lab % 2
        self.side = self.lab // 2
        self.place = ring_place(self.dp, n)
        self.right = (ring_device(self.place + 1, n), self.lab)
        self.left = (ring_device(self.place - 1, n), self.lab)
        self.twin = (self.dp, self.side * 2 + 1 - self.core)
        self.across = (self.dp, (1 - self.side) * 2 + self.core)
        self.far = (
            ring_device(self.place + 1 - 2 * self.core, n),
            self.lab,
        )

    def at(self, distance):
        return ring_device(self.place + distance, self.n)

    def greet(self):
        barrier = pltpu.get_barrier_semaphore()
        for other in (self.right, self.left, self.twin, self.across):
            pl.semaphore_signal(barrier, inc=1, device_id=other, device_id_type=MESH)
        pl.semaphore_wait(barrier, 4)


def remote(src, dst, send_sem, recv_sem, device):
    return pltpu.make_async_remote_copy(
        src_ref=src,
        dst_ref=dst,
        send_sem=send_sem,
        recv_sem=recv_sem,
        device_id=device,
        device_id_type=MESH,
    )


class Gather:
    def __init__(self, where, source, target, rows, ring_recv, x_recv, sems):
        self.w, self.source, self.target, self.rows = where, source, target, rows
        self.width = target.shape[1]
        self.half = self.width // 2
        self.cut = x_rows(rows, 0.3)
        self.ring_recv, self.x_recv, self.sems = ring_recv, x_recv, sems
        self.steps = where.n // 2

    def lanes(self):
        return pl.ds(pl.multiple_of(self.w.core * self.half, 128), self.half)

    def rows_at(self, shard, offset, size):
        base = shard * self.rows if shard is not None else 0
        return pl.ds(pl.multiple_of(base + offset, TILE), size)

    def ring_part(self, ref, shard):
        return ref.at[self.rows_at(shard, self.w.side * self.cut, self.rows - self.cut), self.lanes()]

    def x_part(self, ref, shard, side):
        return ref.at[self.rows_at(shard, side * (self.rows - self.cut), self.cut), self.lanes()]

    def slot(self, distance):
        return distance + self.steps - 1 if distance < 0 else distance + self.steps - 2

    def hop(self, distance, first):
        w = self.w
        if distance == self.steps:
            shard = w.at((2 * w.core - 1) * (self.steps - 1))
            device = w.far
        else:
            shard = w.at(distance + 1) if distance < 0 else w.at(distance - 1)
            device = w.right if distance < 0 else w.left
        src = self.ring_part(self.source, None) if first else self.ring_part(self.target, shard)
        slot = 2 * self.steps - 2 if distance == self.steps else self.slot(distance)
        remote(src, self.ring_part(self.target, shard), self.sems.at[1], self.ring_recv.at[slot], device).start()

    def own(self):
        pltpu.make_async_copy(
            self.source, self.target.at[self.rows_at(self.w.dp, 0, self.rows), :], self.sems.at[4]
        ).start()

    def arrived(self, distance):
        w = self.w
        shard = w.at(distance)
        slot = 2 * self.steps - 2 if distance == self.steps else self.slot(distance)
        part = self.ring_part(self.target, shard)
        remote(part, part, self.sems.at[1], self.ring_recv.at[slot], w.right).wait_recv()

    def spread(self, distance):
        w = self.w
        shard = w.at(distance)
        slot = 2 * self.steps - 2 if distance == self.steps else self.slot(distance)
        if self.cut:
            part = self.x_part(self.target, shard, w.side)
            remote(part, part, self.sems.at[2], self.x_recv.at[slot], w.across).start()
        part = self.ring_part(self.target, shard)
        remote(part, part, self.sems.at[3], self.sems.at[0], w.twin).start()

    def crossed(self, distance):
        if not self.cut:
            return
        w = self.w
        shard = w.at(distance)
        slot = 2 * self.steps - 2 if distance == self.steps else self.slot(distance)
        part = self.x_part(self.target, shard, 1 - w.side)
        remote(part, part, self.sems.at[2], self.x_recv.at[slot], w.across).wait_recv()
        remote(part, part, self.sems.at[3], self.sems.at[0], w.twin).start()

    def whole(self):
        part = self.target.at[pl.ds(0, (self.w.n - 1) * self.rows), pl.ds(0, self.half)]
        remote(part, part, self.sems.at[3], self.sems.at[0], self.w.twin).wait_recv()
        pltpu.make_async_copy(
            self.source, self.target.at[self.rows_at(self.w.dp, 0, self.rows), :], self.sems.at[4]
        ).wait()

    def drain(self):
        count = self.w.n - 1
        for sem, rows in ((1, self.rows - self.cut), (2, self.cut), (3, self.rows)):
            if rows:
                part = self.target.at[pl.ds(0, count * rows), pl.ds(0, self.half)]
                remote(part, part, self.sems.at[sem], self.sems.at[sem], self.w.twin).wait_send()

    def step(self, s):
        if s == 0:
            self.own()
        if 1 <= s < self.steps:
            self.arrived(-s)
            self.arrived(s)
        if s == self.steps:
            self.arrived(self.steps)
        if s < self.steps - 1:
            self.hop(-s - 1, s == 0)
            self.hop(s + 1, s == 0)
        elif s == self.steps - 1:
            self.hop(self.steps, False)
        if 1 <= s < self.steps:
            self.spread(-s)
            self.spread(s)
        if s == self.steps:
            self.spread(self.steps)
        if 2 <= s <= self.steps:
            self.crossed(-s + 1)
            self.crossed(s - 1)
        if s == self.steps + 1:
            self.crossed(self.steps)


def gather_kernel(n, rows_list, *refs):
    k = len(rows_list)
    sources, targets = refs[:k], refs[k : 2 * k]
    ring_recv, x_recv, sems = refs[2 * k :]
    w = Where(n)
    w.greet()
    parts = [
        Gather(w, sources[i], targets[i], rows_list[i], ring_recv.at[i], x_recv.at[i], sems.at[i])
        for i in range(k)
    ]
    turns = n // 2 + 2
    for tick in range(k + turns - 1):
        for s in range(turns - 1, -1, -1):
            g = tick - s
            if 0 <= g < k:
                parts[g].step(s)
    for part in parts:
        part.whole()
        part.drain()


def gather_all(n, shards):
    k = len(shards)
    rows_list = [s.shape[0] for s in shards]
    return pl.pallas_call(
        functools.partial(gather_kernel, n, rows_list),
        out_shape=[jax.ShapeDtypeStruct((n * s.shape[0], s.shape[1]), s.dtype) for s in shards],
        in_specs=[pl.BlockSpec(memory_space=pltpu.VMEM)] * k,
        out_specs=[pl.BlockSpec(memory_space=pltpu.VMEM)] * k,
        scratch_shapes=[
            pltpu.SemaphoreType.DMA((k, n - 1)),
            pltpu.SemaphoreType.DMA((k, n - 1)),
            pltpu.SemaphoreType.DMA((k, 5)),
        ],
        compiler_params=pltpu.CompilerParams(
            collective_id=0, has_side_effects=True, vmem_limit_bytes=56 * 2**20
        ),
    )(*shards)


class Scatter:
    STAGES = 9

    def __init__(self, where, grads, out, rows, bufs, send, recv):
        self.w, self.grads, self.out, self.rows = where, grads, out, rows
        self.held, self.xbuf, self.rbuf, self.final = bufs
        self.half = grads.shape[1] // 2
        self.cut = x_rows(rows, SHARE_RS)
        self.send, self.recv = send, recv
        self.depth = where.n // 2 - 1
        self.started = []

    def lanes(self, core):
        return pl.ds(pl.multiple_of(core * self.half, 128), self.half)

    def rows_at(self, shard, offset, size):
        return pl.ds(pl.multiple_of(shard * self.rows + offset, TILE), size)

    def go(self, sem, src, dst, device):
        copy = remote(src, dst, self.send.at[sem], self.recv.at[sem], device)
        copy.start()
        self.started.append(copy)

    def got(self, sem, dst):
        remote(dst, dst, self.send.at[sem], self.recv.at[sem], self.w.twin).wait_recv()

    def mine(self, shard):
        return self.held[self.rows_at(shard, self.w.side * self.cut, self.rows - self.cut), :].astype(F32)

    def stage(self, s):
        w, rows, cut, depth = self.w, self.rows, self.cut, self.depth
        n, keep = w.n, self.rows - self.cut
        if s == 0:
            self.go(0, self.grads.at[:, self.lanes(1 - w.core)], self.held, w.twin)
        elif s == 1:
            self.got(0, self.held)

            def add(i, _):
                at = self.rows_at(i, 0, rows)
                self.held[at, :] = (
                    self.held[at, :].astype(F32) + self.grads[at, self.lanes(w.core)].astype(F32)
                ).astype(BF)
                return 0

            lax.fori_loop(0, n, add, 0)
            if cut:
                for i in range(n):
                    src = self.held.at[self.rows_at(i, (1 - w.side) * keep, cut), :]
                    remote(src, self.xbuf.at[i], self.send.at[1], self.recv.at[1], w.across).start()
        elif s == 2:
            if cut:
                self.got(1, self.xbuf)

                def add(i, _):
                    at = self.rows_at(i, w.side * keep, cut)
                    self.held[at, :] = (
                        self.held[at, :].astype(F32) + self.xbuf[i].astype(F32)
                    ).astype(BF)
                    return 0

                lax.fori_loop(0, n, add, 0)
            dest = w.at((2 * w.core - 1) * (depth + 1))
            src = self.held.at[self.rows_at(dest, w.side * cut, keep), :]
            self.go(2, src, self.rbuf.at[2 * depth], w.far_back)
        elif s < 3 + depth:
            hop = s - 3
            for way in (0, 1):
                sign = 1 - 2 * way
                own = self.mine(w.at(sign * (depth - hop)))
                slot = 2 * hop + way
                if hop == 0:
                    if way == 0:
                        self.got(2, self.rbuf.at[2 * depth])
                    far = self.rbuf[2 * depth].astype(F32)
                    pick = w.core if way == 0 else 1 - w.core
                    own = own + jnp.where(pick == 1, far, 0.0)
                    at = 2 * depth + 1 + way
                else:
                    at = slot - 2
                    self.got(3 + at, self.rbuf.at[at])
                    own = own + self.rbuf[at].astype(F32)
                self.rbuf[at] = own.astype(BF)
                self.go(3 + slot, self.rbuf.at[at], self.rbuf.at[slot], w.right if way == 0 else w.left)
        elif s == 3 + depth:
            total = self.mine(w.dp)
            for way in (0, 1):
                at = 2 * depth - 2 + way
                self.got(3 + at, self.rbuf.at[at])
                total = total + self.rbuf[at].astype(F32)
            self.final[0] = total.astype(BF)
            self.go(3 + 2 * depth, self.final.at[0], self.final.at[1], w.across)
        elif s == 4 + depth:
            self.got(3 + 2 * depth, self.final.at[1])
            lanes = self.lanes(w.core)
            own, other = self.final[0].astype(F32), self.final[1].astype(F32)
            if cut:
                first = w.side == 0
                low, high = jnp.where(first, own, other), jnp.where(first, other, own)
                self.out[:cut, lanes] = low[:cut].astype(BF)
                if keep > cut:
                    self.out[cut:keep, lanes] = (low[cut:] + high[: keep - cut]).astype(BF)
                self.out[keep:, lanes] = high[keep - cut :].astype(BF)
            else:
                self.out[:, lanes] = (own + other).astype(BF)
            part = self.out.at[:, lanes]
            self.go(4 + 2 * depth, part, part, w.twin)
        elif s == 5 + depth:
            self.got(4 + 2 * depth, self.out.at[:, self.lanes(1 - w.core)])

    def drain(self):
        for copy in self.started:
            copy.wait_send()
        if self.cut:
            remote(self.xbuf, self.xbuf, self.send.at[1], self.recv.at[1], self.w.across).wait_send()


SHARE_RS = 0.25


def scatter_scratch(n, rows, width, k_index=None):
    half, cut, depth = width // 2, x_rows(rows, SHARE_RS), n // 2 - 1
    return [
        pltpu.VMEM((n * rows, half), BF),
        pltpu.VMEM((n, max(cut, TILE), half), BF),
        pltpu.VMEM((2 * depth + 3, rows - cut, half), BF),
        pltpu.VMEM((2, rows - cut, half), BF),
    ]


def scatter_sems(n, k):
    return [pltpu.SemaphoreType.DMA((k, n + 3)), pltpu.SemaphoreType.DMA((k, n + 3))]


def scatter_kernel(n, rows_list, skew, *refs):
    k = len(rows_list)
    grads, outs = refs[:k], refs[k : 2 * k]
    bufs = refs[2 * k : 2 * k + 4 * k]
    send, recv = refs[6 * k :]
    w = Where(n)
    w.far_back = (ring_device(w.place + 2 * w.core - 1, n), w.lab)
    w.greet()
    parts = [
        Scatter(w, grads[i], outs[i], rows_list[i], bufs[4 * i : 4 * i + 4], send.at[i], recv.at[i])
        for i in range(k)
    ]
    stages = n // 2 + 5
    for tick in range(k + skew * (stages - 1)):
        for s in range(stages - 1, -1, -1):
            g = tick - skew * s
            if 0 <= g < k:
                parts[g].stage(s)
    for part in parts:
        part.drain()


def scatter_all(n, grads, skew=1):
    k = len(grads)
    rows_list = [g.shape[0] // n for g in grads]
    scratch = []
    for g, rows in zip(grads, rows_list):
        scratch += scatter_scratch(n, rows, g.shape[1])
    return pl.pallas_call(
        functools.partial(scatter_kernel, n, rows_list, skew),
        out_shape=[jax.ShapeDtypeStruct((rows, g.shape[1]), BF) for g, rows in zip(grads, rows_list)],
        in_specs=[pl.BlockSpec(memory_space=pltpu.VMEM)] * k,
        out_specs=[pl.BlockSpec(memory_space=pltpu.VMEM)] * k,
        scratch_shapes=scratch + scatter_sems(n, k),
        compiler_params=pltpu.CompilerParams(
            collective_id=1, has_side_effects=True, vmem_limit_bytes=60 * 2**20
        ),
    )(*grads)


LOW = -100000.0
TOK = 1024
KINDS = 7
BIAS_LANE = 6


def mm(a, b):
    return lax.dot_general(a, b, (((1,), (0,)), ((), ())), preferred_element_type=F32)


def mm_t(a, b):
    return lax.dot_general(a, b, (((1,), (1,)), ((), ())), preferred_element_type=F32)


def t_mm(a, b):
    return lax.dot_general(a, b, (((0,), (0,)), ((), ())), preferred_element_type=F32)


def lane_ids(shape):
    return lax.broadcasted_iota(jnp.int32, shape, len(shape) - 1)


def row_ids(shape):
    return lax.broadcasted_iota(jnp.int32, shape, 0)


class Peers:
    def __init__(self):
        self.dp, self.lab = lax.axis_index("dp"), lax.axis_index("lab")
        self.core, self.side = self.lab % 2, self.lab // 2

    def owner(self, j):
        return ((self.side + j // 2) % 2) * 2 + (self.core + j % 2) % 2

    def device(self, j):
        return (self.dp, self.owner(j))


def seg_of(t, ends):
    return sum((t >= e).astype(jnp.int32) for e in ends[:-1])


def pick(seg, values):
    out = values[0]
    for s in range(1, len(values)):
        out = jnp.where(seg == s, values[s], out)
    return out


def scalar_ends(lengths, r, segs):
    ends, total = [], 0
    for s in range(segs):
        total = total + lengths[r, s]
        ends.append(total)
    return ends


def lse_of(terms):
    top = functools.reduce(jnp.maximum, terms)
    return top, functools.reduce(jnp.add, [jnp.exp(v - top) for v in terms])


def lattice(peers, lengths, counts, terms, skewed, hist, grads, loss, dims):
    frames, rows, segs, own_u, labs = dims
    wide = (frames, 128)
    lane = lane_ids(wide)
    group = rows * own_u
    j, row, u = lane % own_u, (lane % group) // own_u, (lane // group) * own_u + lane % own_u
    t = row_ids(wide)
    all_ends = [scalar_ends(lengths, r, segs) for r in range(rows)]

    def per_lane(values):
        out = jnp.zeros(wide, jnp.int32)
        for r in range(rows):
            out = jnp.where(row == r, values[r], out)
        return out

    ends = [per_lane([all_ends[r][s] for r in range(rows)]) for s in range(segs)]
    labels_in = [per_lane([counts[r, s] for r in range(rows)]) for s in range(segs)]
    seg = seg_of(t, ends)
    stop = pick(seg, ends)
    begin = pick(seg, [jnp.zeros(wide, jnp.int32)] + ends[:-1])
    target = pick(seg, labels_in)
    remain, first = stop - t, t == begin

    kinds = []
    per_vreg = 128 // group
    for k in range(KINDS):
        value = None
        for dev in range(labs):
            part = terms[dev, :, (k // per_vreg) * 128 : (k // per_vreg) * 128 + 128]
            shift = (dev - k % per_vreg) * group % 128
            part = pltpu.roll(part, shift, 1) if shift else part
            value = part if value is None else jnp.where(lane // group == dev, part, value)
        kinds.append(value)
    blank_lp, durs, label_lp = kinds[0], kinds[1:6], kinds[6]
    last_u = own_u * labs - 1
    emit, blank, blank_raw = [], [None], [None]
    for d in range(5):
        ok = (u < last_u) & (d <= remain - 1)
        emit.append(jnp.where(ok, label_lp + durs[d], LOW))
        if d:
            blank_raw.append(blank_lp + durs[d])
            blank.append(jnp.where(d <= remain - 1, blank_raw[d], LOW))
    final = (u == target) & (remain <= 4)
    closing = jnp.zeros(wide, F32)
    for d in range(1, 5):
        closing = jnp.where(remain == d, blank_raw[d], closing)
    closing = jnp.where(final, closing, LOW)
    start = jnp.where(first & (u == 0), 0.0, LOW)

    tall = frames + 16
    tall_u = (lane_ids((tall, 128)) // group) * own_u + lane_ids((tall, 128)) % own_u
    tall_j = lane_ids((tall, 128)) % own_u
    pad = jnp.full((16, 128), LOW, F32)

    def skew(value):
        value = jnp.concatenate([value, pad], axis=0)
        for bit in (1, 2, 4, 8):
            value = jnp.where((tall_u // bit) % 2 == 1, pltpu.roll(value, bit, 0), value)
        return value

    def unskew(value):
        for bit in (1, 2, 4, 8):
            value = jnp.where((tall_u // bit) % 2 == 1, pltpu.roll(value, tall - bit, 0), value)
        return value[:frames]

    up = 128 - (group - own_u + 1)

    def next_up(value, jj):
        return jnp.where(jj == 0, pltpu.roll(value, group - own_u + 1, 1), pltpu.roll(value, 1, 1))

    def next_down(value, jj):
        return jnp.where(jj == own_u - 1, pltpu.roll(value, up, 1), pltpu.roll(value, 127, 1))

    lead = jnp.full((8, 128), LOW, F32)

    def keep(i, value):
        skewed[i, 0:8, :] = lead
        skewed[i, 8 : 8 + tall, :] = value

    for d in range(1, 5):
        keep(d - 1, skew(blank[d]))
    for d in range(5):
        value = skew(emit[d])
        keep(4 + d, value)
        keep(9 + d, next_up(value, tall_j))
    keep(14, skew(start))
    keep(15, skew(closing))
    waves = frames + last_u
    one_j = lane_ids((1, 128)) % own_u
    low_row = skewed[0, 0:1, :]

    def at(i, w):
        return skewed[i, pl.ds(w + 8, 1), :]

    def combine(old, near):
        top_old, sum_old = lse_of(old)
        top = functools.reduce(jnp.maximum, near, top_old)
        total = sum_old * jnp.exp(top_old - top)
        for v in near:
            total = total + jnp.exp(v - top)
        return top + jnp.log(total)

    def wave(i, carry):
        a, ra, b, rb = carry
        old = [at(14, i)]
        for d in range(2, 5):
            old.append(a[d - 1] + at(d - 1, i - d))
        for d in range(2, 6):
            old.append(ra[d - 1] + at(8 + d, i - d))
        new_a = combine(old, [a[0] + at(0, i - 1), ra[0] + at(9, i - 1)])
        back = waves - 1 - i
        old = [at(15, back)]
        for d in range(2, 5):
            old.append(b[d - 1] + at(d - 1, back))
        for d in range(2, 6):
            old.append(rb[d - 1] + at(3 + d, back))
        new_b = combine(old, [b[0] + at(0, back), rb[0] + at(4, back)])
        hist[0, pl.ds(i, 1), :] = new_a
        hist[1, pl.ds(back, 1), :] = new_b
        return (
            (new_a,) + a[:-1],
            (next_up(new_a, one_j),) + ra[:-1],
            (new_b,) + b[:-1],
            (next_down(new_b, one_j),) + rb[:-1],
        )

    hist[...] = jnp.full(hist.shape, LOW, F32)
    lax.fori_loop(
        0, waves, wave, ((low_row,) * 4, (low_row,) * 5, (low_row,) * 4, (low_row,) * 5)
    )
    alpha, beta = unskew(hist[0]), unskew(hist[1])
    ahead = next_down(beta, j)
    norm = jnp.zeros(wide, F32)
    heads = jnp.where(first & (u == 0), beta, 0.0)
    for s in range(segs):
        value = jnp.sum(jnp.where(seg == s, heads, 0.0), axis=0, keepdims=True)
        step = 1
        while step < own_u:
            value = value + pltpu.roll(value, step, 1)
            step *= 2
        step = group
        while step < 128:
            value = value + pltpu.roll(value, step, 1)
            step *= 2
        norm = jnp.where(seg == s, value, norm)
        length = ends[s] - (ends[s - 1] if s else 0)
        loss[pl.ds(s, 1), :] = -value / length[:1].astype(F32)
    base = alpha - norm
    total_a, total_b = None, None
    for d in range(5):
        there = pltpu.roll(ahead, frames - d, 0) if d else ahead
        g = -jnp.exp(base + emit[d] + there)
        total_a = g if d == 0 else total_a + g
        if d:
            gb = -jnp.exp(base + blank[d] + pltpu.roll(beta, frames - d, 0))
            gb = gb - jnp.exp(jnp.where(final & (remain == d), base + blank_raw[d], LOW))
            total_b = gb if d == 1 else total_b + gb
            g = g + gb
        grads[1 + d] = g
    grads[0] = total_b
    grads[6] = total_a


def joint_kernel(
    dims,
    enc_own, pred, lengths, counts, labels, predx, tok, tail, bias,
    g_enc, g_predictor, g_pack, g_mix, g_bias, loss,
    enc_all, proj, hid, slope, prob, prob_tail, mine, terms, skewed, hist, grads, g_pred, part, came,
    send, recv,
):
    frames, rows, segs, own_u, labs = dims
    micro = rows // labs
    peers = Peers()
    barrier = pltpu.get_barrier_semaphore()
    for j in range(1, labs):
        pl.semaphore_signal(barrier, inc=1, device_id=peers.device(j), device_id_type=MESH)
    pl.semaphore_wait(barrier, labs - 1)
    width = enc_own.shape[-1]
    span = own_u * frames
    own_rows = pl.ds(peers.lab * micro, micro)

    def enc_copy(j, source):
        return remote(enc_own, enc_all.at[pl.ds(source * micro, micro)], send.at[0, j], recv.at[0, j], peers.device(j))

    for j in range(1, labs):
        enc_copy(j, peers.lab).start()
    enc_all[own_rows] = enc_own[...]
    proj[...] = mm_t(pred[...], predx[...])
    lane_t = lane_ids((frames, 128))
    lane_w = lane_ids((frames, TOK))
    group = rows * own_u
    per_vreg = 128 // group

    def row_of(k):
        return peers.owner(k // micro) * micro + k % micro

    def forward(k, _):
        for j in range(1, labs):
            @pl.when(k == j * micro)
            def _():
                enc_copy(j, peers.owner(j)).wait_recv()
        r = row_of(k)
        seg = seg_of(row_ids((frames, width)), scalar_ends(lengths, r, segs))
        enc = enc_all[r].astype(F32)
        for u in range(own_u):
            per_frame = pick(
                seg, [proj[pl.ds(r * segs * own_u + s * own_u + u, 1), :] for s in range(segs)]
            )
            value = jnp.tanh(enc + per_frame)
            hid[r, u * frames : (u + 1) * frames, :] = value.astype(BF)
            slope[r, u * frames : (u + 1) * frames, :] = (1.0 - value * value).astype(BF)
        h = hid[r]
        end = mm(h, tail[...]) + bias[:, TOK:]
        wide = mm(h, tok[...]) + bias[:, :TOK]
        seg_l = seg_of(row_ids((frames, TOK)), scalar_ends(lengths, r, segs))
        for u in range(own_u):
            logit, last = wide[u * frames : (u + 1) * frames], end[u * frames : (u + 1) * frames]
            top = jnp.maximum(jnp.max(logit, axis=1, keepdims=True), last[:, 0:1])
            top_dur = jnp.max(
                jnp.where((lane_t >= 1) & (lane_t <= 5), last, -jnp.inf), axis=1, keepdims=True
            )
            is_tok = lane_t == 0
            e_last = jnp.where(
                lane_t < 6, jnp.exp(jnp.where(lane_t < 6, last - jnp.where(is_tok, top, top_dur), 0.0)), 0.0
            )
            e = jnp.exp(logit - top)
            total = jnp.sum(e, axis=1, keepdims=True) + e_last[:, 0:1]
            total_dur = jnp.sum(jnp.where(is_tok, 0.0, e_last), axis=1, keepdims=True)
            prob[r, u * frames : (u + 1) * frames, :] = (e * (1.0 / total)).astype(BF)
            prob_tail[r, u * frames : (u + 1) * frames, :] = e_last * (1.0 / jnp.where(is_tok, total, total_dur))
            norm_tok, norm_dur = top + jnp.log(total), top_dur + jnp.log(total_dur)
            label = pick(seg_l, [labels[r, s * own_u + u] for s in range(segs)])
            at_label = jnp.sum(jnp.where(lane_w == label, logit, 0.0), axis=1, keepdims=True) - norm_tok
            lp = last - jnp.where(is_tok, norm_tok, norm_dur)
            for kind in range(KINDS):
                column = at_label if kind == 6 else lp[:, kind : kind + 1]
                cols = slice((kind // per_vreg) * 128, (kind // per_vreg) * 128 + 128)
                place = (kind % per_vreg) * group + r * own_u + u
                mine[:, cols] = jnp.where(lane_t == place, column, mine[:, cols])
        return 0

    mine[...] = jnp.zeros(mine.shape, F32)
    lax.fori_loop(0, rows, forward, 0)
    terms[peers.lab] = mine[...]

    def term_copy(j, source):
        return remote(mine, terms.at[source], send.at[1, j], recv.at[1, j], peers.device(j))

    for j in range(1, labs):
        term_copy(j, peers.lab).start()
    for j in range(1, labs):
        term_copy(j, peers.owner(j)).wait_recv()
    lattice(peers, lengths, counts, terms, skewed, hist, grads, loss, dims)

    def part_copy(j):
        return remote(part.at[j], came.at[j], send.at[2, j], recv.at[2, j], peers.device(j))

    def backward(i, sums):
        k = rows - 1 - i
        r = row_of(k)
        shift = (256 - peers.lab * group - r * own_u) % 128
        rolled = [pltpu.roll(grads[kind], shift, 1) for kind in range(KINDS)]
        seg_l = seg_of(row_ids((frames, TOK)), scalar_ends(lengths, r, segs))
        sum_tok, sum_tail = sums
        for u in range(own_u):
            at = slice(u * frames, (u + 1) * frames)
            a, b = rolled[6][:, u : u + 1], rolled[0][:, u : u + 1]
            both = a + b
            label = pick(seg_l, [labels[r, s * own_u + u] for s in range(segs)])
            g = (jnp.where(lane_w == label, a, 0.0) - prob[r, at, :].astype(F32) * both).astype(BF)
            prob[r, at, :] = g
            aim = jnp.zeros((frames, 128), F32)
            for kind in range(6):
                aim = jnp.where(lane_t == kind, rolled[kind][:, u : u + 1], aim)
            gt = (aim - prob_tail[r, at, :] * both).astype(BF)
            prob_tail[r, at, :] = gt.astype(F32)
            sum_tok = sum_tok + jnp.sum(g.astype(F32).reshape(frames // 8, 8, TOK), axis=0)
            sum_tail = sum_tail + jnp.sum(gt.astype(F32).reshape(frames // 8, 8, 128), axis=0)
        back = mm_t(prob[r], tok[...]) + mm_t(prob_tail[r].astype(BF), tail[...])
        back = back * slope[r].astype(F32)
        summed = back[:frames]
        for u in range(1, own_u):
            summed = summed + back[u * frames : (u + 1) * frames]
        part[k // micro, k % micro] = summed.astype(BF)
        shape = (segs * own_u, span)
        lanes = lane_ids(shape)
        seg_t = seg_of(lanes % frames, scalar_ends(lengths, r, segs))
        hit = (row_ids(shape) == seg_t * own_u + lanes // frames).astype(BF)
        g_pred[pl.ds(r * segs * own_u, segs * own_u), :] = mm(hit, back.astype(BF)).astype(BF)
        for j in range(1, labs):
            @pl.when(k == j * micro)
            def _():
                part_copy(j).start()
        return sum_tok, sum_tail

    zero = (jnp.zeros((8, TOK), F32), jnp.zeros((8, 128), F32))
    sum_tok, sum_tail = lax.fori_loop(0, rows, backward, zero)
    sum_tok = jnp.sum(sum_tok, axis=0, keepdims=True).astype(BF)
    sum_tail = jnp.sum(sum_tail, axis=0, keepdims=True).astype(BF)
    g_bias[...] = jnp.zeros(g_bias.shape, F32)
    for i in range(4):
        g_bias[i : i + 1, :] = sum_tok[:, 256 * i : 256 * i + 256].astype(F32)
    g_bias[4:5, :128] = sum_tail.astype(F32)
    gp = g_pred[...]
    g_predictor[...] = mm(gp, predx[:, : g_predictor.shape[1]])
    shards = lax.axis_size("dp")
    block = width // shards
    h_all = hid[...].reshape(rows * span, width)
    from_pred = t_mm(gp, pred[...])
    for i in range(2):
        piece = t_mm(h_all, prob[:, :, i * 512 : i * 512 + 512].reshape(rows * span, 512)).astype(BF)
        for d in range(shards):
            g_pack[d * 3 * block + (i + 1) * block : d * 3 * block + (i + 2) * block, :] = piece[d * block : (d + 1) * block]
    ends_w = t_mm(h_all, prob_tail[...].reshape(rows * span, 128).astype(BF)) + from_pred[:, 640:768]
    for d in range(shards):
        at = slice(d * block, (d + 1) * block)
        g_pack[d * 3 * block : d * 3 * block + block, :] = from_pred[at, :512].astype(BF)
        g_mix[at, :128] = from_pred[at, 512:640].astype(BF)
        g_mix[at, 128:] = ends_w[at].astype(BF)
    for j in range(1, labs):
        part_copy(j).wait_recv()
    total = part[0].astype(F32)
    for j in range(1, labs):
        total = total + came[j].astype(F32)
    g_enc[...] = total.astype(BF)
    for j in range(1, labs):
        enc_copy(j, peers.lab).wait_send()
        term_copy(j, peers.lab).wait_send()
        part_copy(j).wait_send()


def joint_call(enc_own, pred, lengths, counts, labels, predx, tok, tail, bias, dims):
    frames, rows, segs, own_u, labs = dims
    width = enc_own.shape[-1]
    span = own_u * frames
    micro = rows // labs
    vm = pl.BlockSpec(memory_space=pltpu.VMEM)
    sm = pl.BlockSpec(memory_space=pltpu.SMEM)
    return pl.pallas_call(
        functools.partial(joint_kernel, dims),
        out_shape=[
            jax.ShapeDtypeStruct((micro, frames, width), BF),
            jax.ShapeDtypeStruct((rows * segs * own_u, 640), F32),
            jax.ShapeDtypeStruct((3 * width, 512), BF),
            jax.ShapeDtypeStruct((width, 256), BF),
            jax.ShapeDtypeStruct((16, 256), F32),
            jax.ShapeDtypeStruct((8, 128), F32),
        ],
        in_specs=[vm, vm, sm, sm, sm, vm, vm, vm, vm],
        out_specs=[vm] * 6,
        scratch_shapes=[
            pltpu.VMEM((rows, frames, width), BF),
            pltpu.VMEM((rows * segs * own_u, width), F32),
            pltpu.VMEM((rows, span, width), BF),
            pltpu.VMEM((rows, span, width), BF),
            pltpu.VMEM((rows, span, TOK), BF),
            pltpu.VMEM((rows, span, 128), F32),
            pltpu.VMEM((frames, 256), F32),
            pltpu.VMEM((labs, frames, 256), F32),
            pltpu.VMEM((16, frames + 24, 128), F32),
            pltpu.VMEM((2, frames + 16, 128), F32),
            pltpu.VMEM((KINDS, frames, 128), F32),
            pltpu.VMEM((rows * segs * own_u, width), BF),
            pltpu.VMEM((labs, micro, frames, width), BF),
            pltpu.VMEM((labs, micro, frames, width), BF),
            pltpu.SemaphoreType.DMA((3, labs)),
            pltpu.SemaphoreType.DMA((3, labs)),
        ],
        compiler_params=pltpu.CompilerParams(
            collective_id=2, has_side_effects=True, vmem_limit_bytes=60 * 2**20
        ),
    )(enc_own, pred, lengths, counts, labels, predx, tok, tail, bias)


HEADS = 8
HD = 64
H = 8
epsilon = 1e-05
very_low = -100000.0


def product(first_op, second_op):
    return jnp.dot(first_op, second_op, preferred_element_type=jnp.float32)


def contract_rows(first_op, second_op):
    return lax.dot_general(
        first_op, second_op, (((0,), (0,)), ((), ())), preferred_element_type=jnp.float32
    )


def against(first_op, second_op):
    return lax.dot_general(
        first_op, second_op, (((1,), (1,)), ((), ())), preferred_element_type=jnp.float32
    )


def layer_norm(inputs, gain_vec):
    centre = inputs - jnp.mean(inputs, axis=-1, keepdims=True)
    spread = jnp.mean(centre * centre, axis=-1, keepdims=True)
    return centre * lax.rsqrt(spread + epsilon) * gain_vec


def segments(lengths, frames):
    seg_ends = jnp.cumsum(lengths, axis=-1)
    starts = seg_ends - lengths
    position = jnp.arange(frames, dtype=jnp.int32)
    passed = position[:, None] >= seg_ends[..., None, :]
    seg_index = jnp.sum(passed.astype(jnp.int32), axis=-1)
    member = seg_index[..., None] == jnp.arange(lengths.shape[-1], dtype=jnp.int32)
    seg_start = jnp.sum(jnp.where(member, starts[..., None, :], 0), axis=-1)
    seg_stop = jnp.sum(jnp.where(member, seg_ends[..., None, :], 0), axis=-1)
    return (seg_index, member, position - seg_start, seg_stop - position)


def conv_piece(conv_pre, w_depth, gain_depth, seg_index):
    width_in = w_depth.shape[1]
    frames = conv_pre.shape[0]
    half_taps = w_depth.shape[0] // 2
    gated = conv_pre[:, :width_in] * jax.nn.sigmoid(conv_pre[:, width_in:])
    padded = jnp.pad(gated, ((half_taps, half_taps), (0, 0)))
    seg_pad = jnp.pad(seg_index, (half_taps, half_taps), constant_values=-1)
    summed = jnp.zeros_like(gated)
    for tap_index in range(w_depth.shape[0]):
        same_seg = (seg_pad[tap_index : tap_index + frames] == seg_index).astype(gated.dtype)
        summed = (
            summed + w_depth[tap_index] * padded[tap_index : tap_index + frames] * same_seg[:, None]
        )
    return jax.nn.silu(layer_norm(summed, gain_depth))


def attend_scores(queries, keys, same_seg, score_scale):
    raw = (
        jnp.einsum("thd,shd->hts", queries, keys, preferred_element_type=jnp.float32) * score_scale
    )
    return jnp.where(same_seg[None], raw, very_low)


def block_forward(frames_bf, seg_index, all_weights):
    (
        gain_ffn,
        w_ffn_in,
        w_ffn_out,
        gain_att,
        w_qkv,
        w_att_out,
        gain_conv,
        w_point_in,
        w_depth,
        gain_depth,
        w_point_out,
        gain_out,
        w_enc,
    ) = all_weights[:13]
    frames = frames_bf.shape[0]
    inputs = frames_bf.astype(jnp.float32)
    normed, norm_back_one = jax.vjp(layer_norm, inputs, gain_ffn.astype(jnp.float32))
    ffn_in = normed.astype(jnp.bfloat16)
    ffn_pre = product(ffn_in, w_ffn_in)
    ffn_act = jax.nn.silu(ffn_pre).astype(jnp.bfloat16)
    after_ffn = inputs + 0.5 * product(ffn_act, w_ffn_out)
    normed, norm_back_two = jax.vjp(layer_norm, after_ffn, gain_att.astype(jnp.float32))
    att_in = normed.astype(jnp.bfloat16)
    qkv_all = product(att_in, w_qkv).astype(jnp.bfloat16).reshape(frames, 3, H, HD)
    queries, keys, values = (qkv_all[:, 0], qkv_all[:, 1], qkv_all[:, 2])
    same_seg = seg_index[:, None] == seg_index[None, :]
    scores = attend_scores(queries, keys, same_seg, HD ** (-0.5))
    largest = jnp.max(scores, axis=-1, keepdims=True)
    weights = jnp.exp(scores - largest)
    totals = jnp.sum(weights, axis=-1, keepdims=True)
    norm_log = largest + jnp.log(totals)
    probs = (weights / totals).astype(jnp.bfloat16)
    context = (
        jnp.einsum("hts,shd->thd", probs, values, preferred_element_type=jnp.float32)
        .astype(jnp.bfloat16)
        .reshape(frames, H * HD)
    )
    after_att = after_ffn + product(context, w_att_out)
    normed, norm_back_three = jax.vjp(layer_norm, after_att, gain_conv.astype(jnp.float32))
    conv_in = normed.astype(jnp.bfloat16)
    conv_pre = product(conv_in, w_point_in)
    conv_out, conv_back = jax.vjp(
        functools.partial(conv_piece, seg_index=seg_index),
        conv_pre,
        w_depth.astype(jnp.float32),
        gain_depth.astype(jnp.float32),
    )
    conv_act = conv_out.astype(jnp.bfloat16)
    after_conv = after_att + product(conv_act, w_point_out)
    encoded, norm_back_four = jax.vjp(layer_norm, after_conv, gain_out.astype(jnp.float32))
    enc_in = encoded.astype(jnp.bfloat16)
    enc_proj = product(enc_in, w_enc).astype(jnp.bfloat16)
    kept_state = (
        ffn_in,
        ffn_pre,
        ffn_act,
        att_in,
        queries,
        keys,
        values,
        same_seg,
        norm_log,
        context,
        conv_in,
        conv_act,
        enc_in,
        norm_back_one,
        norm_back_two,
        norm_back_three,
        norm_back_four,
        conv_back,
    )
    return (enc_in, enc_proj, kept_state)


def block_backward(enc_grad, kept_state, all_weights):
    w_ffn_in, w_ffn_out, w_qkv, w_att_out, w_point_in, w_point_out, w_enc = (
        all_weights[1],
        all_weights[2],
        all_weights[4],
        all_weights[5],
        all_weights[7],
        all_weights[10],
        all_weights[12],
    )
    (
        ffn_in,
        ffn_pre,
        ffn_act,
        att_in,
        queries,
        keys,
        values,
        same_seg,
        norm_log,
        context,
        conv_in,
        conv_act,
        enc_in,
        norm_back_one,
        norm_back_two,
        norm_back_three,
        norm_back_four,
        conv_back,
    ) = kept_state
    frames = ffn_in.shape[0]
    score_scale = HD ** (-0.5)
    grad_enc_w = contract_rows(enc_in, enc_grad)
    grad_conv_sum, grad_gain_out = norm_back_four(against(enc_grad, w_enc))
    branch = grad_conv_sum.astype(jnp.bfloat16)
    grad_point_out = contract_rows(conv_act, branch)
    grad_pre, grad_depth, grad_gain_depth = conv_back(against(branch, w_point_out))
    grad_pre_low = grad_pre.astype(jnp.bfloat16)
    grad_point_in = contract_rows(conv_in, grad_pre_low)
    grad_normed, grad_gain_conv = norm_back_three(against(grad_pre_low, w_point_in))
    grad_att_sum = grad_conv_sum + grad_normed
    branch = grad_att_sum.astype(jnp.bfloat16)
    grad_att_out = contract_rows(context, branch)
    grad_context = against(branch, w_att_out).astype(jnp.bfloat16).reshape(frames, H, HD)
    scores = attend_scores(queries, keys, same_seg, score_scale)
    probs = jnp.exp(scores - norm_log)
    grad_probs = jnp.einsum(
        "thd,shd->hts", grad_context, values, preferred_element_type=jnp.float32
    )
    grad_values = jnp.einsum(
        "hts,thd->shd", probs.astype(jnp.bfloat16), grad_context, preferred_element_type=jnp.float32
    )
    grad_scores = (
        probs * (grad_probs - jnp.sum(grad_probs * probs, axis=-1, keepdims=True))
    ).astype(jnp.bfloat16)
    grad_queries = (
        jnp.einsum("hts,shd->thd", grad_scores, keys, preferred_element_type=jnp.float32)
        * score_scale
    )
    grad_keys = (
        jnp.einsum("hts,thd->shd", grad_scores, queries, preferred_element_type=jnp.float32)
        * score_scale
    )
    grad_qkv_all = (
        jnp.stack([grad_queries, grad_keys, grad_values], axis=1)
        .astype(jnp.bfloat16)
        .reshape(frames, 3 * H * HD)
    )
    grad_w_qkv = contract_rows(att_in, grad_qkv_all)
    grad_normed, grad_gain_att = norm_back_two(against(grad_qkv_all, w_qkv))
    grad_ffn_sum = grad_att_sum + grad_normed
    branch = (0.5 * grad_ffn_sum).astype(jnp.bfloat16)
    grad_ffn_out = contract_rows(ffn_act, branch)
    grad_act = against(branch, w_ffn_out)
    grad_pre = jax.vjp(jax.nn.silu, ffn_pre)[1](grad_act)[0]
    grad_pre_low = grad_pre.astype(jnp.bfloat16)
    grad_ffn_in = contract_rows(ffn_in, grad_pre_low)
    grad_normed, grad_gain_ffn = norm_back_one(against(grad_pre_low, w_ffn_in))
    grad_inputs = grad_ffn_sum + grad_normed
    return (
        grad_inputs,
        (
            grad_gain_ffn,
            grad_ffn_in,
            grad_ffn_out,
            grad_gain_att,
            grad_w_qkv,
            grad_att_out,
            grad_gain_conv,
            grad_point_in,
            grad_depth,
            grad_gain_depth,
            grad_point_out,
            grad_gain_out,
            grad_enc_w,
        ),
    )


def pad_rows(value, rows):
    return jnp.pad(value, ((0, rows - value.shape[0]), (0, 0)))


def pad_lanes(value, lanes):
    return jnp.pad(value, ((0, 0), (0, lanes - value.shape[1])))


def pick_rows(gathered, n, first, rows):
    per = gathered.shape[0] // n
    return gathered.reshape(n, per, -1)[:, first : first + rows].reshape(n * rows, -1)


def local(
    frames_in, predictor, seg_lengths, label_counts, label_ids, gain_ffn, w_ffn_in, w_ffn_out, gain_att, w_qkv,
    w_att_out, gain_conv, w_point_in, w_depth, gain_depth, w_point_out, gain_out, w_enc, w_pred, bias_joint,
    w_joint_out, bias_out,
):
    n, labs = lax.axis_size("dp"), lax.axis_size("lab")
    micro, frames, model = frames_in.shape
    rows, segs, own_u, joint = predictor.shape
    ds, js = model // n, w_pred.shape[1]
    jr = -(-js // TILE) * TILE
    ff, qk, pi = w_ffn_in.shape[1], w_qkv.shape[1], w_point_in.shape[1]
    pred_t = pad_rows(w_pred.T, jr)
    tail = jnp.concatenate([w_joint_out[:, TOK:], bias_joint[:, None]], axis=1)
    small = jnp.concatenate(
        [pad_lanes(w_depth.T, 128), pad_lanes(jnp.stack([gain_ffn, gain_att, gain_conv, gain_depth, gain_out], 1), 128)],
        axis=1,
    )
    mix = jnp.concatenate(
        [pred_t[:, 512:], pad_rows(pad_lanes(tail, 128), jr), pad_rows(small, jr)], axis=1
    )
    shards = [
        jnp.concatenate([mix, w_ffn_in.T], 0),
        jnp.concatenate([w_ffn_out, w_qkv.T], 0),
        jnp.concatenate([w_att_out, w_point_in.T, w_point_out, pad_rows(w_enc.T, jr)], 0),
        jnp.concatenate(
            [pred_t[:, :512], pad_rows(w_joint_out[:, :512], jr), pad_rows(w_joint_out[:, 512:TOK], jr)], 0
        ),
    ]
    full = gather_all(n, shards)
    mixes = pick_rows(full[0], n, 0, jr)
    smalls = mixes.reshape(n, jr, 512)[:, :ds, 256:].reshape(model, 256)
    gains = smalls[:, 128:133].T
    weights = (
        gains[0], pick_rows(full[0], n, jr, ff).T, pick_rows(full[1], n, 0, ff), gains[1],
        pick_rows(full[1], n, ff, qk).T, pick_rows(full[2], n, 0, ds), gains[2], pick_rows(full[2], n, ds, pi).T,
        smalls[:, :9].T, gains[3], pick_rows(full[2], n, ds + pi, ds), gains[4],
        pick_rows(full[2], n, 2 * ds + pi, jr).T,
    )
    predx = jnp.concatenate([pick_rows(full[3], n, 0, jr), mixes[:, :256]], axis=1)
    tok = jnp.concatenate([pick_rows(full[3], n, jr, jr), pick_rows(full[3], n, 2 * jr, jr)], axis=1)
    tail_w = mixes[:, 128:256]
    lab = lax.axis_index("lab")
    own_lengths = lax.dynamic_slice_in_dim(seg_lengths, lab * micro, micro)
    seg_index = segments(own_lengths, frames)[0]
    enc_low, enc_proj, kept = jax.vmap(functools.partial(block_forward, all_weights=weights))(frames_in, seg_index)
    pred_ext = pad_lanes(predictor.reshape(-1, joint), 768)
    pred_ext = jnp.where(lax.broadcasted_iota(jnp.int32, pred_ext.shape, 1) == joint + BIAS_LANE, 1.0, pred_ext).astype(BF)
    bias = jnp.pad(bias_out.astype(F32), (0, TOK + 128 - bias_out.shape[0]))[None]
    dims = (frames, rows, segs, own_u, labs)
    g_enc, g_predictor, g_pack, g_mix, g_bias, loss = joint_call(
        enc_proj, pred_ext, seg_lengths, label_counts, label_ids.reshape(rows, -1), predx, tok, tail_w, bias, dims
    )
    grad_frames, block = jax.vmap(functools.partial(block_backward, all_weights=weights))(g_enc, kept)
    block = [jnp.sum(g, axis=0).astype(BF) for g in block]
    (gg_ffn, g_in, g_out, gg_att, g_qkv, g_att, gg_conv, g_pin, g_depth, gg_depth, g_pout, gg_out, g_encw) = block

    def by(value, rows_each):
        return value.reshape(n, rows_each, -1)

    small = jnp.concatenate(
        [pad_lanes(g_depth.T, 128), pad_lanes(jnp.stack([gg_ffn, gg_att, gg_conv, gg_depth, gg_out], 1), 128)], axis=1
    ).reshape(n, ds, 256)
    biases = jnp.broadcast_to(g_bias[None, : jr - ds].astype(BF), (n, min(16, jr - ds), 256))
    small = jnp.concatenate([small, biases, jnp.zeros((n, jr - ds - biases.shape[1], 256), BF)], axis=1)
    mix = jnp.concatenate([by(g_mix, jr), small], axis=2)
    packs = [
        g_pack,
        jnp.concatenate([by(g_att, ds), by(g_pin.T, pi), by(g_pout, ds), by(g_encw.T, jr)], 1).reshape(-1, 512),
        jnp.concatenate([by(g_out, ff), by(g_qkv.T, qk)], 1).reshape(-1, 512),
        jnp.concatenate([mix, by(g_in.T, ff)], 1).reshape(-1, 512),
    ]
    own = [g.astype(F32) for g in scatter_all(n, packs)]
    mix, small = own[3][:jr], own[3][:ds, 256:]
    g_pred_t = jnp.concatenate([own[0][:js], mix[:js, :128]], axis=1)
    g_joint = jnp.concatenate([own[0][jr : jr + js], own[0][2 * jr : 2 * jr + js], mix[:js, 128:134]], axis=1)
    g_bias_out = jnp.concatenate([mix[ds : ds + 4, 256:].reshape(-1), mix[ds + 4, 256:262]])
    loss_out = loss[:segs, : rows * own_u : own_u].T
    return (
        loss_out, enc_low, grad_frames, g_predictor.reshape(predictor.shape),
        small[:, 128], own[3][jr:].T, own[2][:ff], small[:, 129], own[2][ff:].T, own[1][:ds], small[:, 130],
        own[1][ds : ds + pi].T, small[:, :9].T, small[:, 131], own[1][ds + pi : 2 * ds + pi], small[:, 132],
        own[1][2 * ds + pi : 2 * ds + pi + js].T, g_pred_t.T, mix[:js, 128 + BIAS_LANE], g_joint, g_bias_out,
    )


def solution(mesh):
    rows, whole = P(("dp", "lab"), None, None), P()
    predictor, columns, lines, vector = P("dp", None, "lab", None), P(None, "dp"), P("dp", None), P("dp")
    params = (
        vector, columns, lines, vector, columns, lines, vector, columns, columns, vector, lines, vector, columns,
        columns, vector, lines, whole,
    )
    return jax.shard_map(
        local,
        mesh=mesh,
        in_specs=(rows, predictor, lines, lines, P("dp", None, "lab")) + params,
        out_specs=(lines, rows, rows, predictor) + params,
        check_vma=False,
    )
```

```python
import functools

import jax
import jax.numpy as jnp
from jax import lax
from jax.experimental import pallas as pl
from jax.experimental.pallas import tpu as pltpu
from jax.sharding import PartitionSpec as P


MESH = pl.DeviceIdType.MESH
F32 = jnp.float32
BF = jnp.bfloat16
TILE = 16


def ring_place(dp, n):
    odd = dp % 2
    return (1 - odd) * (dp // 2) + odd * (n - 1 - dp // 2)


def ring_device(place, n):
    place = (place + 2 * n) % n
    high = place // (n // 2)
    return (1 - high) * (2 * place) + high * (2 * (n - 1 - place) + 1)


def x_rows(rows, share):
    tiles = rows // TILE
    return min(tiles // 2, int(tiles * share + 0.5)) * TILE


class Where:
    def __init__(self, n):
        self.n = n
        self.dp = lax.axis_index("dp")
        self.lab = lax.axis_index("lab")
        self.core = self.lab % 2
        self.side = self.lab // 2
        self.place = ring_place(self.dp, n)
        self.right = (ring_device(self.place + 1, n), self.lab)
        self.left = (ring_device(self.place - 1, n), self.lab)
        self.twin = (self.dp, self.side * 2 + 1 - self.core)
        self.across = (self.dp, (1 - self.side) * 2 + self.core)
        self.far = (
            ring_device(self.place + 1 - 2 * self.core, n),
            self.lab,
        )

    def at(self, distance):
        return ring_device(self.place + distance, self.n)

    def greet(self):
        barrier = pltpu.get_barrier_semaphore()
        for other in (self.right, self.left, self.twin, self.across):
            pl.semaphore_signal(barrier, inc=1, device_id=other, device_id_type=MESH)
        pl.semaphore_wait(barrier, 4)


def remote(src, dst, send_sem, recv_sem, device):
    return pltpu.make_async_remote_copy(
        src_ref=src,
        dst_ref=dst,
        send_sem=send_sem,
        recv_sem=recv_sem,
        device_id=device,
        device_id_type=MESH,
    )


class Gather:
    def __init__(self, where, source, target, rows, ring_recv, x_recv, sems):
        self.w, self.source, self.target, self.rows = where, source, target, rows
        self.width = target.shape[1]
        self.half = self.width // 2
        self.cut = x_rows(rows, 0.3)
        self.ring_recv, self.x_recv, self.sems = ring_recv, x_recv, sems
        self.steps = where.n // 2

    def lanes(self):
        return pl.ds(pl.multiple_of(self.w.core * self.half, 128), self.half)

    def rows_at(self, shard, offset, size):
        base = shard * self.rows if shard is not None else 0
        return pl.ds(pl.multiple_of(base + offset, TILE), size)

    def ring_part(self, ref, shard):
        return ref.at[self.rows_at(shard, self.w.side * self.cut, self.rows - self.cut), self.lanes()]

    def x_part(self, ref, shard, side):
        return ref.at[self.rows_at(shard, side * (self.rows - self.cut), self.cut), self.lanes()]

    def slot(self, distance):
        return distance + self.steps - 1 if distance < 0 else distance + self.steps - 2

    def hop(self, distance, first):
        w = self.w
        if distance == self.steps:
            shard = w.at((2 * w.core - 1) * (self.steps - 1))
            device = w.far
        else:
            shard = w.at(distance + 1) if distance < 0 else w.at(distance - 1)
            device = w.right if distance < 0 else w.left
        src = self.ring_part(self.source, None) if first else self.ring_part(self.target, shard)
        slot = 2 * self.steps - 2 if distance == self.steps else self.slot(distance)
        remote(src, self.ring_part(self.target, shard), self.sems.at[1], self.ring_recv.at[slot], device).start()

    def own(self):
        pltpu.make_async_copy(
            self.source, self.target.at[self.rows_at(self.w.dp, 0, self.rows), :], self.sems.at[4]
        ).start()

    def arrived(self, distance):
        w = self.w
        shard = w.at(distance)
        slot = 2 * self.steps - 2 if distance == self.steps else self.slot(distance)
        part = self.ring_part(self.target, shard)
        remote(part, part, self.sems.at[1], self.ring_recv.at[slot], w.right).wait_recv()

    def spread(self, distance):
        w = self.w
        shard = w.at(distance)
        slot = 2 * self.steps - 2 if distance == self.steps else self.slot(distance)
        if self.cut:
            part = self.x_part(self.target, shard, w.side)
            remote(part, part, self.sems.at[2], self.x_recv.at[slot], w.across).start()
        part = self.ring_part(self.target, shard)
        remote(part, part, self.sems.at[3], self.sems.at[0], w.twin).start()

    def crossed(self, distance):
        if not self.cut:
            return
        w = self.w
        shard = w.at(distance)
        slot = 2 * self.steps - 2 if distance == self.steps else self.slot(distance)
        part = self.x_part(self.target, shard, 1 - w.side)
        remote(part, part, self.sems.at[2], self.x_recv.at[slot], w.across).wait_recv()
        remote(part, part, self.sems.at[3], self.sems.at[0], w.twin).start()

    def whole(self):
        part = self.target.at[pl.ds(0, (self.w.n - 1) * self.rows), pl.ds(0, self.half)]
        remote(part, part, self.sems.at[3], self.sems.at[0], self.w.twin).wait_recv()
        pltpu.make_async_copy(
            self.source, self.target.at[self.rows_at(self.w.dp, 0, self.rows), :], self.sems.at[4]
        ).wait()

    def drain(self):
        count = self.w.n - 1
        for sem, rows in ((1, self.rows - self.cut), (2, self.cut), (3, self.rows)):
            if rows:
                part = self.target.at[pl.ds(0, count * rows), pl.ds(0, self.half)]
                remote(part, part, self.sems.at[sem], self.sems.at[sem], self.w.twin).wait_send()

    def step(self, s):
        if s == 0:
            self.own()
        if 1 <= s < self.steps:
            self.arrived(-s)
            self.arrived(s)
        if s == self.steps:
            self.arrived(self.steps)
        if s < self.steps - 1:
            self.hop(-s - 1, s == 0)
            self.hop(s + 1, s == 0)
        elif s == self.steps - 1:
            self.hop(self.steps, False)
        if 1 <= s < self.steps:
            self.spread(-s)
            self.spread(s)
        if s == self.steps:
            self.spread(self.steps)
        if 2 <= s <= self.steps:
            self.crossed(-s + 1)
            self.crossed(s - 1)
        if s == self.steps + 1:
            self.crossed(self.steps)


def gather_kernel(n, rows_list, *refs):
    k = len(rows_list)
    sources, targets = refs[:k], refs[k : 2 * k]
    ring_recv, x_recv, sems = refs[2 * k :]
    w = Where(n)
    w.greet()
    parts = [
        Gather(w, sources[i], targets[i], rows_list[i], ring_recv.at[i], x_recv.at[i], sems.at[i])
        for i in range(k)
    ]
    turns = n // 2 + 2
    for tick in range(k + turns - 1):
        for s in range(turns - 1, -1, -1):
            g = tick - s
            if 0 <= g < k:
                parts[g].step(s)
    for part in parts:
        part.whole()
        part.drain()


def gather_all(n, shards):
    k = len(shards)
    rows_list = [s.shape[0] for s in shards]
    return pl.pallas_call(
        functools.partial(gather_kernel, n, rows_list),
        out_shape=[jax.ShapeDtypeStruct((n * s.shape[0], s.shape[1]), s.dtype) for s in shards],
        in_specs=[pl.BlockSpec(memory_space=pltpu.VMEM)] * k,
        out_specs=[pl.BlockSpec(memory_space=pltpu.VMEM)] * k,
        scratch_shapes=[
            pltpu.SemaphoreType.DMA((k, n - 1)),
            pltpu.SemaphoreType.DMA((k, n - 1)),
            pltpu.SemaphoreType.DMA((k, 5)),
        ],
        compiler_params=pltpu.CompilerParams(
            collective_id=0, has_side_effects=True, vmem_limit_bytes=56 * 2**20
        ),
    )(*shards)


class Scatter:
    STAGES = 9

    def __init__(self, where, grads, out, rows, bufs, send, recv):
        self.w, self.grads, self.out, self.rows = where, grads, out, rows
        self.held, self.xbuf, self.rbuf, self.final = bufs
        self.half = grads.shape[1] // 2
        self.cut = x_rows(rows, SHARE_RS)
        self.send, self.recv = send, recv
        self.depth = where.n // 2 - 1
        self.started = []

    def lanes(self, core):
        return pl.ds(pl.multiple_of(core * self.half, 128), self.half)

    def rows_at(self, shard, offset, size):
        return pl.ds(pl.multiple_of(shard * self.rows + offset, TILE), size)

    def go(self, sem, src, dst, device):
        copy = remote(src, dst, self.send.at[sem], self.recv.at[sem], device)
        copy.start()
        self.started.append(copy)

    def got(self, sem, dst):
        remote(dst, dst, self.send.at[sem], self.recv.at[sem], self.w.twin).wait_recv()

    def mine(self, shard):
        return self.held[self.rows_at(shard, self.w.side * self.cut, self.rows - self.cut), :].astype(F32)

    def stage(self, s):
        w, rows, cut, depth = self.w, self.rows, self.cut, self.depth
        n, keep = w.n, self.rows - self.cut
        if s == 0:
            self.go(0, self.grads.at[:, self.lanes(1 - w.core)], self.held, w.twin)
        elif s == 1:
            self.got(0, self.held)

            def add(i, _):
                at = self.rows_at(i, 0, rows)
                self.held[at, :] = (
                    self.held[at, :].astype(F32) + self.grads[at, self.lanes(w.core)].astype(F32)
                ).astype(BF)
                return 0

            lax.fori_loop(0, n, add, 0)
            if cut:
                for i in range(n):
                    src = self.held.at[self.rows_at(i, (1 - w.side) * keep, cut), :]
                    remote(src, self.xbuf.at[i], self.send.at[1], self.recv.at[1], w.across).start()
        elif s == 2:
            if cut:
                self.got(1, self.xbuf)

                def add(i, _):
                    at = self.rows_at(i, w.side * keep, cut)
                    self.held[at, :] = (
                        self.held[at, :].astype(F32) + self.xbuf[i].astype(F32)
                    ).astype(BF)
                    return 0

                lax.fori_loop(0, n, add, 0)
            dest = w.at((2 * w.core - 1) * (depth + 1))
            src = self.held.at[self.rows_at(dest, w.side * cut, keep), :]
            self.go(2, src, self.rbuf.at[2 * depth], w.far_back)
        elif s < 3 + depth:
            hop = s - 3
            for way in (0, 1):
                sign = 1 - 2 * way
                own = self.mine(w.at(sign * (depth - hop)))
                slot = 2 * hop + way
                if hop == 0:
                    if way == 0:
                        self.got(2, self.rbuf.at[2 * depth])
                    far = self.rbuf[2 * depth].astype(F32)
                    pick = w.core if way == 0 else 1 - w.core
                    own = own + jnp.where(pick == 1, far, 0.0)
                    at = 2 * depth + 1 + way
                else:
                    at = slot - 2
                    self.got(3 + at, self.rbuf.at[at])
                    own = own + self.rbuf[at].astype(F32)
                self.rbuf[at] = own.astype(BF)
                self.go(3 + slot, self.rbuf.at[at], self.rbuf.at[slot], w.right if way == 0 else w.left)
        elif s == 3 + depth:
            total = self.mine(w.dp)
            for way in (0, 1):
                at = 2 * depth - 2 + way
                self.got(3 + at, self.rbuf.at[at])
                total = total + self.rbuf[at].astype(F32)
            self.final[0] = total.astype(BF)
            self.go(3 + 2 * depth, self.final.at[0], self.final.at[1], w.across)
        elif s == 4 + depth:
            self.got(3 + 2 * depth, self.final.at[1])
            lanes = self.lanes(w.core)
            own, other = self.final[0].astype(F32), self.final[1].astype(F32)
            if cut:
                first = w.side == 0
                low, high = jnp.where(first, own, other), jnp.where(first, other, own)
                self.out[:cut, lanes] = low[:cut].astype(BF)
                if keep > cut:
                    self.out[cut:keep, lanes] = (low[cut:] + high[: keep - cut]).astype(BF)
                self.out[keep:, lanes] = high[keep - cut :].astype(BF)
            else:
                self.out[:, lanes] = (own + other).astype(BF)
            part = self.out.at[:, lanes]
            self.go(4 + 2 * depth, part, part, w.twin)
        elif s == 5 + depth:
            self.got(4 + 2 * depth, self.out.at[:, self.lanes(1 - w.core)])

    def drain(self):
        for copy in self.started:
            copy.wait_send()
        if self.cut:
            remote(self.xbuf, self.xbuf, self.send.at[1], self.recv.at[1], self.w.across).wait_send()


SHARE_RS = 0.25


def scatter_scratch(n, rows, width, k_index=None):
    half, cut, depth = width // 2, x_rows(rows, SHARE_RS), n // 2 - 1
    return [
        pltpu.VMEM((n * rows, half), BF),
        pltpu.VMEM((n, max(cut, TILE), half), BF),
        pltpu.VMEM((2 * depth + 3, rows - cut, half), BF),
        pltpu.VMEM((2, rows - cut, half), BF),
    ]


def scatter_sems(n, k):
    return [pltpu.SemaphoreType.DMA((k, n + 3)), pltpu.SemaphoreType.DMA((k, n + 3))]


def scatter_kernel(n, rows_list, skew, *refs):
    k = len(rows_list)
    grads, outs = refs[:k], refs[k : 2 * k]
    bufs = refs[2 * k : 2 * k + 4 * k]
    send, recv = refs[6 * k :]
    w = Where(n)
    w.far_back = (ring_device(w.place + 2 * w.core - 1, n), w.lab)
    w.greet()
    parts = [
        Scatter(w, grads[i], outs[i], rows_list[i], bufs[4 * i : 4 * i + 4], send.at[i], recv.at[i])
        for i in range(k)
    ]
    stages = n // 2 + 5
    for tick in range(k + skew * (stages - 1)):
        for s in range(stages - 1, -1, -1):
            g = tick - skew * s
            if 0 <= g < k:
                parts[g].stage(s)
    for part in parts:
        part.drain()


def scatter_all(n, grads, skew=1):
    k = len(grads)
    rows_list = [g.shape[0] // n for g in grads]
    scratch = []
    for g, rows in zip(grads, rows_list):
        scratch += scatter_scratch(n, rows, g.shape[1])
    return pl.pallas_call(
        functools.partial(scatter_kernel, n, rows_list, skew),
        out_shape=[jax.ShapeDtypeStruct((rows, g.shape[1]), BF) for g, rows in zip(grads, rows_list)],
        in_specs=[pl.BlockSpec(memory_space=pltpu.VMEM)] * k,
        out_specs=[pl.BlockSpec(memory_space=pltpu.VMEM)] * k,
        scratch_shapes=scratch + scatter_sems(n, k),
        compiler_params=pltpu.CompilerParams(
            collective_id=1, has_side_effects=True, vmem_limit_bytes=60 * 2**20
        ),
    )(*grads)


LOW = -100000.0
TOK = 1024
KINDS = 7
BIAS_LANE = 6


def mm(a, b):
    return lax.dot_general(a, b, (((1,), (0,)), ((), ())), preferred_element_type=F32)


def mm_t(a, b):
    return lax.dot_general(a, b, (((1,), (1,)), ((), ())), preferred_element_type=F32)


def t_mm(a, b):
    return lax.dot_general(a, b, (((0,), (0,)), ((), ())), preferred_element_type=F32)


def lane_ids(shape):
    return lax.broadcasted_iota(jnp.int32, shape, len(shape) - 1)


def row_ids(shape):
    return lax.broadcasted_iota(jnp.int32, shape, 0)


class Peers:
    def __init__(self):
        self.dp, self.lab = lax.axis_index("dp"), lax.axis_index("lab")
        self.core, self.side = self.lab % 2, self.lab // 2

    def owner(self, j):
        return ((self.side + j // 2) % 2) * 2 + (self.core + j % 2) % 2

    def device(self, j):
        return (self.dp, self.owner(j))


def seg_of(t, ends):
    return sum((t >= e).astype(jnp.int32) for e in ends[:-1])


def pick(seg, values):
    out = values[0]
    for s in range(1, len(values)):
        out = jnp.where(seg == s, values[s], out)
    return out


def scalar_ends(ints, r, segs):
    ends, total = [], 0
    for s in range(segs):
        total = total + ints[r, s]
        ends.append(total)
    return ends


def lse_of(terms):
    top = functools.reduce(jnp.maximum, terms)
    return top, functools.reduce(jnp.add, [jnp.exp(v - top) for v in terms])


def lattice(peers, ints, terms, skewed, hist, grads, loss, dims):
    frames, rows, segs, own_u, labs = dims
    wide = (frames, 128)
    lane = lane_ids(wide)
    group = rows * own_u
    j, row, u = lane % own_u, (lane % group) // own_u, (lane // group) * own_u + lane % own_u
    t = row_ids(wide)
    all_ends = [scalar_ends(ints, r, segs) for r in range(rows)]

    def per_lane(values):
        out = jnp.zeros(wide, jnp.int32)
        for r in range(rows):
            out = jnp.where(row == r, values[r], out)
        return out

    ends = [per_lane([all_ends[r][s] for r in range(rows)]) for s in range(segs)]
    labels_in = [per_lane([ints[r, segs + s] for r in range(rows)]) for s in range(segs)]
    seg = seg_of(t, ends)
    stop = pick(seg, ends)
    begin = pick(seg, [jnp.zeros(wide, jnp.int32)] + ends[:-1])
    target = pick(seg, labels_in)
    remain, first = stop - t, t == begin

    kinds = []
    per_vreg = 128 // group
    for k in range(KINDS):
        value = None
        for dev in range(labs):
            part = terms[dev, :, (k // per_vreg) * 128 : (k // per_vreg) * 128 + 128]
            shift = (dev - k % per_vreg) * group % 128
            part = pltpu.roll(part, shift, 1) if shift else part
            value = part if value is None else jnp.where(lane // group == dev, part, value)
        kinds.append(value)
    blank_lp, durs, label_lp = kinds[0], kinds[1:6], kinds[6]
    last_u = own_u * labs - 1
    emit, blank, blank_raw = [], [None], [None]
    for d in range(5):
        ok = (u < last_u) & (d <= remain - 1)
        emit.append(jnp.where(ok, label_lp + durs[d], LOW))
        if d:
            blank_raw.append(blank_lp + durs[d])
            blank.append(jnp.where(d <= remain - 1, blank_raw[d], LOW))
    final = (u == target) & (remain <= 4)
    closing = jnp.zeros(wide, F32)
    for d in range(1, 5):
        closing = jnp.where(remain == d, blank_raw[d], closing)
    closing = jnp.where(final, closing, LOW)
    start = jnp.where(first & (u == 0), 0.0, LOW)

    tall = frames + 16
    tall_u = (lane_ids((tall, 128)) // group) * own_u + lane_ids((tall, 128)) % own_u
    tall_j = lane_ids((tall, 128)) % own_u
    pad = jnp.full((16, 128), LOW, F32)

    def skew(value):
        value = jnp.concatenate([value, pad], axis=0)
        for bit in (1, 2, 4, 8):
            value = jnp.where((tall_u // bit) % 2 == 1, pltpu.roll(value, bit, 0), value)
        return value

    def unskew(value):
        for bit in (1, 2, 4, 8):
            value = jnp.where((tall_u // bit) % 2 == 1, pltpu.roll(value, tall - bit, 0), value)
        return value[:frames]

    up = 128 - (group - own_u + 1)

    def next_up(value, jj):
        return jnp.where(jj == 0, pltpu.roll(value, group - own_u + 1, 1), pltpu.roll(value, 1, 1))

    def next_down(value, jj):
        return jnp.where(jj == own_u - 1, pltpu.roll(value, up, 1), pltpu.roll(value, 127, 1))

    lead = jnp.full((8, 128), LOW, F32)

    def keep(i, value):
        skewed[i, 0:8, :] = lead
        skewed[i, 8 : 8 + tall, :] = value

    for d in range(1, 5):
        keep(d - 1, skew(blank[d]))
    for d in range(5):
        value = skew(emit[d])
        keep(4 + d, value)
        keep(9 + d, next_up(value, tall_j))
    keep(14, skew(start))
    keep(15, skew(closing))
    waves = frames + last_u
    one_j = lane_ids((1, 128)) % own_u
    low_row = skewed[0, 0:1, :]

    def at(i, w):
        return skewed[i, pl.ds(w + 8, 1), :]

    def combine(old, near):
        top_old, sum_old = lse_of(old)
        top = functools.reduce(jnp.maximum, near, top_old)
        total = sum_old * jnp.exp(top_old - top)
        for v in near:
            total = total + jnp.exp(v - top)
        return top + jnp.log(total)

    def wave(i, carry):
        a, ra, b, rb = carry
        old = [at(14, i)]
        for d in range(2, 5):
            old.append(a[d - 1] + at(d - 1, i - d))
        for d in range(2, 6):
            old.append(ra[d - 1] + at(8 + d, i - d))
        new_a = combine(old, [a[0] + at(0, i - 1), ra[0] + at(9, i - 1)])
        back = waves - 1 - i
        old = [at(15, back)]
        for d in range(2, 5):
            old.append(b[d - 1] + at(d - 1, back))
        for d in range(2, 6):
            old.append(rb[d - 1] + at(3 + d, back))
        new_b = combine(old, [b[0] + at(0, back), rb[0] + at(4, back)])
        hist[0, pl.ds(i, 1), :] = new_a
        hist[1, pl.ds(back, 1), :] = new_b
        return (
            (new_a,) + a[:-1],
            (next_up(new_a, one_j),) + ra[:-1],
            (new_b,) + b[:-1],
            (next_down(new_b, one_j),) + rb[:-1],
        )

    hist[...] = jnp.full(hist.shape, LOW, F32)
    lax.fori_loop(
        0, waves, wave, ((low_row,) * 4, (low_row,) * 5, (low_row,) * 4, (low_row,) * 5)
    )
    alpha, beta = unskew(hist[0]), unskew(hist[1])
    ahead = next_down(beta, j)
    norm = jnp.zeros(wide, F32)
    heads = jnp.where(first & (u == 0), beta, 0.0)
    for s in range(segs):
        value = jnp.sum(jnp.where(seg == s, heads, 0.0), axis=0, keepdims=True)
        step = 1
        while step < own_u:
            value = value + pltpu.roll(value, step, 1)
            step *= 2
        step = group
        while step < 128:
            value = value + pltpu.roll(value, step, 1)
            step *= 2
        norm = jnp.where(seg == s, value, norm)
        length = ends[s] - (ends[s - 1] if s else 0)
        loss[pl.ds(s, 1), :] = -value / length[:1].astype(F32)
    base = alpha - norm
    total_a, total_b = None, None
    for d in range(5):
        there = pltpu.roll(ahead, frames - d, 0) if d else ahead
        g = -jnp.exp(base + emit[d] + there)
        total_a = g if d == 0 else total_a + g
        if d:
            gb = -jnp.exp(base + blank[d] + pltpu.roll(beta, frames - d, 0))
            gb = gb - jnp.exp(jnp.where(final & (remain == d), base + blank_raw[d], LOW))
            total_b = gb if d == 1 else total_b + gb
            g = g + gb
        grads[1 + d] = g
    grads[0] = total_b
    grads[6] = total_a


def joint_kernel(
    dims,
    enc_own, pred, ints, predx, tok, tail, bias,
    g_enc, g_predictor, g_pack, g_mix, g_bias, loss,
    enc_all, proj, hid, slope, prob, prob_tail, mine, terms, skewed, hist, grads, g_pred, part, came,
    send, recv,
):
    frames, rows, segs, own_u, labs = dims
    micro = rows // labs
    peers = Peers()
    barrier = pltpu.get_barrier_semaphore()
    for j in range(1, labs):
        pl.semaphore_signal(barrier, inc=1, device_id=peers.device(j), device_id_type=MESH)
    pl.semaphore_wait(barrier, labs - 1)
    width = enc_own.shape[-1]
    span = own_u * frames
    own_rows = pl.ds(peers.lab * micro, micro)

    def enc_copy(j, source):
        return remote(enc_own, enc_all.at[pl.ds(source * micro, micro)], send.at[0, j], recv.at[0, j], peers.device(j))

    for j in range(1, labs):
        enc_copy(j, peers.lab).start()
    enc_all[own_rows] = enc_own[...]
    proj[...] = mm_t(pred[...], predx[...])
    lane_t = lane_ids((frames, 128))
    lane_w = lane_ids((frames, TOK))
    group = rows * own_u
    per_vreg = 128 // group

    def row_of(k):
        return peers.owner(k // micro) * micro + k % micro

    def forward(k, _):
        for j in range(1, labs):
            @pl.when(k == j * micro)
            def _():
                enc_copy(j, peers.owner(j)).wait_recv()
        r = row_of(k)
        seg = seg_of(row_ids((frames, width)), scalar_ends(ints, r, segs))
        enc = enc_all[r].astype(F32)
        for u in range(own_u):
            per_frame = pick(
                seg, [proj[pl.ds(r * segs * own_u + s * own_u + u, 1), :] for s in range(segs)]
            )
            value = jnp.tanh(enc + per_frame)
            hid[r, u * frames : (u + 1) * frames, :] = value.astype(BF)
            slope[r, u * frames : (u + 1) * frames, :] = (1.0 - value * value).astype(BF)
        h = hid[r]
        end = mm(h, tail[...]) + bias[:, TOK:]
        wide = mm(h, tok[...]) + bias[:, :TOK]
        seg_l = seg_of(row_ids((frames, TOK)), scalar_ends(ints, r, segs))
        for u in range(own_u):
            logit, last = wide[u * frames : (u + 1) * frames], end[u * frames : (u + 1) * frames]
            top = jnp.maximum(jnp.max(logit, axis=1, keepdims=True), last[:, 0:1])
            top_dur = jnp.max(
                jnp.where((lane_t >= 1) & (lane_t <= 5), last, -jnp.inf), axis=1, keepdims=True
            )
            is_tok = lane_t == 0
            e_last = jnp.where(
                lane_t < 6, jnp.exp(jnp.where(lane_t < 6, last - jnp.where(is_tok, top, top_dur), 0.0)), 0.0
            )
            e = jnp.exp(logit - top)
            total = jnp.sum(e, axis=1, keepdims=True) + e_last[:, 0:1]
            total_dur = jnp.sum(jnp.where(is_tok, 0.0, e_last), axis=1, keepdims=True)
            prob[r, u * frames : (u + 1) * frames, :] = (e * (1.0 / total)).astype(BF)
            prob_tail[r, u * frames : (u + 1) * frames, :] = e_last * (1.0 / jnp.where(is_tok, total, total_dur))
            norm_tok, norm_dur = top + jnp.log(total), top_dur + jnp.log(total_dur)
            label = pick(seg_l, [ints[r, 2 * segs + s * own_u + u] for s in range(segs)])
            at_label = jnp.sum(jnp.where(lane_w == label, logit, 0.0), axis=1, keepdims=True) - norm_tok
            lp = last - jnp.where(is_tok, norm_tok, norm_dur)
            for kind in range(KINDS):
                column = at_label if kind == 6 else lp[:, kind : kind + 1]
                cols = slice((kind // per_vreg) * 128, (kind // per_vreg) * 128 + 128)
                place = (kind % per_vreg) * group + r * own_u + u
                mine[:, cols] = jnp.where(lane_t == place, column, mine[:, cols])
        return 0

    mine[...] = jnp.zeros(mine.shape, F32)
    lax.fori_loop(0, rows, forward, 0)
    terms[peers.lab] = mine[...]

    def term_copy(j, source):
        return remote(mine, terms.at[source], send.at[1, j], recv.at[1, j], peers.device(j))

    for j in range(1, labs):
        term_copy(j, peers.lab).start()
    for j in range(1, labs):
        term_copy(j, peers.owner(j)).wait_recv()
    lattice(peers, ints, terms, skewed, hist, grads, loss, dims)

    def part_copy(j):
        return remote(part.at[j], came.at[j], send.at[2, j], recv.at[2, j], peers.device(j))

    def backward(i, sums):
        k = rows - 1 - i
        r = row_of(k)
        shift = (256 - peers.lab * group - r * own_u) % 128
        rolled = [pltpu.roll(grads[kind], shift, 1) for kind in range(KINDS)]
        seg_l = seg_of(row_ids((frames, TOK)), scalar_ends(ints, r, segs))
        sum_tok, sum_tail = sums
        for u in range(own_u):
            at = slice(u * frames, (u + 1) * frames)
            a, b = rolled[6][:, u : u + 1], rolled[0][:, u : u + 1]
            both = a + b
            label = pick(seg_l, [ints[r, 2 * segs + s * own_u + u] for s in range(segs)])
            g = (jnp.where(lane_w == label, a, 0.0) - prob[r, at, :].astype(F32) * both).astype(BF)
            prob[r, at, :] = g
            aim = jnp.zeros((frames, 128), F32)
            for kind in range(6):
                aim = jnp.where(lane_t == kind, rolled[kind][:, u : u + 1], aim)
            gt = (aim - prob_tail[r, at, :] * both).astype(BF)
            prob_tail[r, at, :] = gt.astype(F32)
            sum_tok = sum_tok + jnp.sum(g.astype(F32).reshape(frames // 8, 8, TOK), axis=0)
            sum_tail = sum_tail + jnp.sum(gt.astype(F32).reshape(frames // 8, 8, 128), axis=0)
        back = mm_t(prob[r], tok[...]) + mm_t(prob_tail[r].astype(BF), tail[...])
        back = back * slope[r].astype(F32)
        summed = back[:frames]
        for u in range(1, own_u):
            summed = summed + back[u * frames : (u + 1) * frames]
        part[k // micro, k % micro] = summed.astype(BF)
        shape = (segs * own_u, span)
        lanes = lane_ids(shape)
        seg_t = seg_of(lanes % frames, scalar_ends(ints, r, segs))
        hit = (row_ids(shape) == seg_t * own_u + lanes // frames).astype(BF)
        g_pred[pl.ds(r * segs * own_u, segs * own_u), :] = mm(hit, back.astype(BF)).astype(BF)
        for j in range(1, labs):
            @pl.when(k == j * micro)
            def _():
                part_copy(j).start()
        return sum_tok, sum_tail

    zero = (jnp.zeros((8, TOK), F32), jnp.zeros((8, 128), F32))
    sum_tok, sum_tail = lax.fori_loop(0, rows, backward, zero)
    sum_tok = jnp.sum(sum_tok, axis=0, keepdims=True).astype(BF)
    sum_tail = jnp.sum(sum_tail, axis=0, keepdims=True).astype(BF)
    g_bias[...] = jnp.zeros(g_bias.shape, F32)
    for i in range(4):
        g_bias[i : i + 1, :] = sum_tok[:, 256 * i : 256 * i + 256].astype(F32)
    g_bias[4:5, :128] = sum_tail.astype(F32)
    gp = g_pred[...]
    g_predictor[...] = mm(gp, predx[:, : g_predictor.shape[1]])
    shards = lax.axis_size("dp")
    block = width // shards
    h_all = hid[...].reshape(rows * span, width)
    from_pred = t_mm(gp, pred[...])
    for i in range(2):
        piece = t_mm(h_all, prob[:, :, i * 512 : i * 512 + 512].reshape(rows * span, 512)).astype(BF)
        for d in range(shards):
            g_pack[d * 3 * block + (i + 1) * block : d * 3 * block + (i + 2) * block, :] = piece[d * block : (d + 1) * block]
    ends_w = t_mm(h_all, prob_tail[...].reshape(rows * span, 128).astype(BF)) + from_pred[:, 640:768]
    for d in range(shards):
        at = slice(d * block, (d + 1) * block)
        g_pack[d * 3 * block : d * 3 * block + block, :] = from_pred[at, :512].astype(BF)
        g_mix[at, :128] = from_pred[at, 512:640].astype(BF)
        g_mix[at, 128:] = ends_w[at].astype(BF)
    for j in range(1, labs):
        part_copy(j).wait_recv()
    total = part[0].astype(F32)
    for j in range(1, labs):
        total = total + came[j].astype(F32)
    g_enc[...] = total.astype(BF)
    for j in range(1, labs):
        enc_copy(j, peers.lab).wait_send()
        term_copy(j, peers.lab).wait_send()
        part_copy(j).wait_send()


def joint_call(enc_own, pred, ints, predx, tok, tail, bias, dims):
    frames, rows, segs, own_u, labs = dims
    width = enc_own.shape[-1]
    span = own_u * frames
    micro = rows // labs
    vm = pl.BlockSpec(memory_space=pltpu.VMEM)
    sm = pl.BlockSpec(memory_space=pltpu.SMEM)
    return pl.pallas_call(
        functools.partial(joint_kernel, dims),
        out_shape=[
            jax.ShapeDtypeStruct((micro, frames, width), BF),
            jax.ShapeDtypeStruct((rows * segs * own_u, 640), F32),
            jax.ShapeDtypeStruct((3 * width, 512), BF),
            jax.ShapeDtypeStruct((width, 256), BF),
            jax.ShapeDtypeStruct((16, 256), F32),
            jax.ShapeDtypeStruct((8, 128), F32),
        ],
        in_specs=[vm, vm, sm, vm, vm, vm, vm],
        out_specs=[vm] * 6,
        scratch_shapes=[
            pltpu.VMEM((rows, frames, width), BF),
            pltpu.VMEM((rows * segs * own_u, width), F32),
            pltpu.VMEM((rows, span, width), BF),
            pltpu.VMEM((rows, span, width), BF),
            pltpu.VMEM((rows, span, TOK), BF),
            pltpu.VMEM((rows, span, 128), F32),
            pltpu.VMEM((frames, 256), F32),
            pltpu.VMEM((labs, frames, 256), F32),
            pltpu.VMEM((16, frames + 24, 128), F32),
            pltpu.VMEM((2, frames + 16, 128), F32),
            pltpu.VMEM((KINDS, frames, 128), F32),
            pltpu.VMEM((rows * segs * own_u, width), BF),
            pltpu.VMEM((labs, micro, frames, width), BF),
            pltpu.VMEM((labs, micro, frames, width), BF),
            pltpu.SemaphoreType.DMA((3, labs)),
            pltpu.SemaphoreType.DMA((3, labs)),
        ],
        compiler_params=pltpu.CompilerParams(
            collective_id=2, has_side_effects=True, vmem_limit_bytes=60 * 2**20
        ),
    )(enc_own, pred, ints, predx, tok, tail, bias)


HEADS = 8
EPS = 1e-05
TAPS = 9
GAIN_ROW = 9
STATE = (
    ("n_ffn", 512, F32), ("n_att", 512, F32), ("n_conv", 512, F32), ("n_depth", 512, F32), ("n_out", 512, F32),
    ("scales", 128, F32), ("act", 2048, BF), ("slope", 2048, BF), ("qkv", 1536, BF), ("context", 512, BF),
    ("value", 512, F32), ("gate", 512, F32),
)


def sigmoid(v):
    return 0.5 * jnp.tanh(0.5 * v) + 0.5


def norm_parts(v):
    c = v - jnp.mean(v, axis=1, keepdims=True)
    r = lax.rsqrt(jnp.mean(c * c, axis=1, keepdims=True) + EPS)
    return c * r, r


def norm_back(gy, n, r, gain):
    gg = gy * gain
    gain_grad = jnp.sum(gy * n, axis=0, keepdims=True)
    inner = gg - jnp.mean(gg, axis=1, keepdims=True) - n * jnp.mean(gg * n, axis=1, keepdims=True)
    return r * inner, gain_grad


def rows_of(ref, n, first, count):
    per = ref.shape[0] // n
    return jnp.concatenate([ref[d * per + first : d * per + first + count, :] for d in range(n)], axis=0)


def put_rows(ref, n, first, count, value):
    per = ref.shape[0] // n
    for d in range(n):
        ref[d * per + first : d * per + first + count, :] = value[d * count : (d + 1) * count].astype(ref.dtype)


def own_ends(ints, micro, segs):
    first = lax.axis_index("lab") * micro
    return [scalar_ends(ints, first + m, segs) for m in range(micro)]


def seg_id(position, ends, frames):
    t, row = position % frames, position // frames
    out = seg_of(t, ends[0])
    for m in range(1, len(ends)):
        out = jnp.where(row == m, seg_of(t, ends[m]), out)
    return out + row * len(ends[0])


def shifted(value, step):
    rows = value.shape[0]
    return pltpu.roll(value, (-step) % rows, 0) if step % rows else value


def assemble_small(target, n, per, ds):
    lane = lane_ids((16, 128))
    columns = [jnp.zeros((16, 128), F32) for _ in range(n * ds // 128)]
    for d in range(n):
        piece = jnp.where(lane < ds, target[d * per : d * per + 16, 256:384].astype(F32), 0.0)
        at = d * ds % 128
        columns[d * ds // 128] = columns[d * ds // 128] + (pltpu.roll(piece, at, 1) if at else piece)
    return jnp.concatenate(columns, axis=1)


def split_small(value, d, ds):
    at = d * ds % 128
    piece = value[:, d * ds // 128 * 128 : d * ds // 128 * 128 + 128]
    piece = pltpu.roll(piece, 128 - at, 1) if at else piece
    return jnp.where(lane_ids((16, 128)) < ds, piece, 0.0)


class Sizes:
    def __init__(self, n, ds, ff, qk, pi, jr):
        self.n, self.ds, self.ff, self.qk, self.pi, self.jr = n, ds, ff, qk, pi, jr
        self.rows = (jr + ff, ff + qk, 2 * ds + pi + jr, 3 * jr)
        self.model = n * ds


def head_pair(ref, block, pair):
    at = block * 512 + pair * 128
    return ref[:, at : at + 128]


def forward_pieces(z, x_ref, ints, dims, full, small_ref, st, probs, encoded, enc_proj):
    frames, rows, segs, own_u, labs = dims
    n, micro = z.n, rows // labs
    count = micro * frames
    ends = own_ends(ints, micro, segs)
    ids_r = seg_id(row_ids((count, 128)), ends, frames)
    ids_c = seg_id(lane_ids((count, count)), ends, frames)
    scale_lane = lane_ids((count, 128))

    def norm(v, name, which):
        nv, r = norm_parts(v)
        st[name][...] = nv
        st["scales"][...] = jnp.where(scale_lane == which, r, st["scales"][...])
        return nv * small_ref[GAIN_ROW + which : GAIN_ROW + which + 1, :]

    small_ref[...] = assemble_small(full[0], n, z.rows[0], z.ds)
    st["scales"][...] = jnp.zeros((count, 128), F32)
    x = x_ref[...].reshape(count, z.model).astype(F32)
    ffn_in = norm(x, "n_ffn", 0).astype(BF)
    half = n // 2
    per = z.rows[0]
    for part in range(2):
        w = jnp.concatenate(
            [full[0][d * per + z.jr : d * per + z.jr + z.ff, :] for d in range(part * half, part * half + half)], axis=0
        )
        pre = mm_t(ffn_in, w)
        sg = sigmoid(pre)
        at = slice(part * half * z.ff, (part + 1) * half * z.ff)
        st["act"][:, at] = (pre * sg).astype(BF)
        st["slope"][:, at] = (sg * (1.0 + pre * (1.0 - sg))).astype(BF)
    yield
    after_ffn = x + 0.5 * mm(st["act"][...], rows_of(full[1], n, 0, z.ff))
    att_in = norm(after_ffn, "n_att", 1).astype(BF)
    st["qkv"][...] = mm_t(att_in, rows_of(full[1], n, z.ff, z.qk)).astype(BF)
    same = ids_r == ids_c
    low_half = lane_ids((count, 128)) < 64
    for pair in range(HEADS // 2):
        q, k, v = (head_pair(st["qkv"], b, pair) for b in range(3))
        total = None
        for side in range(2):
            keep = low_half if side == 0 else ~low_half
            score = mm_t(jnp.where(keep, q, 0), k) * (64 ** -0.5)
            score = jnp.where(same, score, LOW)
            e = jnp.exp(score - jnp.max(score, axis=1, keepdims=True))
            p = (e * (1.0 / jnp.sum(e, axis=1, keepdims=True))).astype(BF)
            probs[2 * pair + side] = p
            part = mm(p, jnp.where(keep, v, 0))
            total = part if total is None else total + part
        st["context"][:, pair * 128 : pair * 128 + 128] = total.astype(BF)
    yield
    after_att = after_ffn + mm(st["context"][...], rows_of(full[2], n, 0, z.ds))
    conv_in = norm(after_att, "n_conv", 2).astype(BF)
    conv_pre = mm_t(conv_in, rows_of(full[2], n, z.ds, z.pi))
    st["value"][...] = conv_pre[:, : z.model]
    st["gate"][...] = sigmoid(conv_pre[:, z.model :])
    depth = []
    for c in range(z.model // 128):
        at = slice(c * 128, c * 128 + 128)
        gated = st["value"][:, at] * st["gate"][:, at]
        total = jnp.zeros((count, 128), F32)
        for j in range(TAPS):
            ok = shifted(ids_r, j - TAPS // 2) == ids_r
            total = total + jnp.where(ok, shifted(gated, j - TAPS // 2), 0.0) * small_ref[j : j + 1, at]
        depth.append(total)
    dn = norm(jnp.concatenate(depth, axis=1), "n_depth", 3)
    conv_act = (dn * sigmoid(dn)).astype(BF)
    after_conv = after_att + mm(conv_act, rows_of(full[2], n, z.ds + z.pi, z.ds))
    out = norm(after_conv, "n_out", 4).astype(BF)
    encoded[...] = out.reshape(encoded.shape)
    enc_proj[...] = mm_t(out, rows_of(full[2], n, 2 * z.ds + z.pi, z.jr)).astype(BF).reshape(enc_proj.shape)
    yield


def backward_pieces(z, g_enc, ints, dims, full, small_ref, st, probs, grads, small_grad, grad_frames):
    frames, rows, segs, own_u, labs = dims
    n, micro = z.n, rows // labs
    count = micro * frames
    ends = own_ends(ints, micro, segs)
    ids_r = seg_id(row_ids((count, 128)), ends, frames)

    def gain(which):
        return small_ref[GAIN_ROW + which : GAIN_ROW + which + 1, :]

    def back(gy, name, which):
        g, gain_grad = norm_back(gy, st[name][...], st["scales"][:, which : which + 1], gain(which))
        small_grad[GAIN_ROW + which : GAIN_ROW + which + 1, :] = gain_grad
        return g

    def normed(name, which):
        return (st[name][...] * gain(which)).astype(BF)

    small_grad[...] = jnp.zeros(small_grad.shape, F32)
    ge = g_enc[...].reshape(count, -1)
    off = 2 * z.ds + z.pi
    put_rows(grads[2], n, off, z.jr, t_mm(ge, normed("n_out", 4)))
    g_conv_sum = back(mm(ge, rows_of(full[2], n, off, z.jr)), "n_out", 4)
    branch = g_conv_sum.astype(BF)
    dn = st["n_depth"][...] * gain(3)
    sg = sigmoid(dn)
    put_rows(grads[2], n, z.ds + z.pi, z.ds, t_mm((dn * sg).astype(BF), branch))
    g_act = mm_t(branch, rows_of(full[2], n, z.ds + z.pi, z.ds))
    g_depth = back(g_act * (sg * (1.0 + dn * (1.0 - sg))), "n_depth", 3)
    yield
    low_a, low_b = [], []
    for c in range(z.model // 128):
        at = slice(c * 128, c * 128 + 128)
        value, gate = st["value"][:, at], st["gate"][:, at]
        gated, gd = value * gate, g_depth[:, at]
        total = jnp.zeros((count, 128), F32)
        for j in range(TAPS):
            step = j - TAPS // 2
            ok = shifted(ids_r, step) == ids_r
            small_grad[j : j + 1, at] = jnp.sum(jnp.where(ok, shifted(gated, step), 0.0) * gd, axis=0, keepdims=True)
            ok = shifted(ids_r, -step) == ids_r
            total = total + jnp.where(ok, shifted(gd, -step), 0.0) * small_ref[j : j + 1, at]
        low_a.append((total * gate).astype(BF))
        low_b.append((total * value * gate * (1.0 - gate)).astype(BF))
    low = jnp.concatenate(low_a + low_b, axis=1)
    put_rows(grads[2], n, z.ds, z.pi, t_mm(low, normed("n_conv", 2)))
    g_att_sum = g_conv_sum + back(mm(low, rows_of(full[2], n, z.ds, z.pi)), "n_conv", 2)
    branch = g_att_sum.astype(BF)
    put_rows(grads[2], n, 0, z.ds, t_mm(st["context"][...], branch))
    g_context = mm_t(branch, rows_of(full[2], n, 0, z.ds)).astype(BF)
    yield
    low_half = lane_ids((count, 128)) < 64
    columns = [[], [], []]
    for pair in range(HEADS // 2):
        q, k, v = (head_pair(st["qkv"], b, pair) for b in range(3))
        gc = g_context[:, pair * 128 : pair * 128 + 128]
        sums = [None, None, None]
        for side in range(2):
            keep = low_half if side == 0 else ~low_half
            p = probs[2 * pair + side]
            gc_h = jnp.where(keep, gc, 0)
            gp = mm_t(gc_h, v)
            pf = p.astype(F32)
            gs = (pf * (gp - jnp.sum(gp * pf, axis=1, keepdims=True))).astype(BF)
            parts = (
                mm(gs, jnp.where(keep, k, 0)) * (64 ** -0.5),
                t_mm(gs, jnp.where(keep, q, 0)) * (64 ** -0.5),
                t_mm(p, gc_h),
            )
            sums = [b if a is None else a + b for a, b in zip(sums, parts)]
        for b in range(3):
            columns[b].append(sums[b].astype(BF))
    g_qkv = jnp.concatenate(columns[0] + columns[1] + columns[2], axis=1)
    yield
    put_rows(grads[1], n, z.ff, z.qk, t_mm(g_qkv, normed("n_att", 1)))
    g_ffn_sum = g_att_sum + back(mm(g_qkv, rows_of(full[1], n, z.ff, z.qk)), "n_att", 1)
    branch = (0.5 * g_ffn_sum).astype(BF)
    put_rows(grads[1], n, 0, z.ff, t_mm(st["act"][...], branch))
    yield
    g_pre = (mm_t(branch, rows_of(full[1], n, 0, z.ff)) * st["slope"][...].astype(F32)).astype(BF)
    put_rows(grads[0], n, z.jr, z.ff, t_mm(g_pre, normed("n_ffn", 0)))
    gx = g_ffn_sum + back(mm(g_pre, rows_of(full[0], n, z.jr, z.ff)), "n_ffn", 0)
    grad_frames[...] = gx.reshape(grad_frames.shape)
    yield


def encode_kernel(
    z, dims, x_ref, ints, w_in, w_out, w_qkv, w_att, w_pin, w_pout, w_enc, w_pred, tail, small_in, w_joint,
    full0, full1, full2, predx, tok, tail_out, small_out, encoded, enc_proj, *rest,
):
    k = len(STATE)
    st = {name: ref for (name, _, _), ref in zip(STATE, rest[:k])}
    probs, rest = rest[k], rest[k + 1 :]
    sources, full = rest[0:4], rest[4:8]
    ring_recv, x_recv, sems, out_sem = rest[8:]
    n = z.n
    w = Where(n)
    w.greet()
    jr, js, ds = z.jr, w_pred.shape[1], z.ds

    def down(value, count):
        return jnp.concatenate([value, jnp.zeros((count - value.shape[0],) + value.shape[1:], value.dtype)], 0) if count > value.shape[0] else value

    pred_t = down(w_pred[...].astype(F32).T.astype(BF), jr)
    sources[0][jr:, :] = w_in[...].astype(F32).T.astype(BF)
    sources[0][:jr, 0:128] = pred_t[:, 512:]
    sources[0][:jr, 128:256] = tail[...]
    sources[0][:jr, 256:] = jnp.zeros((jr, 256), BF)
    sources[0][:16, 256:384] = small_in[...]
    parts = [
        Gather(w, sources[i], full[i], z.rows[i], ring_recv.at[i], x_recv.at[i], sems.at[i]) for i in range(4)
    ]
    turns = n // 2 + 2
    skew = 2

    def fill(g):
        if g == 1:
            sources[1][: z.ff, :] = w_out[...]
            sources[1][z.ff :, :] = w_qkv[...].astype(F32).T.astype(BF)
        elif g == 2:
            sources[2][:ds, :] = w_att[...]
            sources[2][ds : ds + z.pi, :] = w_pin[...].astype(F32).T.astype(BF)
            sources[2][ds + z.pi : 2 * ds + z.pi, :] = w_pout[...]
            sources[2][2 * ds + z.pi :, :] = down(w_enc[...].astype(F32).T.astype(BF), jr)
        elif g == 3:
            sources[3][:jr, :] = pred_t[:, :512]
            sources[3][jr : 2 * jr, :] = down(w_joint[:, :512], jr)
            sources[3][2 * jr :, :] = down(w_joint[:, 512:1024], jr)

    def tick(i):
        for s in range(turns - 1, -1, -1):
            g = i - skew * s
            if 0 <= g < 4:
                if s == 0:
                    fill(g)
                parts[g].step(s)

    outs = (full0, full1, full2)

    def finish(g):
        parts[g].whole()
        if g < 3:
            pltpu.make_async_copy(full[g], outs[g], out_sem.at[g]).start()

    last = 4 + skew * (turns - 1)
    compute = forward_pieces(z, x_ref, ints, dims, full, small_out, st, probs, encoded, enc_proj)
    done = 0
    for i in range(last):
        tick(i)
        g = i - skew * (turns - 1)
        if g >= 0:
            finish(g)
            if g < 3:
                next(compute)
    predx[:, :512] = rows_of(full[3], n, 0, jr)
    tok[:, :512] = rows_of(full[3], n, jr, jr)
    tok[:, 512:] = rows_of(full[3], n, 2 * jr, jr)
    mixes = rows_of(full[0], n, 0, jr)
    predx[:, 512:] = mixes[:, :256]
    tail_out[...] = mixes[:, 128:256]
    for part in parts:
        part.drain()
    for g in range(3):
        pltpu.make_async_copy(full[g], outs[g], out_sem.at[g]).wait()


def encode_call(z, dims, x, ints, w_in, w_out, w_qkv, w_att, w_pin, w_pout, w_enc, w_pred, tail, small, w_joint):
    frames, rows, segs, own_u, labs = dims
    n, micro = z.n, rows // labs
    count, width = micro * frames, n * z.jr
    vm, sm, hbm = (pl.BlockSpec(memory_space=m) for m in (pltpu.VMEM, pltpu.SMEM, pl.ANY))
    shape = jax.ShapeDtypeStruct
    outs = [shape((n * z.rows[i], 512), BF) for i in range(3)]
    outs += [shape((width, 768), BF), shape((width, 1024), BF), shape((width, 128), BF), shape((16, z.model), F32)]
    outs += [shape((micro, frames, z.model), BF), shape((micro, frames, width), BF)]
    outs += [shape((count, lanes), dtype) for _, lanes, dtype in STATE]
    outs += [shape((HEADS, count, count), BF)]
    return pl.pallas_call(
        functools.partial(encode_kernel, z, dims),
        out_shape=outs,
        in_specs=[vm, sm] + [vm] * 11,
        out_specs=[hbm] * 3 + [vm] * (len(outs) - 3),
        scratch_shapes=[pltpu.VMEM((r, 512), BF) for r in z.rows]
        + [pltpu.VMEM((n * r, 512), BF) for r in z.rows]
        + [
            pltpu.SemaphoreType.DMA((4, n - 1)),
            pltpu.SemaphoreType.DMA((4, n - 1)),
            pltpu.SemaphoreType.DMA((4, 5)),
            pltpu.SemaphoreType.DMA((3,)),
        ],
        compiler_params=pltpu.CompilerParams(collective_id=0, has_side_effects=True, vmem_limit_bytes=60 * 2**20),
    )(x, ints, w_in, w_out, w_qkv, w_att, w_pin, w_pout, w_enc, w_pred, tail, small, w_joint)


def grad_kernel(z, dims, skew, *refs):
    g_enc, ints, small_ref, g_pack, g_mix, g_bias = refs[:6]
    hbm = refs[6:9]
    refs = refs[9:]
    k = len(STATE)
    st = {name: ref for (name, _, _), ref in zip(STATE, refs[:k])}
    probs, refs = refs[k], refs[k + 1 :]
    outs, grad_frames, refs = refs[:4], refs[4], refs[5:]
    full, refs = refs[:3], refs[3:]
    grads, refs = list(refs[:3]) + [g_pack], refs[3:]
    small_grad, bufs, (send, recv, in_sem) = refs[0], refs[1:17], refs[17:]
    n = z.n
    w = Where(n)
    w.far_back = (ring_device(w.place + 2 * w.core - 1, n), w.lab)
    for g in (2, 1, 0):
        pltpu.make_async_copy(hbm[g], full[g], in_sem.at[g]).start()
    w.greet()
    order = (3, 2, 1, 0)
    parts = [
        Scatter(w, grads[g], outs[g], z.rows[g], bufs[4 * g : 4 * g + 4], send.at[g], recv.at[g]) for g in order
    ]
    stages = n // 2 + 5
    compute = backward_pieces(z, g_enc, ints, dims, full, small_ref, st, probs, grads, small_grad, grad_frames)

    def load(g):
        pltpu.make_async_copy(hbm[g], full[g], in_sem.at[g]).wait()

    def work(i):
        if i == 1:
            load(2)
            next(compute)
            next(compute)
        elif i == 2:
            load(1)
            next(compute)
            next(compute)
        elif i == 3:
            load(0)
            next(compute)
            per, ds = z.rows[0], z.ds
            for d in range(n):
                at = d * per
                grads[0][at : at + z.jr, :256] = g_mix[d * z.jr : (d + 1) * z.jr, :]
                if z.jr > 32:
                    grads[0][at + 32 : at + z.jr, 256:] = jnp.zeros((z.jr - 32, 256), BF)
                grads[0][at : at + 16, 256:384] = split_small(small_grad[...], d, ds).astype(BF)
                grads[0][at : at + 16, 384:] = jnp.zeros((16, 128), BF)
                grads[0][at + 16 : at + 32, 256:] = g_bias[...].astype(BF)

    for tick in range(4 + skew * (stages - 1)):
        for s in range(stages - 1, -1, -1):
            g = tick - skew * s
            if 0 <= g < 4:
                if s == 0:
                    work(g)
                parts[g].stage(s)
    for part in parts:
        part.drain()


def grad_call(z, dims, g_enc, ints, small, g_pack, g_mix, g_bias, full, state, probs, skew=1):
    frames, rows, segs, own_u, labs = dims
    n, micro = z.n, rows // labs
    vm, sm, hbm = (pl.BlockSpec(memory_space=m) for m in (pltpu.VMEM, pltpu.SMEM, pl.ANY))
    shape = jax.ShapeDtypeStruct
    scratch = [pltpu.VMEM((n * z.rows[g], 512), BF) for g in range(3)] * 2 + [pltpu.VMEM((16, z.model), F32)]
    for r in z.rows:
        scratch += scatter_scratch(n, r, 512)
    return pl.pallas_call(
        functools.partial(grad_kernel, z, dims, skew),
        out_shape=[shape((r, 512), BF) for r in z.rows] + [shape((micro, frames, z.model), F32)],
        in_specs=[vm, sm, vm, vm, vm, vm] + [hbm] * 3 + [vm] * (len(STATE) + 1),
        out_specs=[vm] * 5,
        scratch_shapes=scratch + scatter_sems(n, 4) + [pltpu.SemaphoreType.DMA((3,))],
        compiler_params=pltpu.CompilerParams(collective_id=1, has_side_effects=True, vmem_limit_bytes=60 * 2**20),
    )(g_enc, ints, small, g_pack, g_mix, g_bias, *full, *state, probs)

def pad_to(value, rows, lanes):
    return jnp.pad(value, ((0, rows - value.shape[0]), (0, lanes - value.shape[1])))


def local(
    frames_in, predictor, seg_lengths, label_counts, label_ids, gain_ffn, w_ffn_in, w_ffn_out, gain_att, w_qkv,
    w_att_out, gain_conv, w_point_in, w_depth, gain_depth, w_point_out, gain_out, w_enc, w_pred, bias_joint,
    w_joint_out, bias_out,
):
    n, labs = lax.axis_size("dp"), lax.axis_size("lab")
    micro, frames, model = frames_in.shape
    rows, segs, own_u, joint = predictor.shape
    ds, js = model // n, w_pred.shape[1]
    jr = max(-(-js // TILE), 2) * TILE
    z = Sizes(n, ds, w_ffn_in.shape[1], w_qkv.shape[1], w_point_in.shape[1], jr)
    dims = (frames, rows, segs, own_u, labs)
    tail = pad_to(jnp.concatenate([w_joint_out[:, TOK:], bias_joint[:, None]], axis=1), jr, 128)
    gains = jnp.stack([gain_ffn, gain_att, gain_conv, gain_depth, gain_out])
    small = pad_to(jnp.concatenate([w_depth, gains]), 16, 128)
    ints = jnp.concatenate([seg_lengths, label_counts, label_ids.reshape(rows, segs * own_u)], axis=1)
    out = encode_call(
        z, dims, frames_in, ints, w_ffn_in, w_ffn_out, w_qkv, w_att_out, w_point_in, w_point_out, w_enc, w_pred,
        tail, small, w_joint_out,
    )
    full, (predx, tok, tail_w, small_w, encoded, enc_proj) = out[:3], out[3:9]
    state, probs = out[9:-1], out[-1]
    pred_ext = pad_to(predictor.reshape(-1, joint), rows * segs * own_u, 768)
    pred_ext = jnp.where(lax.broadcasted_iota(jnp.int32, pred_ext.shape, 1) == joint + BIAS_LANE, 1.0, pred_ext).astype(BF)
    bias = jnp.pad(bias_out.astype(F32), (0, TOK + 128 - bias_out.shape[0]))[None]
    g_enc, g_predictor, g_pack, g_mix, g_bias, loss = joint_call(
        enc_proj, pred_ext, ints, predx, tok, tail_w, bias, dims
    )
    own0, own1, own2, own3, grad_frames = grad_call(
        z, dims, g_enc, ints, small_w, g_pack, g_mix, g_bias, full, state, probs
    )
    ff, pi = z.ff, z.pi
    own0, own1, own2, own3 = (g.astype(F32) for g in (own0, own1, own2, own3))
    g_small = own0[:16, 256 : 256 + ds]
    g_pred_t = jnp.concatenate([own3[:js], own0[:js, :128]], axis=1)
    g_joint = jnp.concatenate([own3[jr : jr + js], own3[2 * jr : 2 * jr + js], own0[:js, 128:134]], axis=1)
    g_bias_out = jnp.concatenate([own0[16:20, 256:].reshape(-1), own0[20, 256:262]])
    loss_out = loss[:segs, : rows * own_u : own_u].T
    return (
        loss_out, encoded, grad_frames, g_predictor.reshape(predictor.shape),
        g_small[9], own0[jr:].T, own1[:ff], g_small[10], own1[ff:].T, own2[:ds], g_small[11],
        own2[ds : ds + pi].T, g_small[:9], g_small[12], own2[ds + pi : 2 * ds + pi], g_small[13],
        own2[2 * ds + pi : 2 * ds + pi + js].T, g_pred_t.T, own0[:js, 128 + BIAS_LANE], g_joint, g_bias_out,
    )


def solution(mesh):
    rows, whole = P(("dp", "lab"), None, None), P()
    predictor, columns, lines, vector = P("dp", None, "lab", None), P(None, "dp"), P("dp", None), P("dp")
    params = (
        vector, columns, lines, vector, columns, lines, vector, columns, columns, vector, lines, vector, columns,
        columns, vector, lines, whole,
    )
    return jax.shard_map(
        local,
        mesh=mesh,
        in_specs=(rows, predictor, lines, lines, P("dp", None, "lab")) + params,
        out_specs=(lines, rows, rows, predictor) + params,
        check_vma=False,
    )
```

```python
import functools

import jax
import jax.numpy as jnp
from jax import lax
from jax.experimental import pallas as pl
from jax.experimental.pallas import tpu as pltpu
from jax.sharding import PartitionSpec as P


MESH = pl.DeviceIdType.MESH
F32 = jnp.float32
BF = jnp.bfloat16
TILE = 16


def ring_place(dp, n):
    odd = dp % 2
    return (1 - odd) * (dp // 2) + odd * (n - 1 - dp // 2)


def ring_device(place, n):
    place = (place + 2 * n) % n
    high = place // (n // 2)
    return (1 - high) * (2 * place) + high * (2 * (n - 1 - place) + 1)


def x_rows(rows, share):
    tiles = rows // TILE
    return min(tiles // 2, int(tiles * share + 0.5)) * TILE


class Where:
    def __init__(self, n):
        self.n = n
        self.dp = lax.axis_index("dp")
        self.lab = lax.axis_index("lab")
        self.core = self.lab % 2
        self.side = self.lab // 2
        self.place = ring_place(self.dp, n)
        self.right = (ring_device(self.place + 1, n), self.lab)
        self.left = (ring_device(self.place - 1, n), self.lab)
        self.twin = (self.dp, self.side * 2 + 1 - self.core)
        self.across = (self.dp, (1 - self.side) * 2 + self.core)
        self.far = (
            ring_device(self.place + 1 - 2 * self.core, n),
            self.lab,
        )

    def at(self, distance):
        return ring_device(self.place + distance, self.n)

    def greet(self):
        barrier = pltpu.get_barrier_semaphore()
        for other in (self.right, self.left, self.twin, self.across):
            pl.semaphore_signal(barrier, inc=1, device_id=other, device_id_type=MESH)
        pl.semaphore_wait(barrier, 4)


def remote(src, dst, send_sem, recv_sem, device):
    return pltpu.make_async_remote_copy(
        src_ref=src,
        dst_ref=dst,
        send_sem=send_sem,
        recv_sem=recv_sem,
        device_id=device,
        device_id_type=MESH,
    )


class Gather:
    def __init__(self, where, source, target, rows, ring_recv, x_recv, sems):
        self.w, self.source, self.target, self.rows = where, source, target, rows
        self.width = target.shape[1]
        self.half = self.width // 2
        self.cut = x_rows(rows, 0.3)
        self.ring_recv, self.x_recv, self.sems = ring_recv, x_recv, sems
        self.steps = where.n // 2

    def lanes(self):
        return pl.ds(pl.multiple_of(self.w.core * self.half, 128), self.half)

    def rows_at(self, shard, offset, size):
        base = shard * self.rows if shard is not None else 0
        return pl.ds(pl.multiple_of(base + offset, TILE), size)

    def ring_part(self, ref, shard):
        return ref.at[self.rows_at(shard, self.w.side * self.cut, self.rows - self.cut), self.lanes()]

    def x_part(self, ref, shard, side):
        return ref.at[self.rows_at(shard, side * (self.rows - self.cut), self.cut), self.lanes()]

    def slot(self, distance):
        return distance + self.steps - 1 if distance < 0 else distance + self.steps - 2

    def hop(self, distance, first):
        w = self.w
        if distance == self.steps:
            shard = w.at((2 * w.core - 1) * (self.steps - 1))
            device = w.far
        else:
            shard = w.at(distance + 1) if distance < 0 else w.at(distance - 1)
            device = w.right if distance < 0 else w.left
        src = self.ring_part(self.source, None) if first else self.ring_part(self.target, shard)
        slot = 2 * self.steps - 2 if distance == self.steps else self.slot(distance)
        remote(src, self.ring_part(self.target, shard), self.sems.at[1], self.ring_recv.at[slot], device).start()

    def own(self):
        pltpu.make_async_copy(
            self.source, self.target.at[self.rows_at(self.w.dp, 0, self.rows), :], self.sems.at[4]
        ).start()

    def arrived(self, distance):
        w = self.w
        shard = w.at(distance)
        slot = 2 * self.steps - 2 if distance == self.steps else self.slot(distance)
        part = self.ring_part(self.target, shard)
        remote(part, part, self.sems.at[1], self.ring_recv.at[slot], w.right).wait_recv()

    def spread(self, distance):
        w = self.w
        shard = w.at(distance)
        slot = 2 * self.steps - 2 if distance == self.steps else self.slot(distance)
        if self.cut:
            part = self.x_part(self.target, shard, w.side)
            remote(part, part, self.sems.at[2], self.x_recv.at[slot], w.across).start()
        part = self.ring_part(self.target, shard)
        remote(part, part, self.sems.at[3], self.sems.at[0], w.twin).start()

    def crossed(self, distance):
        if not self.cut:
            return
        w = self.w
        shard = w.at(distance)
        slot = 2 * self.steps - 2 if distance == self.steps else self.slot(distance)
        part = self.x_part(self.target, shard, 1 - w.side)
        remote(part, part, self.sems.at[2], self.x_recv.at[slot], w.across).wait_recv()
        remote(part, part, self.sems.at[3], self.sems.at[0], w.twin).start()

    def whole(self):
        part = self.target.at[pl.ds(0, (self.w.n - 1) * self.rows), pl.ds(0, self.half)]
        remote(part, part, self.sems.at[3], self.sems.at[0], self.w.twin).wait_recv()
        pltpu.make_async_copy(
            self.source, self.target.at[self.rows_at(self.w.dp, 0, self.rows), :], self.sems.at[4]
        ).wait()

    def drain(self):
        count = self.w.n - 1
        for sem, rows in ((1, self.rows - self.cut), (2, self.cut), (3, self.rows)):
            if rows:
                part = self.target.at[pl.ds(0, count * rows), pl.ds(0, self.half)]
                remote(part, part, self.sems.at[sem], self.sems.at[sem], self.w.twin).wait_send()

    def step(self, s):
        if s == 0:
            self.own()
        if 1 <= s < self.steps:
            self.arrived(-s)
            self.arrived(s)
        if s == self.steps:
            self.arrived(self.steps)
        if s < self.steps - 1:
            self.hop(-s - 1, s == 0)
            self.hop(s + 1, s == 0)
        elif s == self.steps - 1:
            self.hop(self.steps, False)
        if 1 <= s < self.steps:
            self.spread(-s)
            self.spread(s)
        if s == self.steps:
            self.spread(self.steps)
        if 2 <= s <= self.steps:
            self.crossed(-s + 1)
            self.crossed(s - 1)
        if s == self.steps + 1:
            self.crossed(self.steps)


def gather_kernel(n, rows_list, *refs):
    k = len(rows_list)
    sources, targets = refs[:k], refs[k : 2 * k]
    ring_recv, x_recv, sems = refs[2 * k :]
    w = Where(n)
    w.greet()
    parts = [
        Gather(w, sources[i], targets[i], rows_list[i], ring_recv.at[i], x_recv.at[i], sems.at[i])
        for i in range(k)
    ]
    turns = n // 2 + 2
    for tick in range(k + turns - 1):
        for s in range(turns - 1, -1, -1):
            g = tick - s
            if 0 <= g < k:
                parts[g].step(s)
    for part in parts:
        part.whole()
        part.drain()


def gather_all(n, shards):
    k = len(shards)
    rows_list = [s.shape[0] for s in shards]
    return pl.pallas_call(
        functools.partial(gather_kernel, n, rows_list),
        out_shape=[jax.ShapeDtypeStruct((n * s.shape[0], s.shape[1]), s.dtype) for s in shards],
        in_specs=[pl.BlockSpec(memory_space=pltpu.VMEM)] * k,
        out_specs=[pl.BlockSpec(memory_space=pltpu.VMEM)] * k,
        scratch_shapes=[
            pltpu.SemaphoreType.DMA((k, n - 1)),
            pltpu.SemaphoreType.DMA((k, n - 1)),
            pltpu.SemaphoreType.DMA((k, 5)),
        ],
        compiler_params=pltpu.CompilerParams(
            collective_id=0, has_side_effects=True, vmem_limit_bytes=56 * 2**20
        ),
    )(*shards)


class Pair:
    def __init__(self, where, grads, held, rows, send, recv):
        self.w, self.grads, self.held, self.rows = where, grads, held, rows
        self.half = grads.shape[1] // 2
        self.copy = remote(self.grads.at[:, self.lanes(1 - where.core)], held, send.at[0], recv.at[0], where.twin)

    def lanes(self, core):
        return pl.ds(pl.multiple_of(core * self.half, 128), self.half)

    def give(self):
        self.copy.start()

    def add(self):
        self.copy.wait_recv()

        def body(i, _):
            at = pl.ds(pl.multiple_of(i * self.rows, TILE), self.rows)
            self.held[at, :] = (
                self.held[at, :].astype(F32) + self.grads[at, self.lanes(self.w.core)].astype(F32)
            ).astype(BF)
            return 0

        lax.fori_loop(0, self.w.n, body, 0)

    def drain(self):
        self.copy.wait_send()


class Chain:
    def __init__(self, pair, out, crossed, bufs, send, recv, share):
        self.pair, self.w, self.out, self.crossed = pair, pair.w, out, crossed
        self.cut = x_rows(pair.rows, share)
        self.size = self.cut if crossed else pair.rows - 2 * self.cut
        self.depth = self.w.n // 2 - 1
        self.xbuf, self.rbuf = bufs
        self.send, self.recv = send, recv
        self.stages = self.depth + 5

    def first(self, side):
        return side * (self.pair.rows - self.cut) if self.crossed else self.cut

    def rows_at(self, shard, side=None):
        base = shard * self.pair.rows + self.first(self.w.side if side is None else side)
        return pl.ds(pl.multiple_of(base, TILE), self.size)

    def out_at(self, side=None):
        at = pl.ds(pl.multiple_of(self.first(self.w.side if side is None else side), TILE), self.size)
        return self.out.at[at, self.pair.lanes(self.w.core)]

    def got(self, sem, dst):
        remote(dst, dst, self.send.at[0], self.recv.at[sem], self.w.twin).wait_recv()

    def ring(self, slot, src, device):
        remote(src, self.rbuf.at[slot], self.send.at[1], self.recv.at[slot], device).start()

    def stage(self, s):
        if not self.size:
            return
        w, n, depth, held = self.w, self.w.n, self.depth, self.pair.held
        last = 2 * depth + 1
        if s == 0:
            if self.crossed:
                for i in range(n):
                    remote(
                        held.at[self.rows_at(i, 1 - w.side), :], self.xbuf.at[i], self.send.at[0], self.recv.at[last],
                        w.across,
                    ).start()
        elif s == 1:
            if self.crossed:
                self.got(last, self.xbuf)

                def body(i, _):
                    at = self.rows_at(i)
                    held[at, :] = (held[at, :].astype(F32) + self.xbuf[i].astype(F32)).astype(BF)
                    return 0

                lax.fori_loop(0, n, body, 0)
            dest = w.at((2 * w.core - 1) * (depth + 1))
            self.ring(2 * depth, held.at[self.rows_at(dest), :], w.far_back)
        elif s < 2 + depth:
            hop = s - 2
            for way in (0, 1):
                sign = 1 - 2 * way
                own = held[self.rows_at(w.at(sign * (depth - hop))), :].astype(F32)
                slot = 2 * hop + way
                if hop == 0:
                    if way == 0:
                        self.got(2 * depth, self.rbuf.at[2 * depth])
                    far = self.rbuf[2 * depth].astype(F32)
                    pick = w.core if way == 0 else 1 - w.core
                    own = own + jnp.where(pick == 1, far, 0.0)
                    at = 2 * depth + 1 + way
                else:
                    at = slot - 2
                    self.got(at, self.rbuf.at[at])
                    own = own + self.rbuf[at].astype(F32)
                self.rbuf[at] = own.astype(BF)
                self.ring(slot, self.rbuf.at[at], w.right if way == 0 else w.left)
        elif s == 2 + depth:
            total = held[self.rows_at(w.dp), :].astype(F32)
            for way in (0, 1):
                at = 2 * depth - 2 + way
                self.got(at, self.rbuf.at[at])
                total = total + self.rbuf[at].astype(F32)
            if self.crossed:
                mine = self.out_at()
                mine[...] = total.astype(BF)
                remote(mine, mine, self.send.at[2], self.recv.at[last + 1], w.across).start()
                remote(mine, mine, self.send.at[3], self.recv.at[last + 2], w.twin).start()
            else:
                self.xbuf[0] = total.astype(BF)
                remote(self.xbuf.at[0], self.xbuf.at[1], self.send.at[2], self.recv.at[last + 1], w.across).start()
        elif s == 3 + depth:
            if self.crossed:
                other = self.out_at(1 - w.side)
                self.got(last + 1, other)
                remote(other, other, self.send.at[4], self.recv.at[last + 3], w.twin).start()
            else:
                self.got(last + 1, self.xbuf.at[1])
                mine = self.out_at()
                mine[...] = (self.xbuf[0].astype(F32) + self.xbuf[1].astype(F32)).astype(BF)
                remote(mine, mine, self.send.at[3], self.recv.at[last + 2], w.twin).start()
        elif s == 4 + depth:
            part = self.out_at()
            self.got(last + 2, part)
            if self.crossed:
                self.got(last + 3, part)

    def drain(self):
        if not self.size:
            return
        ring = self.rbuf.at[pl.ds(0, 2 * self.depth + 1)]
        remote(ring, ring, self.send.at[1], self.recv.at[0], self.w.twin).wait_send()
        part = self.out_at()
        remote(part, part, self.send.at[2], self.recv.at[0], self.w.twin).wait_send()
        remote(part, part, self.send.at[3], self.recv.at[0], self.w.twin).wait_send()
        if self.crossed:
            remote(part, part, self.send.at[4], self.recv.at[0], self.w.twin).wait_send()
            remote(self.xbuf, self.xbuf, self.send.at[0], self.recv.at[0], self.w.twin).wait_send()


def scatter_scratch(n, rows, width, share):
    half, cut, depth = width // 2, x_rows(rows, share), n // 2 - 1
    out = [pltpu.VMEM((n * rows, half), BF)]
    for count, size in ((2, rows - 2 * cut), (n, cut)):
        out += [pltpu.VMEM((count, max(size, TILE), half), BF), pltpu.VMEM((2 * depth + 3, max(size, TILE), half), BF)]
    return out


def scatter_sems(n, k):
    return [pltpu.SemaphoreType.DMA((k, 11)), pltpu.SemaphoreType.DMA((k, 2 * n + 8))]


class Scatter:
    def __init__(self, where, grads, out, rows, bufs, send, recv, share):
        n = where.n
        self.pair = Pair(where, grads, bufs[0], rows, send.at[pl.ds(10, 1)], recv.at[pl.ds(2 * n + 7, 1)])
        self.straight = Chain(self.pair, out, False, bufs[1:3], send.at[pl.ds(0, 5)], recv.at[pl.ds(0, n + 2)], share)
        self.crossed = Chain(self.pair, out, True, bufs[3:5], send.at[pl.ds(5, 5)], recv.at[pl.ds(n + 2, n + 3)], share)

    def drain(self):
        for part in (self.pair, self.straight, self.crossed):
            part.drain()


def sum_up(parts, work, order):
    depth = parts[0].straight.depth
    for what, g, stage in order:
        part = parts[g]
        if what == 0:
            work(g)
            part.pair.give()
        elif what == 1:
            part.pair.add()
        else:
            chain = part.straight if what == 2 else part.crossed
            stages = [stage] if stage < 4 else range(4, depth + 2) if stage == 4 else [stage + depth - 3]
            for s in stages:
                chain.stage(s)
    for part in parts:
        part.drain()


LOW = -100000.0
TOK = 1024
KINDS = 7
BIAS_LANE = 6


def mm(a, b):
    return lax.dot_general(a, b, (((1,), (0,)), ((), ())), preferred_element_type=F32)


def mm_t(a, b):
    return lax.dot_general(a, b, (((1,), (1,)), ((), ())), preferred_element_type=F32)


def t_mm(a, b):
    return lax.dot_general(a, b, (((0,), (0,)), ((), ())), preferred_element_type=F32)


def lane_ids(shape):
    return lax.broadcasted_iota(jnp.int32, shape, len(shape) - 1)


def row_ids(shape):
    return lax.broadcasted_iota(jnp.int32, shape, 0)


class Peers:
    def __init__(self):
        self.dp, self.lab = lax.axis_index("dp"), lax.axis_index("lab")
        self.core, self.side = self.lab % 2, self.lab // 2

    def owner(self, j):
        return ((self.side + j // 2) % 2) * 2 + (self.core + j % 2) % 2

    def device(self, j):
        return (self.dp, self.owner(j))


def seg_of(t, ends):
    return sum((t >= e).astype(jnp.int32) for e in ends[:-1])


def pick(seg, values):
    out = values[0]
    for s in range(1, len(values)):
        out = jnp.where(seg == s, values[s], out)
    return out


def scalar_ends(lengths, r, segs):
    ends, total = [], 0
    for s in range(segs):
        total = total + lengths[s, r]
        ends.append(total)
    return ends


def lse_of(terms):
    top = functools.reduce(jnp.maximum, terms)
    return top, functools.reduce(jnp.add, [jnp.exp(v - top) for v in terms])


def lattice(peers, lengths, counts, terms, skewed, hist, grads, loss, dims):
    frames, rows, segs, own_u, labs = dims
    wide = (frames, 128)
    lane = lane_ids(wide)
    group = rows * own_u
    j, row, u = lane % own_u, (lane % group) // own_u, (lane // group) * own_u + lane % own_u
    t = row_ids(wide)
    all_ends = [scalar_ends(lengths, r, segs) for r in range(rows)]

    def per_lane(values):
        out = jnp.zeros(wide, jnp.int32)
        for r in range(rows):
            out = jnp.where(row == r, values[r], out)
        return out

    ends = [per_lane([all_ends[r][s] for r in range(rows)]) for s in range(segs)]
    labels_in = [per_lane([counts[s, r] for r in range(rows)]) for s in range(segs)]
    seg = seg_of(t, ends)
    stop = pick(seg, ends)
    begin = pick(seg, [jnp.zeros(wide, jnp.int32)] + ends[:-1])
    target = pick(seg, labels_in)
    remain, first = stop - t, t == begin

    kinds = []
    per_vreg = 128 // group
    for k in range(KINDS):
        value = None
        for dev in range(labs):
            part = terms[dev, :, (k // per_vreg) * 128 : (k // per_vreg) * 128 + 128]
            shift = (dev - k % per_vreg) * group % 128
            part = pltpu.roll(part, shift, 1) if shift else part
            value = part if value is None else jnp.where(lane // group == dev, part, value)
        kinds.append(value)
    blank_lp, durs, label_lp = kinds[0], kinds[1:6], kinds[6]
    last_u = own_u * labs - 1
    emit, blank, blank_raw = [], [None], [None]
    for d in range(5):
        ok = (u < last_u) & (d <= remain - 1)
        emit.append(jnp.where(ok, label_lp + durs[d], LOW))
        if d:
            blank_raw.append(blank_lp + durs[d])
            blank.append(jnp.where(d <= remain - 1, blank_raw[d], LOW))
    final = (u == target) & (remain <= 4)
    closing = jnp.zeros(wide, F32)
    for d in range(1, 5):
        closing = jnp.where(remain == d, blank_raw[d], closing)
    closing = jnp.where(final, closing, LOW)
    start = jnp.where(first & (u == 0), 0.0, LOW)

    tall = frames + 16
    tall_u = (lane_ids((tall, 128)) // group) * own_u + lane_ids((tall, 128)) % own_u
    tall_j = lane_ids((tall, 128)) % own_u
    pad = jnp.full((16, 128), LOW, F32)

    def skew(value):
        value = jnp.concatenate([value, pad], axis=0)
        for bit in (1, 2, 4, 8):
            value = jnp.where((tall_u // bit) % 2 == 1, pltpu.roll(value, bit, 0), value)
        return value

    def unskew(value):
        for bit in (1, 2, 4, 8):
            value = jnp.where((tall_u // bit) % 2 == 1, pltpu.roll(value, tall - bit, 0), value)
        return value[:frames]

    up = 128 - (group - own_u + 1)

    def next_up(value, jj):
        return jnp.where(jj == 0, pltpu.roll(value, group - own_u + 1, 1), pltpu.roll(value, 1, 1))

    def next_down(value, jj):
        return jnp.where(jj == own_u - 1, pltpu.roll(value, up, 1), pltpu.roll(value, 127, 1))

    lead = jnp.full((8, 128), LOW, F32)

    def keep(i, value):
        skewed[i, 0:8, :] = lead
        skewed[i, 8 : 8 + tall, :] = value

    for d in range(1, 5):
        keep(d - 1, skew(blank[d]))
    for d in range(5):
        value = skew(emit[d])
        keep(4 + d, value)
        keep(9 + d, next_up(value, tall_j))
    keep(14, skew(start))
    keep(15, skew(closing))
    waves = frames + last_u
    one_j = lane_ids((1, 128)) % own_u
    low_row = skewed[0, 0:1, :]

    def at(i, w):
        return skewed[i, pl.ds(w + 8, 1), :]

    def combine(old, near):
        top_old, sum_old = lse_of(old)
        top = functools.reduce(jnp.maximum, near, top_old)
        total = sum_old * jnp.exp(top_old - top)
        for v in near:
            total = total + jnp.exp(v - top)
        return top + jnp.log(total)

    def wave(i, carry):
        a, ra, b, rb = carry
        old = [at(14, i)]
        for d in range(2, 5):
            old.append(a[d - 1] + at(d - 1, i - d))
        for d in range(2, 6):
            old.append(ra[d - 1] + at(8 + d, i - d))
        new_a = combine(old, [a[0] + at(0, i - 1), ra[0] + at(9, i - 1)])
        back = waves - 1 - i
        old = [at(15, back)]
        for d in range(2, 5):
            old.append(b[d - 1] + at(d - 1, back))
        for d in range(2, 6):
            old.append(rb[d - 1] + at(3 + d, back))
        new_b = combine(old, [b[0] + at(0, back), rb[0] + at(4, back)])
        hist[0, pl.ds(i, 1), :] = new_a
        hist[1, pl.ds(back, 1), :] = new_b
        return (
            (new_a,) + a[:-1],
            (next_up(new_a, one_j),) + ra[:-1],
            (new_b,) + b[:-1],
            (next_down(new_b, one_j),) + rb[:-1],
        )

    hist[...] = jnp.full(hist.shape, LOW, F32)
    lax.fori_loop(
        0, waves, wave, ((low_row,) * 4, (low_row,) * 5, (low_row,) * 4, (low_row,) * 5)
    )
    alpha, beta = unskew(hist[0]), unskew(hist[1])
    ahead = next_down(beta, j)
    norm = jnp.zeros(wide, F32)
    heads = jnp.where(first & (u == 0), beta, 0.0)
    for s in range(segs):
        value = jnp.sum(jnp.where(seg == s, heads, 0.0), axis=0, keepdims=True)
        step = 1
        while step < own_u:
            value = value + pltpu.roll(value, step, 1)
            step *= 2
        step = group
        while step < 128:
            value = value + pltpu.roll(value, step, 1)
            step *= 2
        norm = jnp.where(seg == s, value, norm)
        length = ends[s] - (ends[s - 1] if s else 0)
        loss[pl.ds(s, 1), :] = -value / length[:1].astype(F32)
    base = alpha - norm
    total_a, total_b = None, None
    for d in range(5):
        there = pltpu.roll(ahead, frames - d, 0) if d else ahead
        g = -jnp.exp(base + emit[d] + there)
        total_a = g if d == 0 else total_a + g
        if d:
            gb = -jnp.exp(base + blank[d] + pltpu.roll(beta, frames - d, 0))
            gb = gb - jnp.exp(jnp.where(final & (remain == d), base + blank_raw[d], LOW))
            total_b = gb if d == 1 else total_b + gb
            g = g + gb
        grads[1 + d] = g
    grads[0] = total_b
    grads[6] = total_a


def joint_kernel(
    dims,
    enc_own, predictor, lengths, counts, labels, predx, tok, tail, bias_out,
    g_enc, g_predictor, g_pack, g_mix, g_bias, loss,
    enc_all, pred_wide, pred, proj, hid, slope, wide, back_w, prob, prob_tail, mine, terms, skewed, hist, grads, g_pred,
    part, came, send, recv,
):
    frames, rows, segs, own_u, labs = dims
    micro = rows // labs
    peers = Peers()
    barrier = pltpu.get_barrier_semaphore()
    for j in range(1, labs):
        pl.semaphore_signal(barrier, inc=1, device_id=peers.device(j), device_id_type=MESH)
    pl.semaphore_wait(barrier, labs - 1)
    width = enc_own.shape[-1]
    span = own_u * frames
    own_rows = pl.ds(peers.lab * micro, micro)

    def enc_copy(j, source):
        return remote(enc_own, enc_all.at[pl.ds(source * micro, micro)], send.at[0, j], recv.at[0, j], peers.device(j))

    for j in range(1, labs):
        enc_copy(j, peers.lab).start()
    enc_all[own_rows] = enc_own[...]
    features = predictor.shape[-1]
    for r in range(rows):
        for s in range(segs):
            first = (r * segs + s) * own_u
            pred_wide[first : first + own_u, :] = predictor[r, s].astype(F32)
    pred[:, :features] = pred_wide[...].astype(BF)
    pred[:, features:] = (lane_ids((pred.shape[0], 128)) == BIAS_LANE).astype(BF)
    proj[...] = mm_t(pred[...], predx[...])
    wide[:width, :TOK] = tok[...]
    wide[:width, TOK:VOCAB] = tail[...]
    top_row = row_ids((128, TOK)) == 0
    wide[width:, :TOK] = jnp.where(top_row, bias_out[:, :TOK].astype(F32), 0.0).astype(BF)
    mine[:, :128] = jnp.zeros((frames, 128), F32)
    mine[:1, : bias_out.shape[1] - TOK] = bias_out[:, TOK:].astype(F32)
    wide[width:, TOK:VOCAB] = jnp.where(row_ids((128, 128)) == 0, mine[:1, :128], 0.0).astype(BF)
    lane_1 = lane_ids((1, 128))
    wanted = jnp.zeros((1, 128), jnp.int32)
    for r in range(rows):
        for s in range(segs):
            for u in range(own_u):
                wanted = jnp.where(lane_1 == (r * segs + s) * own_u + u, labels[s, u, r], wanted)
    wide[:, VOCAB:] = mm(wide[:, :TOK], (row_ids((TOK, 128)) == wanted).astype(BF)).astype(BF)
    back_w[...] = wide[:width, :VOCAB].astype(F32).T.astype(BF)
    hid[:, :, width:] = (lane_ids((rows, span, 128)) == 0).astype(BF)
    lane_t = lane_ids((frames, 128))
    lane_w = lane_ids((frames, TOK))
    group = rows * own_u
    per_vreg = 128 // group

    def row_of(k):
        return peers.owner(k // micro) * micro + k % micro

    def forward(k):
        r = row_of(k)
        ends = scalar_ends(lengths, r, segs)
        seg = seg_of(row_ids((frames, width)), ends)
        enc = enc_all[r].astype(F32)
        for u in range(own_u):
            at = slice(u * frames, (u + 1) * frames)
            per_frame = pick(
                seg, [proj[pl.ds(r * segs * own_u + s * own_u + u, 1), :] for s in range(segs)]
            )
            value = jnp.tanh(enc + per_frame)
            hid[r, at, :width] = value.astype(BF)
            slope[r, at, :] = (1.0 - value * value).astype(BF)
        logits = mm(hid[r], wide[...])
        seg_l = seg_of(row_ids((frames, 128)), ends)
        for u in range(own_u):
            at = slice(u * frames, (u + 1) * frames)
            logit, last, named = logits[at, :TOK], logits[at, TOK:VOCAB], logits[at, VOCAB:]
            top = jnp.maximum(jnp.max(logit, axis=1, keepdims=True), last[:, 0:1])
            top_dur = jnp.max(
                jnp.where((lane_t >= 1) & (lane_t <= 5), last, -jnp.inf), axis=1, keepdims=True
            )
            is_tok = lane_t == 0
            e_last = jnp.where(
                lane_t < 6, jnp.exp(jnp.where(lane_t < 6, last - jnp.where(is_tok, top, top_dur), 0.0)), 0.0
            )
            e = jnp.exp(logit - top)
            total = jnp.sum(e, axis=1, keepdims=True) + e_last[:, 0:1]
            total_dur = jnp.sum(jnp.where(is_tok, 0.0, e_last), axis=1, keepdims=True)
            prob[r, at, :TOK] = e.astype(BF)
            over = 1.0 / total
            prob_tail[r, at, :] = jnp.where(lane_t == 6, over, e_last * jnp.where(is_tok, over, 1.0 / total_dur))
            norm_tok, norm_dur = top + jnp.log(total), top_dur + jnp.log(total_dur)
            column = r * segs * own_u + seg_l * own_u + u
            at_label = jnp.sum(jnp.where(lane_t == column, named, 0.0), axis=1, keepdims=True) - norm_tok
            lp = last - jnp.where(is_tok, norm_tok, norm_dur)
            for half in range(2):
                cols = slice(half * 128, half * 128 + 128)
                value = mine[:, cols]
                for kind in range(half * per_vreg, min(KINDS, (half + 1) * per_vreg)):
                    column = at_label if kind == 6 else lp[:, kind : kind + 1]
                    value = jnp.where(lane_t == (kind % per_vreg) * group + r * own_u + u, column, value)
                mine[:, cols] = value

    mine[...] = jnp.zeros(mine.shape, F32)

    def forward_step(i, _):
        for j in range(1, labs):
            @pl.when(i * STEP == j * micro)
            def _():
                enc_copy(j, peers.owner(j)).wait_recv()
        for k in range(STEP):
            forward(i * STEP + k)
        return 0

    lax.fori_loop(0, rows // STEP, forward_step, 0)
    terms[peers.lab] = mine[...]

    def term_copy(j, source):
        return remote(mine, terms.at[source], send.at[1, j], recv.at[1, j], peers.device(j))

    for j in range(1, labs):
        term_copy(j, peers.lab).start()
    for j in range(1, labs):
        term_copy(j, peers.owner(j)).wait_recv()
    lattice(peers, lengths, counts, terms, skewed, hist, grads, loss, dims)

    def part_copy(j):
        return remote(part.at[j], came.at[j], send.at[2, j], recv.at[2, j], peers.device(j))

    def backward(k):
        r = row_of(k)
        ends = scalar_ends(lengths, r, segs)
        shift = (256 - peers.lab * group - r * own_u) % 128
        rolled = [pltpu.roll(grads[kind], shift, 1) for kind in range(KINDS)]
        seg_l = seg_of(row_ids((frames, TOK)), ends)
        for u in range(own_u):
            at = slice(u * frames, (u + 1) * frames)
            a, b = rolled[6][:, u : u + 1], rolled[0][:, u : u + 1]
            both = a + b
            label = pick(seg_l, [labels[s, u, r] for s in range(segs)])
            tails = prob_tail[r, at, :]
            scaled = both * tails[:, 6:7]
            prob[r, at, :TOK] = (jnp.where(lane_w == label, a, 0.0) - prob[r, at, :TOK].astype(F32) * scaled).astype(BF)
            aim = jnp.zeros((frames, 128), F32)
            for kind in range(6):
                aim = jnp.where(lane_t == kind, rolled[kind][:, u : u + 1], aim)
            prob[r, at, TOK:] = jnp.where(lane_t < 6, aim - tails * both, 0.0).astype(BF)
        back = mm(prob[r], back_w[...]) * slope[r].astype(F32)
        summed = back[:frames]
        for u in range(1, own_u):
            summed = summed + back[u * frames : (u + 1) * frames]
        part[k // micro, k % micro] = summed.astype(BF)
        shape = (segs * own_u, span)
        lanes = lane_ids(shape)
        seg_t = seg_of(lanes % frames, ends)
        hit = (row_ids(shape) == seg_t * own_u + lanes // frames).astype(BF)
        g_pred[pl.ds(r * segs * own_u, segs * own_u), :] = mm(hit, back.astype(BF)).astype(BF)

    def backward_step(i, _):
        first = rows - (i + 1) * STEP
        for k in range(STEP - 1, -1, -1):
            backward(first + k)
        for j in range(1, labs):
            @pl.when(first == j * micro)
            def _():
                part_copy(j).start()
        return 0

    lax.fori_loop(0, rows // STEP, backward_step, 0)
    gp = g_pred[...]
    g_predictor[...] = mm(gp, predx[:, :features])
    shards = lax.axis_size("dp")
    block = width // shards
    h_all = hid[...].reshape(rows * span, width + 128)
    g_bias[...] = jnp.zeros(g_bias.shape, F32)
    from_pred = t_mm(gp, pred[...])
    for i in range(2):
        piece = t_mm(h_all, prob[:, :, i * 512 : i * 512 + 512].reshape(rows * span, 512))
        for q in range(2):
            g_bias[2 * i + q : 2 * i + q + 1, :] = piece[width : width + 1, 256 * q : 256 * q + 256]
        for d in range(shards):
            first = d * 3 * block + (i + 1) * block
            g_pack[first : first + block, :] = piece[d * block : (d + 1) * block].astype(BF)
    ends_w = t_mm(h_all, prob[:, :, TOK:].reshape(rows * span, 128))
    g_bias[4:5, :128] = ends_w[width : width + 1]
    ends_w = ends_w[:width] + from_pred[:, 640:768]
    for d in range(shards):
        at = slice(d * block, (d + 1) * block)
        g_pack[d * 3 * block : d * 3 * block + block, :] = from_pred[at, :512].astype(BF)
        g_mix[at, :128] = from_pred[at, 512:640].astype(BF)
        g_mix[at, 128:] = ends_w[at].astype(BF)
    for j in range(1, labs):
        part_copy(j).wait_recv()
    total = part[0].astype(F32)
    for j in range(1, labs):
        total = total + came[j].astype(F32)
    g_enc[...] = total.astype(BF)
    for j in range(1, labs):
        enc_copy(j, peers.lab).wait_send()
        term_copy(j, peers.lab).wait_send()
        part_copy(j).wait_send()


VOCAB = TOK + 128
STEP = 2


def joint_call(enc_own, predictor, ints, predx, tok, tail, bias_out, dims):
    frames, rows, segs, own_u, labs = dims
    width = enc_own.shape[-1]
    span = own_u * frames
    micro = rows // labs
    vm = pl.BlockSpec(memory_space=pltpu.VMEM)
    sm = pl.BlockSpec(memory_space=pltpu.SMEM)
    return pl.pallas_call(
        functools.partial(joint_kernel, dims),
        out_shape=[
            jax.ShapeDtypeStruct((micro, frames, width), BF),
            jax.ShapeDtypeStruct((rows * segs * own_u, 640), F32),
            jax.ShapeDtypeStruct((3 * width, 512), BF),
            jax.ShapeDtypeStruct((width, 256), BF),
            jax.ShapeDtypeStruct((16, 256), F32),
            jax.ShapeDtypeStruct((8, 128), F32),
        ],
        in_specs=[vm, vm, sm, sm, sm, vm, vm, vm, vm],
        out_specs=[vm] * 6,
        scratch_shapes=[
            pltpu.VMEM((rows, frames, width), BF),
            pltpu.VMEM((rows * segs * own_u, 640), F32),
            pltpu.VMEM((rows * segs * own_u, 768), BF),
            pltpu.VMEM((rows * segs * own_u, width), F32),
            pltpu.VMEM((rows, span, width + 128), BF),
            pltpu.VMEM((rows, span, width), BF),
            pltpu.VMEM((width + 128, VOCAB + 128), BF),
            pltpu.VMEM((VOCAB, width), BF),
            pltpu.VMEM((rows, span, VOCAB), BF),
            pltpu.VMEM((rows, span, 128), F32),
            pltpu.VMEM((frames, 256), F32),
            pltpu.VMEM((labs, frames, 256), F32),
            pltpu.VMEM((16, frames + 24, 128), F32),
            pltpu.VMEM((2, frames + 16, 128), F32),
            pltpu.VMEM((KINDS, frames, 128), F32),
            pltpu.VMEM((rows * segs * own_u, width), BF),
            pltpu.VMEM((labs, micro, frames, width), BF),
            pltpu.VMEM((labs, micro, frames, width), BF),
            pltpu.SemaphoreType.DMA((3, labs)),
            pltpu.SemaphoreType.DMA((3, labs)),
        ],
        compiler_params=pltpu.CompilerParams(
            collective_id=2, has_side_effects=True, vmem_limit_bytes=60 * 2**20
        ),
    )(enc_own, predictor, *ints, predx, tok, tail, bias_out)


HEADS = 8
EPS = 1e-05
TAPS = 9
GAIN_ROW = 9
STATE = (
    ("n_ffn", 512, F32), ("n_att", 512, F32), ("n_conv", 512, F32), ("n_depth", 512, F32), ("n_out", 512, F32),
    ("scales", 128, F32), ("act", 2048, BF), ("slope", 2048, BF), ("qkv", 1536, BF), ("context", 512, BF),
    ("value", 512, F32), ("gate", 512, F32),
)


def sigmoid(v):
    return 0.5 * jnp.tanh(0.5 * v) + 0.5


def norm_parts(v):
    c = v - jnp.mean(v, axis=1, keepdims=True)
    r = lax.rsqrt(jnp.mean(c * c, axis=1, keepdims=True) + EPS)
    return c * r, r


def norm_back(gy, n, r, gain):
    gg = gy * gain
    gain_grad = jnp.sum(gy * n, axis=0, keepdims=True)
    inner = gg - jnp.mean(gg, axis=1, keepdims=True) - n * jnp.mean(gg * n, axis=1, keepdims=True)
    return r * inner, gain_grad


def rows_of(ref, n, first, count):
    per = ref.shape[0] // n
    return jnp.concatenate([ref[d * per + first : d * per + first + count, :] for d in range(n)], axis=0)


def put_rows(ref, n, first, count, value):
    per = ref.shape[0] // n
    for d in range(n):
        ref[d * per + first : d * per + first + count, :] = value[d * count : (d + 1) * count].astype(ref.dtype)


def own_ends(ints, micro, segs):
    first = lax.axis_index("lab") * micro
    return [scalar_ends(ints, first + m, segs) for m in range(micro)]


def seg_id(position, ends, frames):
    t, row = position % frames, position // frames
    out = seg_of(t, ends[0])
    for m in range(1, len(ends)):
        out = jnp.where(row == m, seg_of(t, ends[m]), out)
    return out + row * len(ends[0])


def shifted(value, step):
    rows = value.shape[0]
    return pltpu.roll(value, (-step) % rows, 0) if step % rows else value


def assemble_small(target, n, per, ds):
    lane = lane_ids((16, 128))
    columns = [jnp.zeros((16, 128), F32) for _ in range(n * ds // 128)]
    for d in range(n):
        piece = jnp.where(lane < ds, target[d * per : d * per + 16, 256:384].astype(F32), 0.0)
        at = d * ds % 128
        columns[d * ds // 128] = columns[d * ds // 128] + (pltpu.roll(piece, at, 1) if at else piece)
    return jnp.concatenate(columns, axis=1)


def split_small(value, d, ds):
    at = d * ds % 128
    piece = value[:, d * ds // 128 * 128 : d * ds // 128 * 128 + 128]
    piece = pltpu.roll(piece, 128 - at, 1) if at else piece
    return jnp.where(lane_ids((16, 128)) < ds, piece, 0.0)


class Sizes:
    def __init__(self, n, ds, ff, qk, pi, jr):
        self.n, self.ds, self.ff, self.qk, self.pi, self.jr = n, ds, ff, qk, pi, jr
        self.rows = (jr + ff, ff + qk, 2 * ds + pi + jr, 3 * jr)
        self.model = n * ds


def head_pair(ref, block, pair):
    at = block * 512 + pair * 128
    return ref[:, at : at + 128]


def forward_pieces(z, x_ref, ints, dims, full, small_ref, st, probs, encoded, enc_proj):
    frames, rows, segs, own_u, labs = dims
    n, micro = z.n, rows // labs
    count = micro * frames
    ends = own_ends(ints, micro, segs)
    ids_r = seg_id(row_ids((count, 128)), ends, frames)
    ids_c = seg_id(lane_ids((count, count)), ends, frames)
    scale_lane = lane_ids((count, 128))

    def norm(v, name, which):
        nv, r = norm_parts(v)
        st[name][...] = nv
        st["scales"][...] = jnp.where(scale_lane == which, r, st["scales"][...])
        return nv * small_ref[GAIN_ROW + which : GAIN_ROW + which + 1, :]

    small_ref[...] = assemble_small(full[0], n, z.rows[0], z.ds)
    st["scales"][...] = jnp.zeros((count, 128), F32)
    x = x_ref[...].reshape(count, z.model).astype(F32)
    ffn_in = norm(x, "n_ffn", 0).astype(BF)
    half = n // 2
    per = z.rows[0]
    for part in range(2):
        w = jnp.concatenate(
            [full[0][d * per + z.jr : d * per + z.jr + z.ff, :] for d in range(part * half, part * half + half)], axis=0
        )
        pre = mm_t(ffn_in, w)
        sg = sigmoid(pre)
        at = slice(part * half * z.ff, (part + 1) * half * z.ff)
        st["act"][:, at] = (pre * sg).astype(BF)
        st["slope"][:, at] = (sg * (1.0 + pre * (1.0 - sg))).astype(BF)
        yield
    after_ffn = x + 0.5 * mm(st["act"][...], rows_of(full[1], n, 0, z.ff))
    att_in = norm(after_ffn, "n_att", 1).astype(BF)
    st["qkv"][...] = mm_t(att_in, rows_of(full[1], n, z.ff, z.qk)).astype(BF)
    yield
    same = ids_r == ids_c
    low_half = lane_ids((count, 128)) < 64
    for pair in range(HEADS // 2):
        q, k, v = (head_pair(st["qkv"], b, pair) for b in range(3))
        total = None
        for side in range(2):
            keep = low_half if side == 0 else ~low_half
            score = mm_t(jnp.where(keep, q, 0), k) * (64 ** -0.5)
            score = jnp.where(same, score, LOW)
            e = jnp.exp(score - jnp.max(score, axis=1, keepdims=True))
            p = (e * (1.0 / jnp.sum(e, axis=1, keepdims=True))).astype(BF)
            probs[2 * pair + side] = p
            part = mm(p, jnp.where(keep, v, 0))
            total = part if total is None else total + part
        st["context"][:, pair * 128 : pair * 128 + 128] = total.astype(BF)
    yield
    after_att = after_ffn + mm(st["context"][...], rows_of(full[2], n, 0, z.ds))
    conv_in = norm(after_att, "n_conv", 2).astype(BF)
    conv_pre = mm_t(conv_in, rows_of(full[2], n, z.ds, z.pi))
    st["value"][...] = conv_pre[:, : z.model]
    st["gate"][...] = sigmoid(conv_pre[:, z.model :])
    depth = []
    for c in range(z.model // 128):
        at = slice(c * 128, c * 128 + 128)
        gated = st["value"][:, at] * st["gate"][:, at]
        total = jnp.zeros((count, 128), F32)
        for j in range(TAPS):
            ok = shifted(ids_r, j - TAPS // 2) == ids_r
            total = total + jnp.where(ok, shifted(gated, j - TAPS // 2), 0.0) * small_ref[j : j + 1, at]
        depth.append(total)
    dn = norm(jnp.concatenate(depth, axis=1), "n_depth", 3)
    conv_act = (dn * sigmoid(dn)).astype(BF)
    after_conv = after_att + mm(conv_act, rows_of(full[2], n, z.ds + z.pi, z.ds))
    out = norm(after_conv, "n_out", 4).astype(BF)
    encoded[...] = out.reshape(encoded.shape)
    enc_proj[...] = mm_t(out, rows_of(full[2], n, 2 * z.ds + z.pi, z.jr)).astype(BF).reshape(enc_proj.shape)
    yield


def backward_pieces(z, g_enc, ints, dims, full, small_ref, st, probs, grads, small_grad, grad_frames):
    frames, rows, segs, own_u, labs = dims
    n, micro = z.n, rows // labs
    count = micro * frames
    ends = own_ends(ints, micro, segs)
    ids_r = seg_id(row_ids((count, 128)), ends, frames)

    def gain(which):
        return small_ref[GAIN_ROW + which : GAIN_ROW + which + 1, :]

    def back(gy, name, which):
        g, gain_grad = norm_back(gy, st[name][...], st["scales"][:, which : which + 1], gain(which))
        small_grad[GAIN_ROW + which : GAIN_ROW + which + 1, :] = gain_grad
        return g

    def normed(name, which):
        return (st[name][...] * gain(which)).astype(BF)

    small_grad[...] = jnp.zeros(small_grad.shape, F32)
    ge = g_enc[...].reshape(count, -1)
    off = 2 * z.ds + z.pi
    put_rows(grads[2], n, off, z.jr, t_mm(ge, normed("n_out", 4)))
    g_conv_sum = back(mm(ge, rows_of(full[2], n, off, z.jr)), "n_out", 4)
    branch = g_conv_sum.astype(BF)
    dn = st["n_depth"][...] * gain(3)
    sg = sigmoid(dn)
    put_rows(grads[2], n, z.ds + z.pi, z.ds, t_mm((dn * sg).astype(BF), branch))
    g_act = mm_t(branch, rows_of(full[2], n, z.ds + z.pi, z.ds))
    g_depth = back(g_act * (sg * (1.0 + dn * (1.0 - sg))), "n_depth", 3)
    yield
    low_a, low_b = [], []
    for c in range(z.model // 128):
        at = slice(c * 128, c * 128 + 128)
        value, gate = st["value"][:, at], st["gate"][:, at]
        gated, gd = value * gate, g_depth[:, at]
        total = jnp.zeros((count, 128), F32)
        for j in range(TAPS):
            step = j - TAPS // 2
            ok = shifted(ids_r, step) == ids_r
            small_grad[j : j + 1, at] = jnp.sum(jnp.where(ok, shifted(gated, step), 0.0) * gd, axis=0, keepdims=True)
            ok = shifted(ids_r, -step) == ids_r
            total = total + jnp.where(ok, shifted(gd, -step), 0.0) * small_ref[j : j + 1, at]
        low_a.append((total * gate).astype(BF))
        low_b.append((total * value * gate * (1.0 - gate)).astype(BF))
    low = jnp.concatenate(low_a + low_b, axis=1)
    put_rows(grads[2], n, z.ds, z.pi, t_mm(low, normed("n_conv", 2)))
    g_att_sum = g_conv_sum + back(mm(low, rows_of(full[2], n, z.ds, z.pi)), "n_conv", 2)
    branch = g_att_sum.astype(BF)
    put_rows(grads[2], n, 0, z.ds, t_mm(st["context"][...], branch))
    g_context = mm_t(branch, rows_of(full[2], n, 0, z.ds)).astype(BF)
    yield
    low_half = lane_ids((count, 128)) < 64
    columns = [[], [], []]
    for pair in range(HEADS // 2):
        q, k, v = (head_pair(st["qkv"], b, pair) for b in range(3))
        gc = g_context[:, pair * 128 : pair * 128 + 128]
        sums = [None, None, None]
        for side in range(2):
            keep = low_half if side == 0 else ~low_half
            p = probs[2 * pair + side]
            gc_h = jnp.where(keep, gc, 0)
            gp = mm_t(gc_h, v)
            pf = p.astype(F32)
            gs = (pf * (gp - jnp.sum(gp * pf, axis=1, keepdims=True))).astype(BF)
            parts = (
                mm(gs, jnp.where(keep, k, 0)) * (64 ** -0.5),
                t_mm(gs, jnp.where(keep, q, 0)) * (64 ** -0.5),
                t_mm(p, gc_h),
            )
            sums = [b if a is None else a + b for a, b in zip(sums, parts)]
        for b in range(3):
            columns[b].append(sums[b].astype(BF))
    g_qkv = jnp.concatenate(columns[0] + columns[1] + columns[2], axis=1)
    yield
    put_rows(grads[1], n, z.ff, z.qk, t_mm(g_qkv, normed("n_att", 1)))
    g_ffn_sum = g_att_sum + back(mm(g_qkv, rows_of(full[1], n, z.ff, z.qk)), "n_att", 1)
    branch = (0.5 * g_ffn_sum).astype(BF)
    put_rows(grads[1], n, 0, z.ff, t_mm(st["act"][...], branch))
    yield
    g_pre = (mm_t(branch, rows_of(full[1], n, 0, z.ff)) * st["slope"][...].astype(F32)).astype(BF)
    put_rows(grads[0], n, z.jr, z.ff, t_mm(g_pre, normed("n_ffn", 0)))
    gx = g_ffn_sum + back(mm(g_pre, rows_of(full[0], n, z.jr, z.ff)), "n_ffn", 0)
    grad_frames[...] = gx.reshape(grad_frames.shape)
    yield


ORDER = (
    (-2, 0), (-2, 1), (-1, 0), (1, 0), (0, 0), (-2, 2), (-1, 1), (0, 0), (-2, 3), (1, 1), (0, 0), (-1, 2), (0, 0), (-1, 3),
    (1, 2), (0, 0), (1, 3),
)


def encode_kernel(
    z, dims, x_ref, ints, w_in, w_out, w_qkv, w_att, w_pin, w_pout, w_enc, w_pred, w_joint, bias_joint, w_depth,
    gain0, gain1, gain2, gain3, gain4,
    full0, full1, full2, predx, tok, tail_out, small_out, encoded, enc_proj, *rest,
):
    k = len(STATE)
    st = {name: ref for (name, _, _), ref in zip(STATE, rest[:k])}
    probs, rest = rest[k], rest[k + 1 :]
    sources, full = rest[0:4], rest[4:8]
    small_in, tail, ring_recv, x_recv, sems, out_sem = rest[8:]
    n = z.n
    w = Where(n)
    w.greet()
    jr, js, ds = z.jr, w_pred.shape[0], z.ds
    small_in[...] = jnp.zeros(small_in.shape, F32)
    small_in[:TAPS, :ds] = w_depth[...].astype(F32)
    for i, gain in enumerate((gain0, gain1, gain2, gain3, gain4)):
        small_in[GAIN_ROW + i : GAIN_ROW + i + 1, :ds] = gain[...].astype(F32)
    tail[...] = jnp.zeros(tail.shape, F32)
    tail[:1, :js] = bias_joint[...].astype(F32)
    column = tail[:8, :].T[:jr, :1]
    tail[:8, :] = jnp.zeros((8, 128), F32)
    tail[:js, : w_joint.shape[1] - 1024] = w_joint[:, 1024:].astype(F32)
    tail[...] = jnp.where(lane_ids((jr, 128)) == BIAS_LANE, column, tail[...])

    def down(value, count):
        return jnp.concatenate([value, jnp.zeros((count - value.shape[0],) + value.shape[1:], value.dtype)], 0) if count > value.shape[0] else value

    pred_t = down(w_pred[...], jr)
    sources[0][jr:, :] = w_in[...].astype(F32).T.astype(BF)
    sources[0][:jr, 0:128] = pred_t[:, 512:]
    sources[0][:jr, 128:256] = tail[...].astype(BF)
    sources[0][:jr, 256:] = jnp.zeros((jr, 256), BF)
    sources[0][:16, 256:384] = small_in[...].astype(BF)
    parts = [
        Gather(w, sources[i], full[i], z.rows[i], ring_recv.at[i], x_recv.at[i], sems.at[i]) for i in range(4)
    ]
    turns = n // 2 + 2
    skew = 2

    def fill(g):
        if g == 1:
            sources[1][: z.ff, :] = w_out[...]
            sources[1][z.ff :, :] = w_qkv[...]
        elif g == 2:
            sources[2][:ds, :] = w_att[...]
            sources[2][ds : ds + z.pi, :] = w_pin[...].astype(F32).T.astype(BF)
            sources[2][ds + z.pi : 2 * ds + z.pi, :] = w_pout[...]
            sources[2][2 * ds + z.pi :, :] = down(w_enc[...], jr)
        elif g == 3:
            sources[3][:jr, :] = pred_t[:, :512]
            sources[3][jr : 2 * jr, :] = down(w_joint[:, :512], jr)
            sources[3][2 * jr :, :] = down(w_joint[:, 512:1024], jr)

    outs = (full0, full1, full2)
    compute = forward_pieces(z, x_ref, ints, dims, full, small_out, st, probs, encoded, enc_proj)

    def finish(g):
        parts[g].whole()
        if g < 3:
            pltpu.make_async_copy(full[g], outs[g], out_sem.at[g]).start()

    for s in range(turns - 2):
        for g in range(4):
            if s == 0:
                fill(g)
            parts[g].step(s)
    for what, g in ORDER:
        if what == 0:
            next(compute)
        elif what == 1:
            finish(g)
        else:
            parts[g].step(turns + what)

    predx[:, :512] = rows_of(full[3], n, 0, jr)
    tok[:, :512] = rows_of(full[3], n, jr, jr)
    tok[:, 512:] = rows_of(full[3], n, 2 * jr, jr)
    mixes = rows_of(full[0], n, 0, jr)
    predx[:, 512:] = mixes[:, :256]
    tail_out[...] = mixes[:, 128:256]
    for part in parts:
        part.drain()
    for g in range(3):
        pltpu.make_async_copy(full[g], outs[g], out_sem.at[g]).wait()


def encode_call(z, dims, x, lengths, *params):
    frames, rows, segs, own_u, labs = dims
    n, micro = z.n, rows // labs
    count, width = micro * frames, n * z.jr
    vm, sm, hbm = (pl.BlockSpec(memory_space=m) for m in (pltpu.VMEM, pltpu.SMEM, pl.ANY))
    shape = jax.ShapeDtypeStruct
    outs = [shape((n * z.rows[i], 512), BF) for i in range(3)]
    outs += [shape((width, 768), BF), shape((width, 1024), BF), shape((width, 128), BF), shape((16, z.model), F32)]
    outs += [shape((micro, frames, z.model), BF), shape((micro, frames, width), BF)]
    outs += [shape((count, lanes), dtype) for _, lanes, dtype in STATE]
    outs += [shape((HEADS, count, count), BF)]
    return pl.pallas_call(
        functools.partial(encode_kernel, z, dims),
        out_shape=outs,
        in_specs=[vm, sm] + [vm] * len(params),
        out_specs=[hbm] * 3 + [vm] * (len(outs) - 3),
        scratch_shapes=[pltpu.VMEM((r, 512), BF) for r in z.rows]
        + [pltpu.VMEM((n * r, 512), BF) for r in z.rows]
        + [
            pltpu.VMEM((16, 128), F32),
            pltpu.VMEM((z.jr, 128), F32),
            pltpu.SemaphoreType.DMA((4, n - 1)),
            pltpu.SemaphoreType.DMA((4, n - 1)),
            pltpu.SemaphoreType.DMA((4, 5)),
            pltpu.SemaphoreType.DMA((3,)),
        ],
        compiler_params=pltpu.CompilerParams(collective_id=0, has_side_effects=True, vmem_limit_bytes=60 * 2**20),
    )(x, lengths, *params)


def grad_kernel(z, dims, skew, *refs):
    g_enc, ints, small_ref, g_pack, g_mix, g_bias = refs[:6]
    hbm = refs[6:9]
    refs = refs[9:]
    k = len(STATE)
    st = {name: ref for (name, _, _), ref in zip(STATE, refs[:k])}
    probs, refs = refs[k], refs[k + 1 :]
    outs, grad_frames, refs = refs[:4], refs[4], refs[5:]
    full, refs = refs[:3], refs[3:]
    grads, refs = list(refs[:3]) + [g_pack], refs[3:]
    small_grad, bufs, (send, recv, in_sem) = refs[0], refs[1:21], refs[21:]
    n = z.n
    w = Where(n)
    w.far_back = (ring_device(w.place + 2 * w.core - 1, n), w.lab)
    for g in (2, 1, 0):
        pltpu.make_async_copy(hbm[g], full[g], in_sem.at[g]).start()
    w.greet()
    order = (3, 2, 1, 0)
    parts = [
        Scatter(w, grads[g], outs[g], z.rows[g], bufs[5 * g : 5 * g + 5], send.at[g], recv.at[g], SHARES[3 - g])
        for g in order
    ]
    compute = backward_pieces(z, g_enc, ints, dims, full, small_ref, st, probs, grads, small_grad, grad_frames)

    def load(g):
        pltpu.make_async_copy(hbm[g], full[g], in_sem.at[g]).wait()

    def work(i):
        if i == 1:
            load(2)
            next(compute)
            next(compute)
        elif i == 2:
            load(1)
            next(compute)
            next(compute)
        elif i == 3:
            load(0)
            next(compute)
            per, ds = z.rows[0], z.ds
            for d in range(n):
                at = d * per
                grads[0][at : at + z.jr, :256] = g_mix[d * z.jr : (d + 1) * z.jr, :]
                if z.jr > 32:
                    grads[0][at + 32 : at + z.jr, 256:] = jnp.zeros((z.jr - 32, 256), BF)
                grads[0][at : at + 16, 256:384] = split_small(small_grad[...], d, ds).astype(BF)
                grads[0][at : at + 16, 384:] = jnp.zeros((16, 128), BF)
                grads[0][at + 16 : at + 32, 256:] = g_bias[...].astype(BF)

    sum_up(parts, work, ORDER_SUMS)


SHARES = (0.2, 0.2, 0.3, 0.25)
ORDER_SUMS = (
    (0, 0, 0), (0, 1, 0), (0, 2, 0), (1, 0, 0), (3, 0, 0), (2, 0, 1), (0, 3, 0), (1, 1, 0), (2, 1, 1), (2, 0, 2),
    (3, 1, 0), (1, 2, 0), (2, 2, 1), (2, 1, 2), (1, 3, 0), (3, 2, 0), (3, 0, 1), (2, 0, 3), (2, 2, 2), (3, 3, 0),
    (2, 3, 1), (2, 1, 3), (3, 0, 2), (3, 1, 1), (2, 0, 4), (2, 2, 3), (2, 3, 2), (2, 1, 4), (3, 0, 3), (3, 1, 2),
    (2, 0, 5), (2, 2, 4), (3, 2, 1), (2, 3, 3), (2, 1, 5), (3, 0, 4), (3, 1, 3), (3, 3, 1), (2, 2, 5), (3, 2, 2),
    (2, 0, 6), (2, 3, 4), (3, 0, 5), (2, 1, 6), (3, 3, 2), (2, 0, 7), (3, 1, 4), (3, 2, 3), (2, 2, 6), (3, 0, 6),
    (2, 1, 7), (2, 3, 5), (3, 3, 3), (2, 2, 7), (3, 0, 7), (3, 1, 5), (3, 2, 4), (3, 3, 4), (2, 3, 6), (3, 1, 6),
    (3, 2, 5), (3, 1, 7), (2, 3, 7), (3, 3, 5), (3, 2, 6), (3, 3, 6), (3, 2, 7), (3, 3, 7),
)


def grad_call(z, dims, g_enc, ints, small, g_pack, g_mix, g_bias, full, state, probs, skew=1):
    frames, rows, segs, own_u, labs = dims
    n, micro = z.n, rows // labs
    vm, sm, hbm = (pl.BlockSpec(memory_space=m) for m in (pltpu.VMEM, pltpu.SMEM, pl.ANY))
    shape = jax.ShapeDtypeStruct
    scratch = [pltpu.VMEM((n * z.rows[g], 512), BF) for g in range(3)] * 2 + [pltpu.VMEM((16, z.model), F32)]
    for g, r in enumerate(z.rows):
        scratch += scatter_scratch(n, r, 512, SHARES[3 - g])
    return pl.pallas_call(
        functools.partial(grad_kernel, z, dims, skew),
        out_shape=[shape((r, 512), BF) for r in z.rows] + [shape((micro, frames, z.model), F32)],
        in_specs=[vm, sm, vm, vm, vm, vm] + [hbm] * 3 + [vm] * (len(STATE) + 1),
        out_specs=[vm] * 5,
        scratch_shapes=scratch + scatter_sems(n, 4) + [pltpu.SemaphoreType.DMA((3,))],
        compiler_params=pltpu.CompilerParams(collective_id=1, has_side_effects=True, vmem_limit_bytes=60 * 2**20),
    )(g_enc, ints, small, g_pack, g_mix, g_bias, *full, *state, probs)


def unpack_kernel(z, dims, js, own0, own1, own2, own3, grads, encoded, loss, g_predictor, *outs):
    frames, rows, segs, own_u, labs = dims
    ds, ff, pi, jr = z.ds, z.ff, z.pi, z.jr
    (
        loss_o, enc_o, grads_o, pred_o, gg0, g_in, g_out, gg1, g_qkv, g_att, gg2, g_pin, g_depth, gg3, g_pout, gg4,
        g_enc, g_pred, g_bias, g_joint, g_bias_out,
    ) = outs
    hit = (row_ids((128, rows)) == lane_ids((128, rows)) * own_u).astype(F32)
    loss_o[...] = lax.dot_general(
        loss[...], hit, (((1,), (0,)), ((), ())), precision=lax.Precision.HIGHEST, preferred_element_type=F32
    )[:segs]
    enc_o[...] = encoded[...]
    grads_o[...] = grads[...]
    for r in range(rows):
        for s in range(segs):
            first = (r * segs + s) * own_u
            pred_o[r, s] = g_predictor[first : first + own_u, :]
    small = own0[:32, 256:].astype(F32)
    for i, out in enumerate((gg0, gg1, gg2, gg3, gg4)):
        out[...] = small[GAIN_ROW + i : GAIN_ROW + i + 1, :ds]
    g_depth[...] = small[:TAPS, :ds]
    for i in range(4):
        g_bias_out[:, 256 * i : 256 * i + 256] = small[16 + i : 17 + i, :]
    g_bias_out[:, 1024:] = small[20:21, : g_bias_out.shape[1] - 1024]
    g_in[...] = own0[jr:, :].astype(F32).T
    g_out[...] = own1[:ff, :].astype(F32)
    g_qkv[...] = own1[ff:, :].astype(F32)
    g_att[...] = own2[:ds, :].astype(F32)
    g_pin[...] = own2[ds : ds + pi, :].astype(F32).T
    g_pout[...] = own2[ds + pi : 2 * ds + pi, :].astype(F32)
    g_enc[...] = own2[2 * ds + pi :, :].astype(F32)[:js]
    g_pred[:, :512] = own3[:jr, :].astype(F32)[:js]
    g_pred[:, 512:] = own0[:jr, :128].astype(F32)[:js]
    tail = own0[:jr, 128:256].astype(F32)
    wide = jnp.concatenate([tail, jnp.zeros((128 - jr, 128), F32)], axis=0) if jr < 128 else tail
    g_bias[...] = wide.T[BIAS_LANE : BIAS_LANE + 1, :js]
    g_joint[:, :512] = own3[jr : 2 * jr, :].astype(F32)[:js]
    g_joint[:, 512:1024] = own3[2 * jr :, :].astype(F32)[:js]
    g_joint[:, 1024:] = tail[:js, : g_joint.shape[1] - 1024]


def unpack_call(z, dims, js, out_width, own, grads, encoded, loss, g_predictor):
    frames, rows, segs, own_u, labs = dims
    shape = jax.ShapeDtypeStruct
    row = shape((1, z.ds), F32)
    line, features = z.model, g_predictor.shape[1]
    outs = [
        shape((segs, rows), F32), shape(encoded.shape, BF), shape(grads.shape, F32),
        shape((rows, segs, own_u, features), F32), row, shape((line, z.ff), F32), shape((z.ff, line), F32), row,
        shape((z.qk, line), F32), shape((z.ds, line), F32), row, shape((line, z.pi), F32), shape((TAPS, z.ds), F32),
        row, shape((z.ds, line), F32), row, shape((js, line), F32), shape((js, features), F32), shape((1, js), F32),
        shape((js, out_width), F32), shape((1, out_width), F32),
    ]
    vm = pl.BlockSpec(memory_space=pltpu.VMEM)
    return pl.pallas_call(
        functools.partial(unpack_kernel, z, dims, js),
        out_shape=outs,
        in_specs=[vm] * 8,
        out_specs=[vm] * len(outs),
        compiler_params=pltpu.CompilerParams(vmem_limit_bytes=60 * 2**20),
    )(*own, grads, encoded, loss, g_predictor)

def local(
    frames_in, predictor, seg_lengths, label_counts, label_ids, gain_ffn, w_ffn_in, w_ffn_out, gain_att, w_qkv,
    w_att_out, gain_conv, w_point_in, w_depth, gain_depth, w_point_out, gain_out, w_enc, w_pred, bias_joint,
    w_joint_out, bias_out,
):
    n, labs = lax.axis_size("dp"), lax.axis_size("lab")
    micro, frames, model = frames_in.shape
    rows, segs, own_u, joint = predictor.shape
    ds, js = model // n, w_pred.shape[1]
    jr = max(-(-js // TILE), 2) * TILE
    z = Sizes(n, ds, w_ffn_in.shape[1], w_qkv.shape[1], w_point_in.shape[1], jr)
    dims = (frames, rows, segs, own_u, labs)
    lengths, counts, labels = seg_lengths.T, label_counts.T, label_ids.transpose(1, 2, 0)
    gains = [g[None] for g in (gain_ffn, gain_att, gain_conv, gain_depth, gain_out)]
    out = encode_call(
        z, dims, frames_in, lengths, w_ffn_in, w_ffn_out, w_qkv.T, w_att_out, w_point_in, w_point_out, w_enc.T, w_pred.T,
        w_joint_out, bias_joint[None], w_depth, *gains,
    )
    full, (predx, tok, tail_w, small_w, encoded, enc_proj) = out[:3], out[3:9]
    state, probs = out[9:-1], out[-1]
    g_enc, g_predictor, g_pack, g_mix, g_bias, loss = joint_call(
        enc_proj, predictor, (lengths, counts, labels), predx, tok, tail_w, bias_out[None], dims
    )
    *own, grad_frames = grad_call(z, dims, g_enc, lengths, small_w, g_pack, g_mix, g_bias, full, state, probs)
    (
        loss, encoded, grad_frames, g_predictor, gg0, g_in, g_out, gg1, g_qkv, g_att, gg2, g_pin, g_depth, gg3, g_pout,
        gg4, g_enc, g_pred, g_bias, g_joint, g_bias_out,
    ) = unpack_call(z, dims, js, bias_out.shape[0], own, grad_frames, encoded, loss, g_predictor)
    return (
        loss.T, encoded, grad_frames, g_predictor, gg0[0], g_in, g_out, gg1[0], g_qkv.T, g_att, gg2[0], g_pin, g_depth,
        gg3[0], g_pout, gg4[0], g_enc.T, g_pred.T, g_bias[0], g_joint, g_bias_out[0],
    )


def solution(mesh):
    rows, whole = P(("dp", "lab"), None, None), P()
    predictor, columns, lines, vector = P("dp", None, "lab", None), P(None, "dp"), P("dp", None), P("dp")
    params = (
        vector, columns, lines, vector, columns, lines, vector, columns, columns, vector, lines, vector, columns,
        columns, vector, lines, whole,
    )
    return jax.shard_map(
        local,
        mesh=mesh,
        in_specs=(rows, predictor, lines, lines, P("dp", None, "lab")) + params,
        out_specs=(lines, rows, rows, predictor) + params,
        check_vma=False,
    )
```

```python
import functools

import jax
import jax.numpy as jnp
from jax import lax
from jax.experimental import pallas as pl
from jax.experimental.pallas import tpu as pltpu
from jax.sharding import PartitionSpec as P


MESH = pl.DeviceIdType.MESH
F32 = jnp.float32
BF = jnp.bfloat16
TILE = 16


def ring_place(dp, n):
    odd = dp % 2
    return (1 - odd) * (dp // 2) + odd * (n - 1 - dp // 2)


def ring_device(place, n):
    place = (place + 2 * n) % n
    high = place // (n // 2)
    return (1 - high) * (2 * place) + high * (2 * (n - 1 - place) + 1)


def x_rows(rows, share):
    tiles = rows // TILE
    return min(tiles // 2, int(tiles * share + 0.5)) * TILE


class Where:
    def __init__(self, n):
        self.n = n
        self.dp = lax.axis_index("dp")
        self.lab = lax.axis_index("lab")
        self.core = self.lab % 2
        self.side = self.lab // 2
        self.place = ring_place(self.dp, n)
        self.right = (ring_device(self.place + 1, n), self.lab)
        self.left = (ring_device(self.place - 1, n), self.lab)
        self.twin = (self.dp, self.side * 2 + 1 - self.core)
        self.across = (self.dp, (1 - self.side) * 2 + self.core)
        self.far = (ring_device(self.place + 1 - 2 * self.core, n), self.lab)
        self.far_back = (ring_device(self.place + 2 * self.core - 1, n), self.lab)
        self.corner = (self.dp, (1 - self.side) * 2 + 1 - self.core)

    def at(self, distance):
        return ring_device(self.place + distance, self.n)

    def greet(self):
        barrier = pltpu.get_barrier_semaphore()
        others = (self.right, self.left, self.twin, self.across, self.corner)
        for other in others:
            pl.semaphore_signal(barrier, inc=1, device_id=other, device_id_type=MESH)
        pl.semaphore_wait(barrier, len(others))


def remote(src, dst, send_sem, recv_sem, device):
    return pltpu.make_async_remote_copy(
        src_ref=src,
        dst_ref=dst,
        send_sem=send_sem,
        recv_sem=recv_sem,
        device_id=device,
        device_id_type=MESH,
    )


class Gather:
    def __init__(self, where, source, target, rows, ring_recv, x_recv, sems):
        self.w, self.source, self.target, self.rows = where, source, target, rows
        self.width = target.shape[1]
        self.half = self.width // 2
        self.cut = x_rows(rows, 0.3)
        self.ring_recv, self.x_recv, self.sems = ring_recv, x_recv, sems
        self.steps = where.n // 2

    def lanes(self):
        return pl.ds(pl.multiple_of(self.w.core * self.half, 128), self.half)

    def rows_at(self, shard, offset, size):
        base = shard * self.rows if shard is not None else 0
        return pl.ds(pl.multiple_of(base + offset, TILE), size)

    def ring_part(self, ref, shard):
        return ref.at[self.rows_at(shard, self.w.side * self.cut, self.rows - self.cut), self.lanes()]

    def x_part(self, ref, shard, side):
        return ref.at[self.rows_at(shard, side * (self.rows - self.cut), self.cut), self.lanes()]

    def slot(self, distance):
        return distance + self.steps - 1 if distance < 0 else distance + self.steps - 2

    def hop(self, distance, first):
        w = self.w
        if distance == self.steps:
            shard = w.at((2 * w.core - 1) * (self.steps - 1))
            device = w.far
        else:
            shard = w.at(distance + 1) if distance < 0 else w.at(distance - 1)
            device = w.right if distance < 0 else w.left
        src = self.ring_part(self.source, None) if first else self.ring_part(self.target, shard)
        slot = 2 * self.steps - 2 if distance == self.steps else self.slot(distance)
        remote(src, self.ring_part(self.target, shard), self.sems.at[1], self.ring_recv.at[slot], device).start()

    def own(self):
        pltpu.make_async_copy(
            self.source, self.target.at[self.rows_at(self.w.dp, 0, self.rows), :], self.sems.at[4]
        ).start()

    def arrived(self, distance):
        w = self.w
        shard = w.at(distance)
        slot = 2 * self.steps - 2 if distance == self.steps else self.slot(distance)
        part = self.ring_part(self.target, shard)
        remote(part, part, self.sems.at[1], self.ring_recv.at[slot], w.right).wait_recv()

    def spread(self, distance):
        w = self.w
        shard = w.at(distance)
        slot = 2 * self.steps - 2 if distance == self.steps else self.slot(distance)
        if self.cut:
            part = self.x_part(self.target, shard, w.side)
            remote(part, part, self.sems.at[2], self.x_recv.at[slot], w.across).start()
        part = self.ring_part(self.target, shard)
        remote(part, part, self.sems.at[3], self.sems.at[0], w.twin).start()

    def crossed(self, distance):
        if not self.cut:
            return
        w = self.w
        shard = w.at(distance)
        slot = 2 * self.steps - 2 if distance == self.steps else self.slot(distance)
        part = self.x_part(self.target, shard, 1 - w.side)
        remote(part, part, self.sems.at[2], self.x_recv.at[slot], w.across).wait_recv()
        remote(part, part, self.sems.at[3], self.sems.at[0], w.twin).start()

    def whole(self):
        part = self.target.at[pl.ds(0, (self.w.n - 1) * self.rows), pl.ds(0, self.half)]
        remote(part, part, self.sems.at[3], self.sems.at[0], self.w.twin).wait_recv()
        pltpu.make_async_copy(
            self.source, self.target.at[self.rows_at(self.w.dp, 0, self.rows), :], self.sems.at[4]
        ).wait()

    def drain(self):
        count = self.w.n - 1
        for sem, rows in ((1, self.rows - self.cut), (2, self.cut), (3, self.rows)):
            if rows:
                part = self.target.at[pl.ds(0, count * rows), pl.ds(0, self.half)]
                remote(part, part, self.sems.at[sem], self.sems.at[sem], self.w.twin).wait_send()

    def step(self, s):
        if s == 0:
            self.own()
        if 1 <= s < self.steps:
            self.arrived(-s)
            self.arrived(s)
        if s == self.steps:
            self.arrived(self.steps)
        if s < self.steps - 1:
            self.hop(-s - 1, s == 0)
            self.hop(s + 1, s == 0)
        elif s == self.steps - 1:
            self.hop(self.steps, False)
        if 1 <= s < self.steps:
            self.spread(-s)
            self.spread(s)
        if s == self.steps:
            self.spread(self.steps)
        if 2 <= s <= self.steps:
            self.crossed(-s + 1)
            self.crossed(s - 1)
        if s == self.steps + 1:
            self.crossed(self.steps)


class Pair:
    def __init__(self, where, grads, held, rows, send, recv):
        self.w, self.grads, self.held, self.rows = where, grads, held, rows
        self.half = grads.shape[1] // 2
        self.copy = remote(self.grads.at[:, self.lanes(1 - where.core)], held, send.at[0], recv.at[0], where.twin)

    def lanes(self, core):
        return pl.ds(pl.multiple_of(core * self.half, 128), self.half)

    def give(self):
        self.copy.start()

    def add(self):
        self.copy.wait_recv()

        def body(i, _):
            at = pl.ds(pl.multiple_of(i * self.rows, TILE), self.rows)
            self.held[at, :] = (
                self.held[at, :].astype(F32) + self.grads[at, self.lanes(self.w.core)].astype(F32)
            ).astype(BF)
            return 0

        lax.fori_loop(0, self.w.n, body, 0)

    def drain(self):
        self.copy.wait_send()


class Chain:
    def __init__(self, pair, out, crossed, bufs, send, recv, share):
        self.pair, self.w, self.out, self.crossed = pair, pair.w, out, crossed
        self.cut = x_rows(pair.rows, share)
        self.size = self.cut if crossed else pair.rows - 2 * self.cut
        self.depth = self.w.n // 2 - 1
        self.xbuf, self.rbuf = bufs
        self.send, self.recv = send, recv
        self.stages = self.depth + 5

    def first(self, side):
        return side * (self.pair.rows - self.cut) if self.crossed else self.cut

    def rows_at(self, shard, side=None):
        base = shard * self.pair.rows + self.first(self.w.side if side is None else side)
        return pl.ds(pl.multiple_of(base, TILE), self.size)

    def out_at(self, side=None):
        at = pl.ds(pl.multiple_of(self.first(self.w.side if side is None else side), TILE), self.size)
        return self.out.at[at, self.pair.lanes(self.w.core)]

    def got(self, sem, dst):
        remote(dst, dst, self.send.at[0], self.recv.at[sem], self.w.twin).wait_recv()

    def ring(self, slot, src, device):
        remote(src, self.rbuf.at[slot], self.send.at[1], self.recv.at[slot], device).start()

    def stage(self, s):
        if not self.size:
            return
        w, n, depth, held = self.w, self.w.n, self.depth, self.pair.held
        last = 2 * depth + 1
        if s == 0:
            if self.crossed:
                for i in range(n):
                    remote(
                        held.at[self.rows_at(i, 1 - w.side), :], self.xbuf.at[i], self.send.at[0], self.recv.at[last],
                        w.across,
                    ).start()
        elif s == 1:
            if self.crossed:
                self.got(last, self.xbuf)

                def body(i, _):
                    at = self.rows_at(i)
                    held[at, :] = (held[at, :].astype(F32) + self.xbuf[i].astype(F32)).astype(BF)
                    return 0

                lax.fori_loop(0, n, body, 0)
            dest = w.at((2 * w.core - 1) * (depth + 1))
            self.ring(2 * depth, held.at[self.rows_at(dest), :], w.far_back)
        elif s < 2 + depth:
            hop = s - 2
            for way in (0, 1):
                sign = 1 - 2 * way
                own = held[self.rows_at(w.at(sign * (depth - hop))), :].astype(F32)
                slot = 2 * hop + way
                if hop == 0:
                    if way == 0:
                        self.got(2 * depth, self.rbuf.at[2 * depth])
                    far = self.rbuf[2 * depth].astype(F32)
                    pick = w.core if way == 0 else 1 - w.core
                    own = own + jnp.where(pick == 1, far, 0.0)
                    at = 2 * depth + 1 + way
                else:
                    at = slot - 2
                    self.got(at, self.rbuf.at[at])
                    own = own + self.rbuf[at].astype(F32)
                self.rbuf[at] = own.astype(BF)
                self.ring(slot, self.rbuf.at[at], w.right if way == 0 else w.left)
        elif s == 2 + depth:
            total = held[self.rows_at(w.dp), :].astype(F32)
            for way in (0, 1):
                at = 2 * depth - 2 + way
                self.got(at, self.rbuf.at[at])
                total = total + self.rbuf[at].astype(F32)
            if self.crossed:
                mine = self.out_at()
                mine[...] = total.astype(BF)
                remote(mine, mine, self.send.at[2], self.recv.at[last + 1], w.across).start()
                remote(mine, mine, self.send.at[3], self.recv.at[last + 2], w.twin).start()
            else:
                self.xbuf[0] = total.astype(BF)
                remote(self.xbuf.at[0], self.xbuf.at[1], self.send.at[2], self.recv.at[last + 1], w.across).start()
        elif s == 3 + depth:
            if self.crossed:
                other = self.out_at(1 - w.side)
                self.got(last + 1, other)
                remote(other, other, self.send.at[4], self.recv.at[last + 3], w.twin).start()
            else:
                self.got(last + 1, self.xbuf.at[1])
                mine = self.out_at()
                mine[...] = (self.xbuf[0].astype(F32) + self.xbuf[1].astype(F32)).astype(BF)
                remote(mine, mine, self.send.at[3], self.recv.at[last + 2], w.twin).start()
        elif s == 4 + depth:
            part = self.out_at()
            self.got(last + 2, part)
            if self.crossed:
                self.got(last + 3, part)

    def drain(self):
        if not self.size:
            return
        ring = self.rbuf.at[pl.ds(0, 2 * self.depth + 1)]
        remote(ring, ring, self.send.at[1], self.recv.at[0], self.w.twin).wait_send()
        part = self.out_at()
        remote(part, part, self.send.at[2], self.recv.at[0], self.w.twin).wait_send()
        remote(part, part, self.send.at[3], self.recv.at[0], self.w.twin).wait_send()
        if self.crossed:
            remote(part, part, self.send.at[4], self.recv.at[0], self.w.twin).wait_send()
            remote(self.xbuf, self.xbuf, self.send.at[0], self.recv.at[0], self.w.twin).wait_send()


def scatter_scratch(n, rows, width, share):
    half, cut, depth = width // 2, x_rows(rows, share), n // 2 - 1
    out = [pltpu.VMEM((n * rows, half), BF)]
    for count, size in ((2, rows - 2 * cut), (n, cut)):
        out += [pltpu.VMEM((count, max(size, TILE), half), BF), pltpu.VMEM((2 * depth + 3, max(size, TILE), half), BF)]
    return out


def scatter_sems(n, k):
    return [pltpu.SemaphoreType.DMA((k, 11)), pltpu.SemaphoreType.DMA((k, 2 * n + 8))]


class Scatter:
    def __init__(self, where, grads, out, rows, bufs, send, recv, share):
        n = where.n
        self.pair = Pair(where, grads, bufs[0], rows, send.at[pl.ds(10, 1)], recv.at[pl.ds(2 * n + 7, 1)])
        self.straight = Chain(self.pair, out, False, bufs[1:3], send.at[pl.ds(0, 5)], recv.at[pl.ds(0, n + 2)], share)
        self.crossed = Chain(self.pair, out, True, bufs[3:5], send.at[pl.ds(5, 5)], recv.at[pl.ds(n + 2, n + 3)], share)

    def drain(self):
        for part in (self.pair, self.straight, self.crossed):
            part.drain()


def sum_up(parts, work, order):
    depth = parts[0].straight.depth
    for what, g, stage in order:
        part = parts[g]
        if what == 0:
            work(g)
            part.pair.give()
        elif what == 1:
            part.pair.add()
        else:
            chain = part.straight if what == 2 else part.crossed
            stages = [stage] if stage < 4 else range(4, depth + 2) if stage == 4 else [stage + depth - 3]
            for s in stages:
                chain.stage(s)
    for part in parts:
        part.drain()


LOW = -100000.0
TOK = 1024
KINDS = 7
BIAS_LANE = 6


def mm(a, b):
    return lax.dot_general(a, b, (((1,), (0,)), ((), ())), preferred_element_type=F32)


def mm_t(a, b):
    return lax.dot_general(a, b, (((1,), (1,)), ((), ())), preferred_element_type=F32)


def t_mm(a, b):
    return lax.dot_general(a, b, (((0,), (0,)), ((), ())), preferred_element_type=F32)


def lane_ids(shape):
    return lax.broadcasted_iota(jnp.int32, shape, len(shape) - 1)


def row_ids(shape):
    return lax.broadcasted_iota(jnp.int32, shape, 0)


def seg_of(t, ends):
    return sum((t >= e).astype(jnp.int32) for e in ends[:-1])


def pick(seg, values):
    out = values[0]
    for s in range(1, len(values)):
        out = jnp.where(seg == s, values[s], out)
    return out


def scalar_ends(lengths, r, segs):
    ends, total = [], 0
    for s in range(segs):
        total = total + lengths[s, r]
        ends.append(total)
    return ends


def lse_of(terms):
    top = functools.reduce(jnp.maximum, terms)
    return top, functools.reduce(jnp.add, [jnp.exp(v - top) for v in terms])


def lattice(lengths, counts, terms, skewed, hist, grads, loss, dims):
    frames, rows, segs, own_u, labs = dims
    wide = (frames, 128)
    lane = lane_ids(wide)
    group = rows * own_u
    j, row, u = lane % own_u, (lane % group) // own_u, (lane // group) * own_u + lane % own_u
    t = row_ids(wide)
    all_ends = [scalar_ends(lengths, r, segs) for r in range(rows)]

    def per_lane(values):
        out = jnp.zeros(wide, jnp.int32)
        for r in range(rows):
            out = jnp.where(row == r, values[r], out)
        return out

    ends = [per_lane([all_ends[r][s] for r in range(rows)]) for s in range(segs)]
    labels_in = [per_lane([counts[s, r] for r in range(rows)]) for s in range(segs)]
    seg = seg_of(t, ends)
    stop = pick(seg, ends)
    begin = pick(seg, [jnp.zeros(wide, jnp.int32)] + ends[:-1])
    target = pick(seg, labels_in)
    remain, first = stop - t, t == begin

    kinds = []
    per_vreg = 128 // group
    for k in range(KINDS):
        value = None
        for dev in range(labs):
            part = terms[dev, :, (k // per_vreg) * 128 : (k // per_vreg) * 128 + 128]
            shift = (dev - k % per_vreg) * group % 128
            part = pltpu.roll(part, shift, 1) if shift else part
            value = part if value is None else jnp.where(lane // group == dev, part, value)
        kinds.append(value)
    blank_lp, durs, label_lp = kinds[0], kinds[1:6], kinds[6]
    last_u = own_u * labs - 1
    emit, blank, blank_raw = [], [None], [None]
    for d in range(5):
        ok = (u < last_u) & (d <= remain - 1)
        emit.append(jnp.where(ok, label_lp + durs[d], LOW))
        if d:
            blank_raw.append(blank_lp + durs[d])
            blank.append(jnp.where(d <= remain - 1, blank_raw[d], LOW))
    final = (u == target) & (remain <= 4)
    closing = jnp.zeros(wide, F32)
    for d in range(1, 5):
        closing = jnp.where(remain == d, blank_raw[d], closing)
    closing = jnp.where(final, closing, LOW)
    start = jnp.where(first & (u == 0), 0.0, LOW)

    tall = frames + 16
    tall_u = (lane_ids((tall, 128)) // group) * own_u + lane_ids((tall, 128)) % own_u
    tall_j = lane_ids((tall, 128)) % own_u
    pad = jnp.full((16, 128), LOW, F32)

    def skew(value):
        value = jnp.concatenate([value, pad], axis=0)
        for bit in (1, 2, 4, 8):
            value = jnp.where((tall_u // bit) % 2 == 1, pltpu.roll(value, bit, 0), value)
        return value

    def unskew(value):
        for bit in (1, 2, 4, 8):
            value = jnp.where((tall_u // bit) % 2 == 1, pltpu.roll(value, tall - bit, 0), value)
        return value[:frames]

    up = 128 - (group - own_u + 1)

    def next_up(value, jj):
        return jnp.where(jj == 0, pltpu.roll(value, group - own_u + 1, 1), pltpu.roll(value, 1, 1))

    def next_down(value, jj):
        return jnp.where(jj == own_u - 1, pltpu.roll(value, up, 1), pltpu.roll(value, 127, 1))

    lead = jnp.full((8, 128), LOW, F32)

    def keep(i, value):
        skewed[i, 0:8, :] = lead
        skewed[i, 8 : 8 + tall, :] = value

    for d in range(1, 5):
        keep(d - 1, skew(blank[d]))
    for d in range(5):
        value = skew(emit[d])
        keep(4 + d, value)
        keep(9 + d, next_up(value, tall_j))
    keep(14, skew(start))
    keep(15, skew(closing))
    waves = frames + last_u
    one_j = lane_ids((1, 128)) % own_u
    low_row = skewed[0, 0:1, :]

    def at(i, w):
        return skewed[i, pl.ds(w + 8, 1), :]

    def combine(old, near):
        top_old, sum_old = lse_of(old)
        top = functools.reduce(jnp.maximum, near, top_old)
        total = sum_old * jnp.exp(top_old - top)
        for v in near:
            total = total + jnp.exp(v - top)
        return top + jnp.log(total)

    def wave(i, carry):
        a, ra, b, rb = carry
        old = [at(14, i)]
        for d in range(2, 5):
            old.append(a[d - 1] + at(d - 1, i - d))
        for d in range(2, 6):
            old.append(ra[d - 1] + at(8 + d, i - d))
        new_a = combine(old, [a[0] + at(0, i - 1), ra[0] + at(9, i - 1)])
        back = waves - 1 - i
        old = [at(15, back)]
        for d in range(2, 5):
            old.append(b[d - 1] + at(d - 1, back))
        for d in range(2, 6):
            old.append(rb[d - 1] + at(3 + d, back))
        new_b = combine(old, [b[0] + at(0, back), rb[0] + at(4, back)])
        hist[0, pl.ds(i, 1), :] = new_a
        hist[1, pl.ds(back, 1), :] = new_b
        return (
            (new_a,) + a[:-1],
            (next_up(new_a, one_j),) + ra[:-1],
            (new_b,) + b[:-1],
            (next_down(new_b, one_j),) + rb[:-1],
        )

    hist[...] = jnp.full(hist.shape, LOW, F32)
    lax.fori_loop(
        0, waves, wave, ((low_row,) * 4, (low_row,) * 5, (low_row,) * 4, (low_row,) * 5)
    )
    alpha, beta = unskew(hist[0]), unskew(hist[1])
    ahead = next_down(beta, j)
    norm = jnp.zeros(wide, F32)
    heads = jnp.where(first & (u == 0), beta, 0.0)
    for s in range(segs):
        value = jnp.sum(jnp.where(seg == s, heads, 0.0), axis=0, keepdims=True)
        step = 1
        while step < own_u:
            value = value + pltpu.roll(value, step, 1)
            step *= 2
        step = group
        while step < 128:
            value = value + pltpu.roll(value, step, 1)
            step *= 2
        norm = jnp.where(seg == s, value, norm)
        length = ends[s] - (ends[s - 1] if s else 0)
        loss[pl.ds(s, 1), :] = -value / length[:1].astype(F32)
    base = alpha - norm
    total_a, total_b = None, None
    for d in range(5):
        there = pltpu.roll(ahead, frames - d, 0) if d else ahead
        g = -jnp.exp(base + emit[d] + there)
        total_a = g if d == 0 else total_a + g
        if d:
            gb = -jnp.exp(base + blank[d] + pltpu.roll(beta, frames - d, 0))
            gb = gb - jnp.exp(jnp.where(final & (remain == d), base + blank_raw[d], LOW))
            total_b = gb if d == 1 else total_b + gb
            g = g + gb
        grads[1 + d] = g
    grads[0] = total_b
    grads[6] = total_a


def joint_scratch(dims, width):
    frames, rows, segs, own_u, labs = dims
    span, inner = own_u * frames, rows * segs * own_u
    return [
        pltpu.VMEM((inner, width), F32),
        pltpu.VMEM((rows, span, width + 128), BF),
        pltpu.VMEM((rows, span, width) if width <= ROOMY else (8, 128), BF),
        pltpu.VMEM((width + 128, VOCAB + 128), BF),
        pltpu.VMEM((VOCAB, width) if width <= ROOMY else (8, 128), BF),
        pltpu.VMEM((rows, span, VOCAB), BF),
        pltpu.VMEM((rows, span, 128), F32),
        pltpu.VMEM((16, frames + 24, 128), F32),
        pltpu.VMEM((2, frames + 16, 128), F32),
        pltpu.VMEM((KINDS, frames, 128), F32),
        pltpu.VMEM((inner, width), BF),
    ]


def joint_shared(dims, width):
    frames, rows, segs, own_u, labs = dims
    micro, inner = rows // labs, rows * segs * own_u
    return [
        pltpu.VMEM((micro, frames, width), BF),
        pltpu.VMEM((rows, frames, width), BF),
        pltpu.VMEM((inner, 640), F32),
        pltpu.VMEM((inner, 768), BF),
        pltpu.VMEM((frames, 256), F32),
        pltpu.VMEM((labs, frames, 256), F32),
        pltpu.VMEM((labs, micro, frames, width), BF),
        pltpu.VMEM((labs, micro, frames, width), BF),
        pltpu.VMEM((micro, frames, width), BF),
        pltpu.VMEM((width, 256), BF),
        pltpu.VMEM((16, 256), F32),
        pltpu.SemaphoreType.DMA((3, labs)),
        pltpu.SemaphoreType.DMA((3, labs)),
    ]


class Joint:
    def __init__(self, z, w, dims, predictor, lengths, counts, labels, bias_out, g_predictor, g_pack, loss, shared):
        self.z, self.w, self.dims = z, w, dims
        self.predictor, self.lengths, self.counts, self.labels = predictor, lengths, counts, labels
        self.bias_out, self.g_predictor, self.g_pack, self.loss = bias_out, g_predictor, g_pack, loss
        (
            self.enc_own, self.enc_all, self.pred_wide, self.pred, self.mine, self.terms, self.part, self.came,
            self.g_enc, self.g_mix, self.g_bias, self.send, self.recv,
        ) = shared
        self.micro = dims[1] // dims[4]

    def owner(self, j):
        return ((self.w.side + j // 2) % 2) * 2 + (self.w.core + j % 2) % 2

    def device(self, j):
        return (self.w.dp, self.owner(j))

    def enc_copy(self, j, source):
        to = self.enc_all.at[pl.ds(source * self.micro, self.micro)]
        return remote(self.enc_own, to, self.send.at[0, j], self.recv.at[0, j], self.device(j))

    def term_copy(self, j, source):
        return remote(self.mine, self.terms.at[source], self.send.at[1, j], self.recv.at[1, j], self.device(j))

    def part_copy(self, j):
        return remote(self.part.at[j], self.came.at[j], self.send.at[2, j], self.recv.at[2, j], self.device(j))

    def prepare(self):
        frames, rows, segs, own_u, labs = self.dims
        features = self.predictor.shape[-1]
        for r in range(rows):
            for s in range(segs):
                first = (r * segs + s) * own_u
                self.pred_wide[first : first + own_u, :] = self.predictor[r, s].astype(F32)
        self.pred[:, :features] = self.pred_wide[...].astype(BF)
        self.pred[:, features:] = (lane_ids((self.pred.shape[0], 128)) == BIAS_LANE).astype(BF)

    def share(self):
        for j in range(1, self.dims[4]):
            self.enc_copy(j, self.w.lab).start()
        self.enc_all[pl.ds(self.w.lab * self.micro, self.micro)] = self.enc_own[...]

    def drain(self):
        for j in range(1, self.dims[4]):
            self.enc_copy(j, self.w.lab).wait_send()
            self.term_copy(j, self.w.lab).wait_send()
            self.part_copy(j).wait_send()

    def run(self, full, *scratch):
        joint_run(self, full, *scratch)


def joint_run(
    job, full, proj, hid, slope, wide, back_w, prob, prob_tail, skewed, hist, grads, g_pred
):
    z, dims, lengths, counts, labels, bias_out = job.z, job.dims, job.lengths, job.counts, job.labels, job.bias_out
    frames, rows, segs, own_u, labs = dims
    micro = rows // labs
    n, width, span, features = z.n, z.n * z.jr, own_u * frames, job.predictor.shape[-1]
    pred, mine, terms, enc_all, part, came = job.pred, job.mine, job.terms, job.enc_all, job.part, job.came
    enc_copy, term_copy, part_copy, owner = job.enc_copy, job.term_copy, job.part_copy, job.owner
    g_predictor, g_pack, g_mix, g_bias, g_enc, loss = (
        job.g_predictor, job.g_pack, job.g_mix, job.g_bias, job.g_enc, job.loss
    )
    turn = STEP if width <= ROOMY else 1
    mixes = rows_of(full[0], n, 0, z.jr)
    proj[...] = mm_t(pred[:, :512], rows_of(full[3], n, 0, z.jr)) + mm_t(pred[:, 512:], mixes[:, :256])
    wide[:width, :512] = rows_of(full[3], n, z.jr, z.jr)
    wide[:width, 512:TOK] = rows_of(full[3], n, 2 * z.jr, z.jr)
    wide[:width, TOK:VOCAB] = mixes[:, 128:256]
    top_row = row_ids((128, TOK)) == 0
    wide[width:, :TOK] = jnp.where(top_row, bias_out[:, :TOK].astype(F32), 0.0).astype(BF)
    mine[:, :128] = jnp.zeros((frames, 128), F32)
    mine[:1, : bias_out.shape[1] - TOK] = bias_out[:, TOK:].astype(F32)
    wide[width:, TOK:VOCAB] = jnp.where(row_ids((128, 128)) == 0, mine[:1, :128], 0.0).astype(BF)
    lane_1 = lane_ids((1, 128))
    wanted = jnp.zeros((1, 128), jnp.int32)
    for r in range(rows):
        for s in range(segs):
            for u in range(own_u):
                wanted = jnp.where(lane_1 == (r * segs + s) * own_u + u, labels[s, u, r], wanted)
    wide[:, VOCAB:] = mm(wide[:, :TOK], (row_ids((TOK, 128)) == wanted).astype(BF)).astype(BF)
    roomy = width <= ROOMY
    if roomy:
        back_w[...] = wide[:width, :VOCAB].astype(F32).T.astype(BF)
    hid[:, :, width:] = (lane_ids((rows, span, 128)) == 0).astype(BF)
    lane_t = lane_ids((frames, 128))
    lane_w = lane_ids((frames, TOK))
    group = rows * own_u
    per_vreg = 128 // group

    def row_of(k):
        return owner(k // micro) * micro + k % micro

    def forward(k):
        r = row_of(k)
        ends = scalar_ends(lengths, r, segs)
        seg = seg_of(row_ids((frames, width)), ends)
        enc = enc_all[r].astype(F32)
        for u in range(own_u):
            at = slice(u * frames, (u + 1) * frames)
            per_frame = pick(
                seg, [proj[pl.ds(r * segs * own_u + s * own_u + u, 1), :] for s in range(segs)]
            )
            value = jnp.tanh(enc + per_frame)
            hid[r, at, :width] = value.astype(BF)
            if roomy:
                slope[r, at, :] = (1.0 - value * value).astype(BF)
        logits = mm(hid[r], wide[...])
        seg_l = seg_of(row_ids((frames, 128)), ends)
        for u in range(own_u):
            at = slice(u * frames, (u + 1) * frames)
            logit, last, named = logits[at, :TOK], logits[at, TOK:VOCAB], logits[at, VOCAB:]
            top = jnp.maximum(jnp.max(logit, axis=1, keepdims=True), last[:, 0:1])
            top_dur = jnp.max(
                jnp.where((lane_t >= 1) & (lane_t <= 5), last, -jnp.inf), axis=1, keepdims=True
            )
            is_tok = lane_t == 0
            e_last = jnp.where(
                lane_t < 6, jnp.exp(jnp.where(lane_t < 6, last - jnp.where(is_tok, top, top_dur), 0.0)), 0.0
            )
            e = jnp.exp(logit - top)
            total = jnp.sum(e, axis=1, keepdims=True) + e_last[:, 0:1]
            total_dur = jnp.sum(jnp.where(is_tok, 0.0, e_last), axis=1, keepdims=True)
            prob[r, at, :TOK] = e.astype(BF)
            over = 1.0 / total
            prob_tail[r, at, :] = jnp.where(lane_t == 6, over, e_last * jnp.where(is_tok, over, 1.0 / total_dur))
            norm_tok, norm_dur = top + jnp.log(total), top_dur + jnp.log(total_dur)
            column = r * segs * own_u + seg_l * own_u + u
            at_label = jnp.sum(jnp.where(lane_t == column, named, 0.0), axis=1, keepdims=True) - norm_tok
            lp = last - jnp.where(is_tok, norm_tok, norm_dur)
            for half in range(2):
                cols = slice(half * 128, half * 128 + 128)
                value = mine[:, cols]
                for kind in range(half * per_vreg, min(KINDS, (half + 1) * per_vreg)):
                    column = at_label if kind == 6 else lp[:, kind : kind + 1]
                    value = jnp.where(lane_t == (kind % per_vreg) * group + r * own_u + u, column, value)
                mine[:, cols] = value

    mine[...] = jnp.zeros(mine.shape, F32)

    def forward_step(i, _):
        for j in range(1, labs):
            @pl.when(i * turn == j * micro)
            def _():
                enc_copy(j, owner(j)).wait_recv()
        for k in range(turn):
            forward(i * turn + k)
        return 0

    lax.fori_loop(0, rows // turn, forward_step, 0)
    terms[job.w.lab] = mine[...]

    for j in range(1, labs):
        term_copy(j, job.w.lab).start()
    for j in range(1, labs):
        term_copy(j, owner(j)).wait_recv()
    lattice(lengths, counts, terms, skewed, hist, grads, loss, dims)

    def backward(k):
        r = row_of(k)
        ends = scalar_ends(lengths, r, segs)
        shift = (256 - job.w.lab * group - r * own_u) % 128
        rolled = [pltpu.roll(grads[kind], shift, 1) for kind in range(KINDS)]
        seg_l = seg_of(row_ids((frames, TOK)), ends)
        for u in range(own_u):
            at = slice(u * frames, (u + 1) * frames)
            a, b = rolled[6][:, u : u + 1], rolled[0][:, u : u + 1]
            both = a + b
            label = pick(seg_l, [labels[s, u, r] for s in range(segs)])
            tails = prob_tail[r, at, :]
            scaled = both * tails[:, 6:7]
            prob[r, at, :TOK] = (jnp.where(lane_w == label, a, 0.0) - prob[r, at, :TOK].astype(F32) * scaled).astype(BF)
            aim = jnp.zeros((frames, 128), F32)
            for kind in range(6):
                aim = jnp.where(lane_t == kind, rolled[kind][:, u : u + 1], aim)
            prob[r, at, TOK:] = jnp.where(lane_t < 6, aim - tails * both, 0.0).astype(BF)
        if roomy:
            back = mm(prob[r], back_w[...]) * slope[r].astype(F32)
        else:
            value = hid[r, :, :width].astype(F32)
            back = mm_t(prob[r], wide[:width, :VOCAB]) * (1.0 - value * value)
        summed = back[:frames]
        for u in range(1, own_u):
            summed = summed + back[u * frames : (u + 1) * frames]
        part[k // micro, k % micro] = summed.astype(BF)
        shape = (segs * own_u, span)
        lanes = lane_ids(shape)
        seg_t = seg_of(lanes % frames, ends)
        hit = (row_ids(shape) == seg_t * own_u + lanes // frames).astype(BF)
        g_pred[pl.ds(r * segs * own_u, segs * own_u), :] = mm(hit, back.astype(BF)).astype(BF)

    def backward_step(i, _):
        first = rows - (i + 1) * turn
        for k in range(turn - 1, -1, -1):
            backward(first + k)
        for j in range(1, labs):
            @pl.when(first == j * micro)
            def _():
                part_copy(j).start()
        return 0

    lax.fori_loop(0, rows // turn, backward_step, 0)
    gp = g_pred[...]
    g_predictor[:, :512] = mm(gp, rows_of(full[3], n, 0, z.jr))
    g_predictor[:, 512:] = mm(gp, rows_of(full[0], n, 0, z.jr)[:, : features - 512])
    shards, block = n, z.jr
    h_all = hid[...].reshape(rows * span, width + 128)
    g_bias[...] = jnp.zeros(g_bias.shape, F32)
    from_pred = t_mm(gp, pred[...])
    for i in range(2):
        piece = t_mm(h_all, prob[:, :, i * 512 : i * 512 + 512].reshape(rows * span, 512))
        for q in range(2):
            g_bias[2 * i + q : 2 * i + q + 1, :] = piece[width : width + 1, 256 * q : 256 * q + 256]
        for d in range(shards):
            first = d * 3 * block + (i + 1) * block
            g_pack[first : first + block, :] = piece[d * block : (d + 1) * block].astype(BF)
    ends_w = t_mm(h_all, prob[:, :, TOK:].reshape(rows * span, 128))
    g_bias[4:5, :128] = ends_w[width : width + 1]
    ends_w = ends_w[:width] + from_pred[:, 640:768]
    for d in range(shards):
        at = slice(d * block, (d + 1) * block)
        g_pack[d * 3 * block : d * 3 * block + block, :] = from_pred[at, :512].astype(BF)
        g_mix[at, :128] = from_pred[at, 512:640].astype(BF)
        g_mix[at, 128:] = ends_w[at].astype(BF)
    for j in range(1, labs):
        part_copy(j).wait_recv()
    total = part[0].astype(F32)
    for j in range(1, labs):
        total = total + came[j].astype(F32)
    g_enc[...] = total.astype(BF)


VOCAB = TOK + 128
STEP = 2
ROOMY = 768


HEADS = 8
EPS = 1e-05
TAPS = 9
GAIN_ROW = 9
STATE = (
    ("n_ffn", 512, F32), ("n_att", 512, F32), ("n_conv", 512, F32), ("n_depth", 512, F32), ("n_out", 512, F32),
    ("scales", 128, F32), ("act", 2048, BF), ("slope", 2048, BF), ("qkv", 1536, BF), ("context", 512, BF),
    ("value", 512, F32), ("gate", 512, F32),
)


def sigmoid(v):
    return 0.5 * jnp.tanh(0.5 * v) + 0.5


def norm_parts(v):
    c = v - jnp.mean(v, axis=1, keepdims=True)
    r = lax.rsqrt(jnp.mean(c * c, axis=1, keepdims=True) + EPS)
    return c * r, r


def norm_back(gy, n, r, gain):
    gg = gy * gain
    gain_grad = jnp.sum(gy * n, axis=0, keepdims=True)
    inner = gg - jnp.mean(gg, axis=1, keepdims=True) - n * jnp.mean(gg * n, axis=1, keepdims=True)
    return r * inner, gain_grad


def rows_of(ref, n, first, count):
    per = ref.shape[0] // n
    return jnp.concatenate([ref[d * per + first : d * per + first + count, :] for d in range(n)], axis=0)


def put_rows(ref, n, first, count, value):
    per = ref.shape[0] // n
    for d in range(n):
        ref[d * per + first : d * per + first + count, :] = value[d * count : (d + 1) * count].astype(ref.dtype)


def own_ends(ints, micro, segs):
    first = lax.axis_index("lab") * micro
    return [scalar_ends(ints, first + m, segs) for m in range(micro)]


def seg_id(position, ends, frames):
    t, row = position % frames, position // frames
    out = seg_of(t, ends[0])
    for m in range(1, len(ends)):
        out = jnp.where(row == m, seg_of(t, ends[m]), out)
    return out + row * len(ends[0])


def shifted(value, step):
    rows = value.shape[0]
    return pltpu.roll(value, (-step) % rows, 0) if step % rows else value


def assemble_small(target, n, per, ds):
    lane = lane_ids((16, 128))
    columns = [jnp.zeros((16, 128), F32) for _ in range(n * ds // 128)]
    for d in range(n):
        piece = jnp.where(lane < ds, target[d * per : d * per + 16, 256:384].astype(F32), 0.0)
        at = d * ds % 128
        columns[d * ds // 128] = columns[d * ds // 128] + (pltpu.roll(piece, at, 1) if at else piece)
    return jnp.concatenate(columns, axis=1)


def split_small(value, d, ds):
    at = d * ds % 128
    piece = value[:, d * ds // 128 * 128 : d * ds // 128 * 128 + 128]
    piece = pltpu.roll(piece, 128 - at, 1) if at else piece
    return jnp.where(lane_ids((16, 128)) < ds, piece, 0.0)


class Sizes:
    def __init__(self, n, ds, ff, qk, pi, jr):
        self.n, self.ds, self.ff, self.qk, self.pi, self.jr = n, ds, ff, qk, pi, jr
        self.rows = (jr + ff, ff + qk, 2 * ds + pi + jr, 3 * jr)
        self.model = n * ds


def head_pair(ref, block, pair):
    at = block * 512 + pair * 128
    return ref[:, at : at + 128]


def forward_pieces(z, x_ref, ints, dims, full, small_ref, st, probs, encoded, enc_proj):
    frames, rows, segs, own_u, labs = dims
    n, micro = z.n, rows // labs
    count = micro * frames
    ends = own_ends(ints, micro, segs)
    ids_r = seg_id(row_ids((count, 128)), ends, frames)
    ids_c = seg_id(lane_ids((count, count)), ends, frames)
    scale_lane = lane_ids((count, 128))

    def norm(v, name, which):
        nv, r = norm_parts(v)
        st[name][...] = nv
        st["scales"][...] = jnp.where(scale_lane == which, r, st["scales"][...])
        return nv * small_ref[GAIN_ROW + which : GAIN_ROW + which + 1, :]

    small_ref[...] = assemble_small(full[0], n, z.rows[0], z.ds)
    st["scales"][...] = jnp.zeros((count, 128), F32)
    x = x_ref[...].reshape(count, z.model).astype(F32)
    ffn_in = norm(x, "n_ffn", 0).astype(BF)
    half = n // 2
    per = z.rows[0]
    for part in range(2):
        w = jnp.concatenate(
            [full[0][d * per + z.jr : d * per + z.jr + z.ff, :] for d in range(part * half, part * half + half)], axis=0
        )
        pre = mm_t(ffn_in, w)
        sg = sigmoid(pre)
        at = slice(part * half * z.ff, (part + 1) * half * z.ff)
        st["act"][:, at] = (pre * sg).astype(BF)
        st["slope"][:, at] = (sg * (1.0 + pre * (1.0 - sg))).astype(BF)
        yield
    after_ffn = x + 0.5 * mm(st["act"][...], rows_of(full[1], n, 0, z.ff))
    att_in = norm(after_ffn, "n_att", 1).astype(BF)
    st["qkv"][...] = mm_t(att_in, rows_of(full[1], n, z.ff, z.qk)).astype(BF)
    yield
    same = ids_r == ids_c
    low_half = lane_ids((count, 128)) < 64
    for pair in range(HEADS // 2):
        q, k, v = (head_pair(st["qkv"], b, pair) for b in range(3))
        total = None
        for side in range(2):
            keep = low_half if side == 0 else ~low_half
            score = mm_t(jnp.where(keep, q, 0), k) * (64 ** -0.5)
            score = jnp.where(same, score, LOW)
            e = jnp.exp(score - jnp.max(score, axis=1, keepdims=True))
            p = (e * (1.0 / jnp.sum(e, axis=1, keepdims=True))).astype(BF)
            probs[2 * pair + side] = p
            part = mm(p, jnp.where(keep, v, 0))
            total = part if total is None else total + part
        st["context"][:, pair * 128 : pair * 128 + 128] = total.astype(BF)
    yield
    after_att = after_ffn + mm(st["context"][...], rows_of(full[2], n, 0, z.ds))
    conv_in = norm(after_att, "n_conv", 2).astype(BF)
    conv_pre = mm_t(conv_in, rows_of(full[2], n, z.ds, z.pi))
    st["value"][...] = conv_pre[:, : z.model]
    st["gate"][...] = sigmoid(conv_pre[:, z.model :])
    depth = []
    for c in range(z.model // 128):
        at = slice(c * 128, c * 128 + 128)
        gated = st["value"][:, at] * st["gate"][:, at]
        total = jnp.zeros((count, 128), F32)
        for j in range(TAPS):
            ok = shifted(ids_r, j - TAPS // 2) == ids_r
            total = total + jnp.where(ok, shifted(gated, j - TAPS // 2), 0.0) * small_ref[j : j + 1, at]
        depth.append(total)
    dn = norm(jnp.concatenate(depth, axis=1), "n_depth", 3)
    conv_act = (dn * sigmoid(dn)).astype(BF)
    after_conv = after_att + mm(conv_act, rows_of(full[2], n, z.ds + z.pi, z.ds))
    out = norm(after_conv, "n_out", 4).astype(BF)
    encoded[...] = out.reshape(encoded.shape)
    enc_proj[...] = mm_t(out, rows_of(full[2], n, 2 * z.ds + z.pi, z.jr)).astype(BF).reshape(enc_proj.shape)
    yield


def backward_pieces(z, g_enc, ints, dims, full, small_ref, st, probs, grads, small_grad, grad_frames):
    frames, rows, segs, own_u, labs = dims
    n, micro = z.n, rows // labs
    count = micro * frames
    ends = own_ends(ints, micro, segs)
    ids_r = seg_id(row_ids((count, 128)), ends, frames)

    def gain(which):
        return small_ref[GAIN_ROW + which : GAIN_ROW + which + 1, :]

    def back(gy, name, which):
        g, gain_grad = norm_back(gy, st[name][...], st["scales"][:, which : which + 1], gain(which))
        small_grad[GAIN_ROW + which : GAIN_ROW + which + 1, :] = gain_grad
        return g

    def normed(name, which):
        return (st[name][...] * gain(which)).astype(BF)

    small_grad[...] = jnp.zeros(small_grad.shape, F32)
    ge = g_enc[...].reshape(count, -1)
    off = 2 * z.ds + z.pi
    put_rows(grads[2], n, off, z.jr, t_mm(ge, normed("n_out", 4)))
    g_conv_sum = back(mm(ge, rows_of(full[2], n, off, z.jr)), "n_out", 4)
    branch = g_conv_sum.astype(BF)
    dn = st["n_depth"][...] * gain(3)
    sg = sigmoid(dn)
    put_rows(grads[2], n, z.ds + z.pi, z.ds, t_mm((dn * sg).astype(BF), branch))
    g_act = mm_t(branch, rows_of(full[2], n, z.ds + z.pi, z.ds))
    g_depth = back(g_act * (sg * (1.0 + dn * (1.0 - sg))), "n_depth", 3)
    yield
    low_a, low_b = [], []
    for c in range(z.model // 128):
        at = slice(c * 128, c * 128 + 128)
        value, gate = st["value"][:, at], st["gate"][:, at]
        gated, gd = value * gate, g_depth[:, at]
        total = jnp.zeros((count, 128), F32)
        for j in range(TAPS):
            step = j - TAPS // 2
            ok = shifted(ids_r, step) == ids_r
            small_grad[j : j + 1, at] = jnp.sum(jnp.where(ok, shifted(gated, step), 0.0) * gd, axis=0, keepdims=True)
            ok = shifted(ids_r, -step) == ids_r
            total = total + jnp.where(ok, shifted(gd, -step), 0.0) * small_ref[j : j + 1, at]
        low_a.append((total * gate).astype(BF))
        low_b.append((total * value * gate * (1.0 - gate)).astype(BF))
    low = jnp.concatenate(low_a + low_b, axis=1)
    put_rows(grads[2], n, z.ds, z.pi, t_mm(low, normed("n_conv", 2)))
    g_att_sum = g_conv_sum + back(mm(low, rows_of(full[2], n, z.ds, z.pi)), "n_conv", 2)
    branch = g_att_sum.astype(BF)
    put_rows(grads[2], n, 0, z.ds, t_mm(st["context"][...], branch))
    g_context = mm_t(branch, rows_of(full[2], n, 0, z.ds)).astype(BF)
    yield
    low_half = lane_ids((count, 128)) < 64
    columns = [[], [], []]
    for pair in range(HEADS // 2):
        q, k, v = (head_pair(st["qkv"], b, pair) for b in range(3))
        gc = g_context[:, pair * 128 : pair * 128 + 128]
        sums = [None, None, None]
        for side in range(2):
            keep = low_half if side == 0 else ~low_half
            p = probs[2 * pair + side]
            gc_h = jnp.where(keep, gc, 0)
            gp = mm_t(gc_h, v)
            pf = p.astype(F32)
            gs = (pf * (gp - jnp.sum(gp * pf, axis=1, keepdims=True))).astype(BF)
            parts = (
                mm(gs, jnp.where(keep, k, 0)) * (64 ** -0.5),
                t_mm(gs, jnp.where(keep, q, 0)) * (64 ** -0.5),
                t_mm(p, gc_h),
            )
            sums = [b if a is None else a + b for a, b in zip(sums, parts)]
        for b in range(3):
            columns[b].append(sums[b].astype(BF))
    g_qkv = jnp.concatenate(columns[0] + columns[1] + columns[2], axis=1)
    yield
    put_rows(grads[1], n, z.ff, z.qk, t_mm(g_qkv, normed("n_att", 1)))
    g_ffn_sum = g_att_sum + back(mm(g_qkv, rows_of(full[1], n, z.ff, z.qk)), "n_att", 1)
    branch = (0.5 * g_ffn_sum).astype(BF)
    put_rows(grads[1], n, 0, z.ff, t_mm(st["act"][...], branch))
    yield
    g_pre = (mm_t(branch, rows_of(full[1], n, 0, z.ff)) * st["slope"][...].astype(F32)).astype(BF)
    put_rows(grads[0], n, z.jr, z.ff, t_mm(g_pre, normed("n_ffn", 0)))
    gx = g_ffn_sum + back(mm(g_pre, rows_of(full[0], n, z.jr, z.ff)), "n_ffn", 0)
    grad_frames[...] = gx.reshape(grad_frames.shape)
    yield


ORDER = (
    (-2, 0), (-2, 1), (-1, 0), (1, 0), (0, 0), (-2, 2), (-1, 1), (0, 0), (-2, 3), (1, 1), (0, 0), (-1, 2), (0, 0), (-1, 3),
    (1, 2), (0, 0), (1, 3),
)


def pass_kernel(
    z, dims, x_ref, lengths, counts, labels, w_in, w_out, w_qkv, w_att, w_pin, w_pout, w_enc, w_pred, w_joint,
    bias_joint, w_depth, gain0, gain1, gain2, gain3, gain4, predictor, bias_out,
    own0, own1, own2, own3, grad_frames, encoded, loss, g_predictor, *rest,
):
    k = len(STATE)
    st = {name: ref for (name, _, _), ref in zip(STATE, rest[:k])}
    probs, small_in, tail, small_ref, small_grad, g_pack = rest[k : k + 6]
    rest = rest[k + 6 :]
    sources, full, bufs, rest = rest[:4], rest[4:8], rest[8:28], rest[28:]
    shared, (ring_recv, x_recv, sems, send, recv) = rest[:-5], rest[-5:]
    n = z.n
    w = Where(n)
    jr, js, ds = z.jr, w_pred.shape[0], z.ds
    job = Joint(z, w, dims, predictor, lengths, counts, labels, bias_out, g_predictor, g_pack, loss, shared)
    small_in[...] = jnp.zeros(small_in.shape, F32)
    small_in[:TAPS, :ds] = w_depth[...].astype(F32)
    for i, gain in enumerate((gain0, gain1, gain2, gain3, gain4)):
        small_in[GAIN_ROW + i : GAIN_ROW + i + 1, :ds] = gain[...].astype(F32)
    tail[...] = jnp.zeros(tail.shape, F32)
    tail[:1, :js] = bias_joint[...].astype(F32)
    column = tail[:8, :].T[:jr, :1]
    tail[:8, :] = jnp.zeros((8, 128), F32)
    tail[:js, : w_joint.shape[1] - 1024] = w_joint[:, 1024:].astype(F32)
    tail[...] = jnp.where(lane_ids((jr, 128)) == BIAS_LANE, column, tail[...])

    def down(value, count):
        rows = value.shape[0]
        return jnp.concatenate([value, jnp.zeros((count - rows,) + value.shape[1:], value.dtype)], 0) if count > rows else value

    pred_t = down(w_pred[...], jr)

    def fill(g):
        if g == 0:
            sources[0][jr:, :] = w_in[...].astype(F32).T.astype(BF)
            sources[0][:jr, 0:128] = pred_t[:, 512:]
            sources[0][:jr, 128:256] = tail[...].astype(BF)
            sources[0][:jr, 256:] = jnp.zeros((jr, 256), BF)
            sources[0][:16, 256:384] = small_in[...].astype(BF)
        elif g == 1:
            sources[1][: z.ff, :] = w_out[...]
            sources[1][z.ff :, :] = w_qkv[...]
        elif g == 2:
            sources[2][:ds, :] = w_att[...]
            sources[2][ds : ds + z.pi, :] = w_pin[...].astype(F32).T.astype(BF)
            sources[2][ds + z.pi : 2 * ds + z.pi, :] = w_pout[...]
            sources[2][2 * ds + z.pi :, :] = down(w_enc[...], jr)
        elif g == 3:
            sources[3][:jr, :] = pred_t[:, :512]
            sources[3][jr : 2 * jr, :] = down(w_joint[:, :512], jr)
            sources[3][2 * jr :, :] = down(w_joint[:, 512:1024], jr)

    parts = [
        Gather(w, sources[i], full[i], z.rows[i], ring_recv.at[i], x_recv.at[i], sems.at[i]) for i in range(4)
    ]
    turns = n // 2 + 2
    fill(0)
    w.greet()
    compute = forward_pieces(z, x_ref, lengths, dims, full, small_ref, st, probs, encoded, job.enc_own)
    for s in range(turns - 2):
        for g in range(4):
            if s == 0 and g:
                fill(g)
            parts[g].step(s)
        if s == 0:
            job.prepare()
    pieces = 0
    for what, g in ORDER:
        if what == 0:
            next(compute)
            pieces += 1
            if pieces == 5:
                job.share()
        elif what == 1:
            parts[g].whole()
        else:
            parts[g].step(turns + what)
    pl.run_scoped(lambda *scratch: job.run(full, *scratch), *joint_scratch(dims, n * jr))
    outs = (own0, own1, own2, own3)

    def finish(*grads):
        packs = list(grads) + [g_pack]
        sums = [
            Scatter(w, packs[g], outs[g], z.rows[g], bufs[5 * g : 5 * g + 5], send.at[g], recv.at[g], SHARES[3 - g])
            for g in (3, 2, 1, 0)
        ]
        pieces = backward_pieces(
            z, job.g_enc, lengths, dims, full, small_ref, st, probs, packs, small_grad, grad_frames
        )

        def work(i):
            for _ in range((0, 2, 2, 1)[i]):
                next(pieces)
            if i == 3:
                for d in range(n):
                    at = d * z.rows[0]
                    packs[0][at : at + jr, :256] = job.g_mix[d * jr : (d + 1) * jr, :]
                    if jr > 32:
                        packs[0][at + 32 : at + jr, 256:] = jnp.zeros((jr - 32, 256), BF)
                    packs[0][at : at + 16, 256:384] = split_small(small_grad[...], d, ds).astype(BF)
                    packs[0][at : at + 16, 384:] = jnp.zeros((16, 128), BF)
                    packs[0][at + 16 : at + 32, 256:] = job.g_bias[...].astype(BF)

        sum_up(sums, work, ORDER_SUMS)

    pl.run_scoped(finish, *[pltpu.VMEM((n * z.rows[g], 512), BF) for g in range(3)])
    job.drain()
    for part in parts:
        part.drain()


def pass_call(z, dims, x, ints, params, predictor, bias_out):
    frames, rows, segs, own_u, labs = dims
    n, micro = z.n, rows // labs
    count, width = micro * frames, n * z.jr
    vm, sm = (pl.BlockSpec(memory_space=m) for m in (pltpu.VMEM, pltpu.SMEM))
    shape = jax.ShapeDtypeStruct
    outs = [shape((r, 512), BF) for r in z.rows]
    outs += [shape((micro, frames, z.model), F32), shape((micro, frames, z.model), BF), shape((8, 128), F32)]
    outs += [shape((rows * segs * own_u, predictor.shape[-1]), F32)]
    scratch = [pltpu.VMEM((count, lanes), dtype) for _, lanes, dtype in STATE]
    scratch += [pltpu.VMEM((HEADS, count, count), BF), pltpu.VMEM((16, 128), F32), pltpu.VMEM((z.jr, 128), F32)]
    scratch += [pltpu.VMEM((16, z.model), F32)] * 2 + [pltpu.VMEM((3 * width, 512), BF)]
    scratch += [pltpu.VMEM((r, 512), BF) for r in z.rows] + [pltpu.VMEM((n * r, 512), BF) for r in z.rows]
    for g, r in enumerate(z.rows):
        scratch += scatter_scratch(n, r, 512, SHARES[3 - g])
    scratch += joint_shared(dims, width)
    scratch += [pltpu.SemaphoreType.DMA((4, n - 1))] * 2 + [pltpu.SemaphoreType.DMA((4, 5))] + scatter_sems(n, 4)
    return pl.pallas_call(
        functools.partial(pass_kernel, z, dims),
        out_shape=outs,
        in_specs=[vm] + [sm] * 3 + [vm] * (len(params) + 2),
        out_specs=[vm] * len(outs),
        scratch_shapes=scratch,
        compiler_params=pltpu.CompilerParams(collective_id=0, has_side_effects=True, vmem_limit_bytes=62 * 2**20),
    )(x, *ints, *params, predictor, bias_out)


SHARES = (0.2, 0.2, 0.3, 0.25)
ORDER_SUMS = (
    (0, 0, 0), (0, 1, 0), (0, 2, 0), (1, 0, 0), (3, 0, 0), (2, 0, 1), (0, 3, 0), (1, 1, 0), (2, 1, 1), (2, 0, 2),
    (3, 1, 0), (1, 2, 0), (2, 2, 1), (2, 1, 2), (1, 3, 0), (3, 2, 0), (3, 0, 1), (2, 0, 3), (2, 2, 2), (3, 3, 0),
    (2, 3, 1), (2, 1, 3), (3, 0, 2), (3, 1, 1), (2, 0, 4), (2, 2, 3), (2, 3, 2), (2, 1, 4), (3, 0, 3), (3, 1, 2),
    (2, 0, 5), (2, 2, 4), (3, 2, 1), (2, 3, 3), (2, 1, 5), (3, 0, 4), (3, 1, 3), (3, 3, 1), (2, 2, 5), (3, 2, 2),
    (2, 0, 6), (2, 3, 4), (3, 0, 5), (2, 1, 6), (3, 3, 2), (2, 0, 7), (3, 1, 4), (3, 2, 3), (2, 2, 6), (3, 0, 6),
    (2, 1, 7), (2, 3, 5), (3, 3, 3), (2, 2, 7), (3, 0, 7), (3, 1, 5), (3, 2, 4), (3, 3, 4), (2, 3, 6), (3, 1, 6),
    (3, 2, 5), (3, 1, 7), (2, 3, 7), (3, 3, 5), (3, 2, 6), (3, 3, 6), (3, 2, 7), (3, 3, 7),
)


def unpack_kernel(z, dims, js, own0, own1, own2, own3, grads, encoded, loss, g_predictor, *outs):
    frames, rows, segs, own_u, labs = dims
    ds, ff, pi, jr = z.ds, z.ff, z.pi, z.jr
    (
        loss_o, enc_o, grads_o, pred_o, gg0, g_in, g_out, gg1, g_qkv, g_att, gg2, g_pin, g_depth, gg3, g_pout, gg4,
        g_enc, g_pred, g_bias, g_joint, g_bias_out,
    ) = outs
    hit = (row_ids((128, rows)) == lane_ids((128, rows)) * own_u).astype(F32)
    loss_o[...] = lax.dot_general(
        loss[...], hit, (((1,), (0,)), ((), ())), precision=lax.Precision.HIGHEST, preferred_element_type=F32
    )[:segs]
    enc_o[...] = encoded[...]
    grads_o[...] = grads[...]
    for r in range(rows):
        for s in range(segs):
            first = (r * segs + s) * own_u
            pred_o[r, s] = g_predictor[first : first + own_u, :]
    small = own0[:32, 256:].astype(F32)
    for i, out in enumerate((gg0, gg1, gg2, gg3, gg4)):
        out[...] = small[GAIN_ROW + i : GAIN_ROW + i + 1, :ds]
    g_depth[...] = small[:TAPS, :ds]
    for i in range(4):
        g_bias_out[:, 256 * i : 256 * i + 256] = small[16 + i : 17 + i, :]
    g_bias_out[:, 1024:] = small[20:21, : g_bias_out.shape[1] - 1024]
    g_in[...] = own0[jr:, :].astype(F32).T
    g_out[...] = own1[:ff, :].astype(F32)
    g_qkv[...] = own1[ff:, :].astype(F32)
    g_att[...] = own2[:ds, :].astype(F32)
    g_pin[...] = own2[ds : ds + pi, :].astype(F32).T
    g_pout[...] = own2[ds + pi : 2 * ds + pi, :].astype(F32)
    g_enc[...] = own2[2 * ds + pi :, :].astype(F32)[:js]
    g_pred[:, :512] = own3[:jr, :].astype(F32)[:js]
    g_pred[:, 512:] = own0[:jr, :128].astype(F32)[:js]
    tail = own0[:jr, 128:256].astype(F32)
    wide = jnp.concatenate([tail, jnp.zeros((128 - jr, 128), F32)], axis=0) if jr < 128 else tail
    g_bias[...] = wide.T[BIAS_LANE : BIAS_LANE + 1, :js]
    g_joint[:, :512] = own3[jr : 2 * jr, :].astype(F32)[:js]
    g_joint[:, 512:1024] = own3[2 * jr :, :].astype(F32)[:js]
    g_joint[:, 1024:] = tail[:js, : g_joint.shape[1] - 1024]


def unpack_call(z, dims, js, out_width, own, grads, encoded, loss, g_predictor):
    frames, rows, segs, own_u, labs = dims
    shape = jax.ShapeDtypeStruct
    row = shape((1, z.ds), F32)
    line, features = z.model, g_predictor.shape[1]
    outs = [
        shape((segs, rows), F32), shape(encoded.shape, BF), shape(grads.shape, F32),
        shape((rows, segs, own_u, features), F32), row, shape((line, z.ff), F32), shape((z.ff, line), F32), row,
        shape((z.qk, line), F32), shape((z.ds, line), F32), row, shape((line, z.pi), F32), shape((TAPS, z.ds), F32),
        row, shape((z.ds, line), F32), row, shape((js, line), F32), shape((js, features), F32), shape((1, js), F32),
        shape((js, out_width), F32), shape((1, out_width), F32),
    ]
    vm = pl.BlockSpec(memory_space=pltpu.VMEM)
    return pl.pallas_call(
        functools.partial(unpack_kernel, z, dims, js),
        out_shape=outs,
        in_specs=[vm] * 8,
        out_specs=[vm] * len(outs),
        compiler_params=pltpu.CompilerParams(vmem_limit_bytes=60 * 2**20),
    )(*own, grads, encoded, loss, g_predictor)

def local(
    frames_in, predictor, seg_lengths, label_counts, label_ids, gain_ffn, w_ffn_in, w_ffn_out, gain_att, w_qkv,
    w_att_out, gain_conv, w_point_in, w_depth, gain_depth, w_point_out, gain_out, w_enc, w_pred, bias_joint,
    w_joint_out, bias_out,
):
    n, labs = lax.axis_size("dp"), lax.axis_size("lab")
    micro, frames, model = frames_in.shape
    rows, segs, own_u, joint = predictor.shape
    ds, js = model // n, w_pred.shape[1]
    jr = max(-(-js // TILE), 2) * TILE
    z = Sizes(n, ds, w_ffn_in.shape[1], w_qkv.shape[1], w_point_in.shape[1], jr)
    dims = (frames, rows, segs, own_u, labs)
    lengths, counts, labels = seg_lengths.T, label_counts.T, label_ids.transpose(1, 2, 0)
    gains = [g[None] for g in (gain_ffn, gain_att, gain_conv, gain_depth, gain_out)]
    params = (
        w_ffn_in, w_ffn_out, w_qkv.T, w_att_out, w_point_in, w_point_out, w_enc.T, w_pred.T, w_joint_out,
        bias_joint[None], w_depth, *gains,
    )
    *own, grad_frames, encoded, loss, g_predictor = pass_call(
        z, dims, frames_in, (lengths, counts, labels), params, predictor, bias_out[None]
    )
    (
        loss, encoded, grad_frames, g_predictor, gg0, g_in, g_out, gg1, g_qkv, g_att, gg2, g_pin, g_depth, gg3, g_pout,
        gg4, g_enc, g_pred, g_bias, g_joint, g_bias_out,
    ) = unpack_call(z, dims, js, bias_out.shape[0], own, grad_frames, encoded, loss, g_predictor)
    return (
        loss.T, encoded, grad_frames, g_predictor, gg0[0], g_in, g_out, gg1[0], g_qkv.T, g_att, gg2[0], g_pin, g_depth,
        gg3[0], g_pout, gg4[0], g_enc.T, g_pred.T, g_bias[0], g_joint, g_bias_out[0],
    )


def solution(mesh):
    rows, whole = P(("dp", "lab"), None, None), P()
    predictor, columns, lines, vector = P("dp", None, "lab", None), P(None, "dp"), P("dp", None), P("dp")
    params = (
        vector, columns, lines, vector, columns, lines, vector, columns, columns, vector, lines, vector, columns,
        columns, vector, lines, whole,
    )
    return jax.shard_map(
        local,
        mesh=mesh,
        in_specs=(rows, predictor, lines, lines, P("dp", None, "lab")) + params,
        out_specs=(lines, rows, rows, predictor) + params,
        check_vma=False,
    )
```

```python
import functools

import jax
import jax.numpy as jnp
from jax import lax
from jax.experimental import pallas as pl
from jax.experimental.pallas import tpu as pltpu
from jax.sharding import PartitionSpec as P


MESH = pl.DeviceIdType.MESH
F32 = jnp.float32
BF = jnp.bfloat16
TILE = 16


def ring_place(dp, n):
    odd = dp % 2
    return (1 - odd) * (dp // 2) + odd * (n - 1 - dp // 2)


def ring_device(place, n):
    place = (place + 2 * n) % n
    high = place // (n // 2)
    return (1 - high) * (2 * place) + high * (2 * (n - 1 - place) + 1)


def x_rows(rows, share):
    tiles = rows // TILE
    return min(tiles // 2, int(tiles * share + 0.5)) * TILE


class Where:
    def __init__(self, n):
        self.n = n
        self.dp = lax.axis_index("dp")
        self.lab = lax.axis_index("lab")
        self.core = self.lab % 2
        self.side = self.lab // 2
        self.place = ring_place(self.dp, n)
        self.right = (ring_device(self.place + 1, n), self.lab)
        self.left = (ring_device(self.place - 1, n), self.lab)
        self.twin = (self.dp, self.side * 2 + 1 - self.core)
        self.across = (self.dp, (1 - self.side) * 2 + self.core)
        self.far = (ring_device(self.place + 1 - 2 * self.core, n), self.lab)
        self.far_back = (ring_device(self.place + 2 * self.core - 1, n), self.lab)
        self.corner = (self.dp, (1 - self.side) * 2 + 1 - self.core)

    def at(self, distance):
        return ring_device(self.place + distance, self.n)

    def greet(self):
        barrier = pltpu.get_barrier_semaphore()
        others = (self.right, self.left, self.twin, self.across, self.corner)
        for other in others:
            pl.semaphore_signal(barrier, inc=1, device_id=other, device_id_type=MESH)
        pl.semaphore_wait(barrier, len(others))


def remote(src, dst, send_sem, recv_sem, device):
    return pltpu.make_async_remote_copy(
        src_ref=src,
        dst_ref=dst,
        send_sem=send_sem,
        recv_sem=recv_sem,
        device_id=device,
        device_id_type=MESH,
    )


class Gather:
    def __init__(self, where, source, target, rows, ring_recv, x_recv, sems, share):
        self.w, self.source, self.target, self.rows = where, source, target, rows
        self.width = target.shape[1]
        self.half = self.width // 2
        self.cut = x_rows(rows, share)
        self.ring_recv, self.x_recv, self.sems = ring_recv, x_recv, sems
        self.steps = where.n // 2

    def lanes(self):
        return pl.ds(pl.multiple_of(self.w.core * self.half, 128), self.half)

    def rows_at(self, shard, offset, size):
        base = shard * self.rows if shard is not None else 0
        return pl.ds(pl.multiple_of(base + offset, TILE), size)

    def ring_part(self, ref, shard):
        return ref.at[self.rows_at(shard, self.w.side * self.cut, self.rows - self.cut), self.lanes()]

    def x_part(self, ref, shard, side):
        return ref.at[self.rows_at(shard, side * (self.rows - self.cut), self.cut), self.lanes()]

    def slot(self, distance):
        return distance + self.steps - 1 if distance < 0 else distance + self.steps - 2

    def hop(self, distance, first):
        w = self.w
        if distance == self.steps:
            shard = w.at((2 * w.core - 1) * (self.steps - 1))
            device = w.far
        else:
            shard = w.at(distance + 1) if distance < 0 else w.at(distance - 1)
            device = w.right if distance < 0 else w.left
        src = self.ring_part(self.source, None) if first else self.ring_part(self.target, shard)
        slot = 2 * self.steps - 2 if distance == self.steps else self.slot(distance)
        remote(src, self.ring_part(self.target, shard), self.sems.at[1], self.ring_recv.at[slot], device).start()

    def own(self):
        pltpu.make_async_copy(
            self.source, self.target.at[self.rows_at(self.w.dp, 0, self.rows), :], self.sems.at[4]
        ).start()

    def arrived(self, distance):
        w = self.w
        shard = w.at(distance)
        slot = 2 * self.steps - 2 if distance == self.steps else self.slot(distance)
        part = self.ring_part(self.target, shard)
        remote(part, part, self.sems.at[1], self.ring_recv.at[slot], w.right).wait_recv()

    def spread(self, distance):
        w = self.w
        shard = w.at(distance)
        slot = 2 * self.steps - 2 if distance == self.steps else self.slot(distance)
        if self.cut:
            part = self.x_part(self.target, shard, w.side)
            remote(part, part, self.sems.at[2], self.x_recv.at[slot], w.across).start()
        part = self.ring_part(self.target, shard)
        remote(part, part, self.sems.at[3], self.sems.at[0], w.twin).start()

    def crossed(self, distance):
        if not self.cut:
            return
        w = self.w
        shard = w.at(distance)
        slot = 2 * self.steps - 2 if distance == self.steps else self.slot(distance)
        part = self.x_part(self.target, shard, 1 - w.side)
        remote(part, part, self.sems.at[2], self.x_recv.at[slot], w.across).wait_recv()
        remote(part, part, self.sems.at[3], self.sems.at[0], w.twin).start()

    def whole(self):
        part = self.target.at[pl.ds(0, (self.w.n - 1) * self.rows), pl.ds(0, self.half)]
        remote(part, part, self.sems.at[3], self.sems.at[0], self.w.twin).wait_recv()
        pltpu.make_async_copy(
            self.source, self.target.at[self.rows_at(self.w.dp, 0, self.rows), :], self.sems.at[4]
        ).wait()

    def drain(self):
        count = self.w.n - 1
        for sem, rows in ((1, self.rows - self.cut), (2, self.cut), (3, self.rows)):
            if rows:
                part = self.target.at[pl.ds(0, count * rows), pl.ds(0, self.half)]
                remote(part, part, self.sems.at[sem], self.sems.at[sem], self.w.twin).wait_send()

    def begin(self):
        self.own()
        self.hop(-1, True)
        self.hop(1, True)

    def distances(self, named):
        sign, last = (1 if named > 0 else -1), self.steps
        if abs(named) == 2:
            return [sign * d for d in range(2, last - 1)]
        return [sign * (abs(named) if abs(named) < 2 else last + abs(named) - 4)]

    def take(self, distance):
        if distance == self.steps:
            self.arrived(distance)
            self.spread(distance)
        elif distance == self.steps - 1:
            self.arrived(-distance)
            self.arrived(distance)
            self.hop(self.steps, False)
            self.spread(-distance)
            self.spread(distance)
        else:
            self.arrived(distance)
            self.hop(distance + (1 if distance > 0 else -1), False)
            self.spread(distance)


class Pair:
    def __init__(self, where, grads, held, rows, send, recv):
        self.w, self.grads, self.held, self.rows = where, grads, held, rows
        self.half = grads.shape[1] // 2
        self.copy = remote(self.grads.at[:, self.lanes(1 - where.core)], held, send.at[0], recv.at[0], where.twin)

    def lanes(self, core):
        return pl.ds(pl.multiple_of(core * self.half, 128), self.half)

    def give(self):
        self.copy.start()

    def add(self):
        self.copy.wait_recv()

        def body(i, _):
            at = pl.ds(pl.multiple_of(i * self.rows, TILE), self.rows)
            self.held[at, :] = (
                self.held[at, :].astype(F32) + self.grads[at, self.lanes(self.w.core)].astype(F32)
            ).astype(BF)
            return 0

        lax.fori_loop(0, self.w.n, body, 0)

    def drain(self):
        self.copy.wait_send()


class Chain:
    def __init__(self, pair, out, crossed, bufs, send, recv, share):
        self.pair, self.w, self.out, self.crossed = pair, pair.w, out, crossed
        self.cut = x_rows(pair.rows, share)
        self.size = self.cut if crossed else pair.rows - 2 * self.cut
        self.depth = self.w.n // 2 - 1
        self.xbuf, self.rbuf = bufs
        self.send, self.recv = send, recv
        self.stages = self.depth + 5

    def first(self, side):
        return side * (self.pair.rows - self.cut) if self.crossed else self.cut

    def rows_at(self, shard, side=None):
        base = shard * self.pair.rows + self.first(self.w.side if side is None else side)
        return pl.ds(pl.multiple_of(base, TILE), self.size)

    def out_at(self, side=None):
        at = pl.ds(pl.multiple_of(self.first(self.w.side if side is None else side), TILE), self.size)
        return self.out.at[at, self.pair.lanes(self.w.core)]

    def got(self, sem, dst):
        remote(dst, dst, self.send.at[0], self.recv.at[sem], self.w.twin).wait_recv()

    def ring(self, slot, src, device):
        remote(src, self.rbuf.at[slot], self.send.at[1], self.recv.at[slot], device).start()

    def stage(self, s):
        if not self.size:
            return
        w, n, depth, held = self.w, self.w.n, self.depth, self.pair.held
        last = 2 * depth + 1
        if s == 0:
            if self.crossed:
                for i in range(n):
                    remote(
                        held.at[self.rows_at(i, 1 - w.side), :], self.xbuf.at[i], self.send.at[0], self.recv.at[last],
                        w.across,
                    ).start()
        elif s == 1:
            if self.crossed:
                self.got(last, self.xbuf)

                def body(i, _):
                    at = self.rows_at(i)
                    held[at, :] = (held[at, :].astype(F32) + self.xbuf[i].astype(F32)).astype(BF)
                    return 0

                lax.fori_loop(0, n, body, 0)
            dest = w.at((2 * w.core - 1) * (depth + 1))
            self.ring(2 * depth, held.at[self.rows_at(dest), :], w.far_back)
        elif s < 2 + depth:
            hop = s - 2
            for way in (0, 1):
                sign = 1 - 2 * way
                own = held[self.rows_at(w.at(sign * (depth - hop))), :].astype(F32)
                slot = 2 * hop + way
                if hop == 0:
                    if way == 0:
                        self.got(2 * depth, self.rbuf.at[2 * depth])
                    far = self.rbuf[2 * depth].astype(F32)
                    pick = w.core if way == 0 else 1 - w.core
                    own = own + jnp.where(pick == 1, far, 0.0)
                    at = 2 * depth + 1 + way
                else:
                    at = slot - 2
                    self.got(at, self.rbuf.at[at])
                    own = own + self.rbuf[at].astype(F32)
                self.rbuf[at] = own.astype(BF)
                self.ring(slot, self.rbuf.at[at], w.right if way == 0 else w.left)
        elif s == 2 + depth:
            total = held[self.rows_at(w.dp), :].astype(F32)
            for way in (0, 1):
                at = 2 * depth - 2 + way
                self.got(at, self.rbuf.at[at])
                total = total + self.rbuf[at].astype(F32)
            if self.crossed:
                mine = self.out_at()
                mine[...] = total.astype(BF)
                remote(mine, mine, self.send.at[2], self.recv.at[last + 1], w.across).start()
                remote(mine, mine, self.send.at[3], self.recv.at[last + 2], w.twin).start()
            else:
                self.xbuf[0] = total.astype(BF)
                remote(self.xbuf.at[0], self.xbuf.at[1], self.send.at[2], self.recv.at[last + 1], w.across).start()
        elif s == 3 + depth:
            if self.crossed:
                other = self.out_at(1 - w.side)
                self.got(last + 1, other)
                remote(other, other, self.send.at[4], self.recv.at[last + 3], w.twin).start()
            else:
                self.got(last + 1, self.xbuf.at[1])
                mine = self.out_at()
                mine[...] = (self.xbuf[0].astype(F32) + self.xbuf[1].astype(F32)).astype(BF)
                remote(mine, mine, self.send.at[3], self.recv.at[last + 2], w.twin).start()
        elif s == 4 + depth:
            part = self.out_at()
            self.got(last + 2, part)
            if self.crossed:
                self.got(last + 3, part)

    def drain(self):
        if not self.size:
            return
        ring = self.rbuf.at[pl.ds(0, 2 * self.depth + 1)]
        remote(ring, ring, self.send.at[1], self.recv.at[0], self.w.twin).wait_send()
        part = self.out_at()
        remote(part, part, self.send.at[2], self.recv.at[0], self.w.twin).wait_send()
        remote(part, part, self.send.at[3], self.recv.at[0], self.w.twin).wait_send()
        if self.crossed:
            remote(part, part, self.send.at[4], self.recv.at[0], self.w.twin).wait_send()
            remote(self.xbuf, self.xbuf, self.send.at[0], self.recv.at[0], self.w.twin).wait_send()


def scatter_scratch(n, rows, width, share):
    half, cut, depth = width // 2, x_rows(rows, share), n // 2 - 1
    out = [pltpu.VMEM((n * rows, half), BF)]
    for count, size in ((2, rows - 2 * cut), (n, cut)):
        out += [pltpu.VMEM((count, max(size, TILE), half), BF), pltpu.VMEM((2 * depth + 3, max(size, TILE), half), BF)]
    return out


def scatter_sems(n, k):
    return [pltpu.SemaphoreType.DMA((k, 11)), pltpu.SemaphoreType.DMA((k, 2 * n + 8))]


class Scatter:
    def __init__(self, where, grads, out, rows, bufs, send, recv, share):
        n = where.n
        self.pair = Pair(where, grads, bufs[0], rows, send.at[pl.ds(10, 1)], recv.at[pl.ds(2 * n + 7, 1)])
        self.straight = Chain(self.pair, out, False, bufs[1:3], send.at[pl.ds(0, 5)], recv.at[pl.ds(0, n + 2)], share)
        self.crossed = Chain(self.pair, out, True, bufs[3:5], send.at[pl.ds(5, 5)], recv.at[pl.ds(n + 2, n + 3)], share)

    def drain(self):
        for part in (self.pair, self.straight, self.crossed):
            part.drain()


def sum_up(parts, work, order):
    depth = parts[0].straight.depth
    for what, g, stage in order:
        part = parts[g]
        if what == 0:
            work(g)
            part.pair.give()
        elif what == 1:
            part.pair.add()
        else:
            chain = part.straight if what == 2 else part.crossed
            stages = [stage] if stage < 4 else range(4, depth + 2) if stage == 4 else [stage + depth - 3]
            for s in stages:
                chain.stage(s)
    for part in parts:
        part.drain()


LOW = -100000.0
TOK = 1024
KINDS = 7
BIAS_LANE = 6


def mm(a, b):
    return lax.dot_general(a, b, (((1,), (0,)), ((), ())), preferred_element_type=F32)


def mm_t(a, b):
    return lax.dot_general(a, b, (((1,), (1,)), ((), ())), preferred_element_type=F32)


def t_mm(a, b):
    return lax.dot_general(a, b, (((0,), (0,)), ((), ())), preferred_element_type=F32)


def lane_ids(shape):
    return lax.broadcasted_iota(jnp.int32, shape, len(shape) - 1)


def row_ids(shape):
    return lax.broadcasted_iota(jnp.int32, shape, 0)


def seg_of(t, ends):
    return sum((t >= e).astype(jnp.int32) for e in ends[:-1])


def pick(seg, values):
    out = values[0]
    for s in range(1, len(values)):
        out = jnp.where(seg == s, values[s], out)
    return out


def scalar_ends(lengths, r, segs):
    ends, total = [], 0
    for s in range(segs):
        total = total + lengths[s, r]
        ends.append(total)
    return ends


def lse_of(terms):
    top = functools.reduce(jnp.maximum, terms)
    return top, functools.reduce(jnp.add, [jnp.exp(v - top) for v in terms])


def lattice(lengths, counts, terms, skewed, hist, grads, loss, dims):
    frames, rows, segs, own_u, labs = dims
    wide = (frames, 128)
    lane = lane_ids(wide)
    group = rows * own_u
    j, row, u = lane % own_u, (lane % group) // own_u, (lane // group) * own_u + lane % own_u
    t = row_ids(wide)
    all_ends = [scalar_ends(lengths, r, segs) for r in range(rows)]

    def per_lane(values):
        out = jnp.zeros(wide, jnp.int32)
        for r in range(rows):
            out = jnp.where(row == r, values[r], out)
        return out

    ends = [per_lane([all_ends[r][s] for r in range(rows)]) for s in range(segs)]
    labels_in = [per_lane([counts[s, r] for r in range(rows)]) for s in range(segs)]
    seg = seg_of(t, ends)
    stop = pick(seg, ends)
    begin = pick(seg, [jnp.zeros(wide, jnp.int32)] + ends[:-1])
    target = pick(seg, labels_in)
    remain, first = stop - t, t == begin

    kinds = []
    per_vreg = 128 // group
    for k in range(KINDS):
        value = None
        for dev in range(labs):
            part = terms[dev, :, (k // per_vreg) * 128 : (k // per_vreg) * 128 + 128]
            shift = (dev - k % per_vreg) * group % 128
            part = pltpu.roll(part, shift, 1) if shift else part
            value = part if value is None else jnp.where(lane // group == dev, part, value)
        kinds.append(value)
    blank_lp, durs, label_lp = kinds[0], kinds[1:6], kinds[6]
    last_u = own_u * labs - 1
    emit, blank, blank_raw = [], [None], [None]
    for d in range(5):
        ok = (u < last_u) & (d <= remain - 1)
        emit.append(jnp.where(ok, label_lp + durs[d], LOW))
        if d:
            blank_raw.append(blank_lp + durs[d])
            blank.append(jnp.where(d <= remain - 1, blank_raw[d], LOW))
    final = (u == target) & (remain <= 4)
    closing = jnp.zeros(wide, F32)
    for d in range(1, 5):
        closing = jnp.where(remain == d, blank_raw[d], closing)
    closing = jnp.where(final, closing, LOW)
    start = jnp.where(first & (u == 0), 0.0, LOW)

    tall = frames + 16
    tall_u = (lane_ids((tall, 128)) // group) * own_u + lane_ids((tall, 128)) % own_u
    tall_j = lane_ids((tall, 128)) % own_u
    pad = jnp.full((16, 128), LOW, F32)

    def skew(value):
        value = jnp.concatenate([value, pad], axis=0)
        for bit in (1, 2, 4, 8):
            value = jnp.where((tall_u // bit) % 2 == 1, pltpu.roll(value, bit, 0), value)
        return value

    def unskew(value):
        for bit in (1, 2, 4, 8):
            value = jnp.where((tall_u // bit) % 2 == 1, pltpu.roll(value, tall - bit, 0), value)
        return value[:frames]

    up = 128 - (group - own_u + 1)

    def next_up(value, jj):
        return jnp.where(jj == 0, pltpu.roll(value, group - own_u + 1, 1), pltpu.roll(value, 1, 1))

    def next_down(value, jj):
        return jnp.where(jj == own_u - 1, pltpu.roll(value, up, 1), pltpu.roll(value, 127, 1))

    lead = jnp.full((8, 128), LOW, F32)

    def keep(i, value):
        skewed[i, 0:8, :] = lead
        skewed[i, 8 : 8 + tall, :] = value

    for d in range(1, 5):
        keep(d - 1, skew(blank[d]))
    for d in range(5):
        value = skew(emit[d])
        keep(4 + d, value)
        keep(9 + d, next_up(value, tall_j))
    keep(14, skew(start))
    keep(15, skew(closing))
    waves = frames + last_u + 1
    one_j = lane_ids((1, 128)) % own_u
    low_row = skewed[0, 0:1, :]

    def at(i, w):
        return skewed[i, pl.ds(w + 8, 1), :]

    def combine(old, near):
        top_old, sum_old = lse_of(old)
        top = functools.reduce(jnp.maximum, near, top_old)
        total = sum_old * jnp.exp(top_old - top)
        for v in near:
            total = total + jnp.exp(v - top)
        return top + jnp.log(total)

    def wave(i, carry):
        a, ra, b, rb = carry
        old = [at(14, i)]
        for d in range(2, 5):
            old.append(a[d - 1] + at(d - 1, i - d))
        for d in range(2, 6):
            old.append(ra[d - 1] + at(8 + d, i - d))
        new_a = combine(old, [a[0] + at(0, i - 1), ra[0] + at(9, i - 1)])
        back = waves - 1 - i
        old = [at(15, back)]
        for d in range(2, 5):
            old.append(b[d - 1] + at(d - 1, back))
        for d in range(2, 6):
            old.append(rb[d - 1] + at(3 + d, back))
        new_b = combine(old, [b[0] + at(0, back), rb[0] + at(4, back)])
        hist[0, pl.ds(i, 1), :] = new_a
        hist[1, pl.ds(back, 1), :] = new_b
        return (
            (new_a,) + a[:-1],
            (next_up(new_a, one_j),) + ra[:-1],
            (new_b,) + b[:-1],
            (next_down(new_b, one_j),) + rb[:-1],
        )

    hist[...] = jnp.full(hist.shape, LOW, F32)
    lax.fori_loop(
        0, waves, wave, ((low_row,) * 4, (low_row,) * 5, (low_row,) * 4, (low_row,) * 5), unroll=UNROLL
    )
    alpha, beta = unskew(hist[0]), unskew(hist[1])
    ahead = next_down(beta, j)
    norm = jnp.zeros(wide, F32)
    heads = jnp.where(first & (u == 0), beta, 0.0)
    for s in range(segs):
        value = jnp.sum(jnp.where(seg == s, heads, 0.0), axis=0, keepdims=True)
        step = 1
        while step < own_u:
            value = value + pltpu.roll(value, step, 1)
            step *= 2
        step = group
        while step < 128:
            value = value + pltpu.roll(value, step, 1)
            step *= 2
        norm = jnp.where(seg == s, value, norm)
        length = ends[s] - (ends[s - 1] if s else 0)
        loss[pl.ds(s, 1), :] = -value / length[:1].astype(F32)
    base = alpha - norm
    total_a, total_b = None, None
    for d in range(5):
        there = pltpu.roll(ahead, frames - d, 0) if d else ahead
        g = -jnp.exp(base + emit[d] + there)
        total_a = g if d == 0 else total_a + g
        if d:
            gb = -jnp.exp(base + blank[d] + pltpu.roll(beta, frames - d, 0))
            gb = gb - jnp.exp(jnp.where(final & (remain == d), base + blank_raw[d], LOW))
            total_b = gb if d == 1 else total_b + gb
            g = g + gb
        grads[1 + d] = g
    grads[0] = total_b
    grads[6] = total_a


def joint_scratch(dims, width):
    frames, rows, segs, own_u, labs = dims
    span, inner = own_u * frames, rows * segs * own_u
    return [
        pltpu.VMEM((inner, width), F32),
        pltpu.VMEM((rows, span, width + 128), BF),
        pltpu.VMEM((rows, span, width) if width <= ROOMY else (8, 128), BF),
        pltpu.VMEM((width + 128, VOCAB + 128), BF),
        pltpu.VMEM((VOCAB, width) if width <= ROOMY else (8, 128), BF),
        pltpu.VMEM((rows, span, VOCAB), BF),
        pltpu.VMEM((rows, span, 128), F32),
        pltpu.VMEM((16, frames + 24, 128), F32),
        pltpu.VMEM((2, frames + 16, 128), F32),
        pltpu.VMEM((KINDS, frames, 128), F32),
        pltpu.VMEM((inner, width), BF),
    ]


def joint_shared(dims, width):
    frames, rows, segs, own_u, labs = dims
    micro, inner = rows // labs, rows * segs * own_u
    return [
        pltpu.VMEM((micro, frames, width), BF),
        pltpu.VMEM((rows, frames, width), BF),
        pltpu.VMEM((inner, 640), F32),
        pltpu.VMEM((inner, 768), BF),
        pltpu.VMEM((frames, 256), F32),
        pltpu.VMEM((labs, frames, 256), F32),
        pltpu.VMEM((labs, micro, frames, width), BF),
        pltpu.VMEM((labs, micro, frames, width), BF),
        pltpu.VMEM((micro, frames, width), BF),
        pltpu.VMEM((width, 256), BF),
        pltpu.VMEM((16, 256), F32),
        pltpu.SemaphoreType.DMA((3, labs)),
        pltpu.SemaphoreType.DMA((3, labs)),
    ]


class Joint:
    def __init__(self, z, w, dims, predictor, lengths, counts, labels, bias_out, g_predictor, g_pack, loss, shared):
        self.z, self.w, self.dims = z, w, dims
        self.predictor, self.lengths, self.counts, self.labels = predictor, lengths, counts, labels
        self.bias_out, self.g_predictor, self.g_pack, self.loss = bias_out, g_predictor, g_pack, loss
        (
            self.enc_own, self.enc_all, self.pred_wide, self.pred, self.mine, self.terms, self.part, self.came,
            self.g_enc, self.g_mix, self.g_bias, self.send, self.recv,
        ) = shared
        self.micro = dims[1] // dims[4]

    def owner(self, j):
        return ((self.w.side + j // 2) % 2) * 2 + (self.w.core + j % 2) % 2

    def device(self, j):
        return (self.w.dp, self.owner(j))

    def enc_copy(self, j, source):
        to = self.enc_all.at[pl.ds(source * self.micro, self.micro)]
        return remote(self.enc_own, to, self.send.at[0, j], self.recv.at[0, j], self.device(j))

    def term_copy(self, j, source):
        return remote(self.mine, self.terms.at[source], self.send.at[1, j], self.recv.at[1, j], self.device(j))

    def part_copy(self, j):
        return remote(self.part.at[j], self.came.at[j], self.send.at[2, j], self.recv.at[2, j], self.device(j))

    def prepare(self):
        frames, rows, segs, own_u, labs = self.dims
        features = self.predictor.shape[-1]
        for r in range(rows):
            for s in range(segs):
                first = (r * segs + s) * own_u
                self.pred_wide[first : first + own_u, :] = self.predictor[r, s].astype(F32)
        self.pred[:, :features] = self.pred_wide[...].astype(BF)
        self.pred[:, features:] = (lane_ids((self.pred.shape[0], 128)) == BIAS_LANE).astype(BF)

    def hand_on(self):
        rows = self.enc_all.at[pl.ds(self.owner(2) * self.micro, self.micro)]
        return remote(rows, rows, self.send.at[0, 3], self.recv.at[0, 3], self.device(1))

    def share(self):
        for j in (1, 2):
            self.enc_copy(j, self.w.lab).start()
        self.enc_all[pl.ds(self.w.lab * self.micro, self.micro)] = self.enc_own[...]

    def drain(self):
        self.hand_on().wait_send()
        for j in range(1, self.dims[4]):
            if j < 3:
                self.enc_copy(j, self.w.lab).wait_send()
            self.term_copy(j, self.w.lab).wait_send()
            self.part_copy(j).wait_send()

    def run(self, full, *scratch):
        joint_run(self, full, *scratch)


def joint_run(
    job, full, proj, hid, slope, wide, back_w, prob, prob_tail, skewed, hist, grads, g_pred
):
    z, dims, lengths, counts, labels, bias_out = job.z, job.dims, job.lengths, job.counts, job.labels, job.bias_out
    frames, rows, segs, own_u, labs = dims
    micro = rows // labs
    bias_out = bias_out[...].astype(F32).reshape(1, -1)
    n, width, span, features = z.n, z.n * z.jr, own_u * frames, job.predictor.shape[-1]
    pred, mine, terms, enc_all, part, came = job.pred, job.mine, job.terms, job.enc_all, job.part, job.came
    enc_copy, term_copy, part_copy, owner = job.enc_copy, job.term_copy, job.part_copy, job.owner
    g_predictor, g_pack, g_mix, g_bias, g_enc, loss = (
        job.g_predictor, job.g_pack, job.g_mix, job.g_bias, job.g_enc, job.loss
    )
    turn = STEP if width <= ROOMY else 1
    mixes = rows_of(full[0], n, 0, z.jr)
    proj[...] = mm_t(pred[:, :512], rows_of(full[3], n, 0, z.jr)) + mm_t(pred[:, 512:], mixes[:, :256])
    wide[:width, :512] = rows_of(full[3], n, z.jr, z.jr)
    wide[:width, 512:TOK] = rows_of(full[3], n, 2 * z.jr, z.jr)
    wide[:width, TOK:VOCAB] = mixes[:, 128:256]
    top_row = row_ids((128, TOK)) == 0
    wide[width:, :TOK] = jnp.where(top_row, bias_out[:, :TOK].astype(F32), 0.0).astype(BF)
    mine[:, :128] = jnp.zeros((frames, 128), F32)
    mine[:1, : bias_out.shape[1] - TOK] = bias_out[:, TOK:].astype(F32)
    wide[width:, TOK:VOCAB] = jnp.where(row_ids((128, 128)) == 0, mine[:1, :128], 0.0).astype(BF)
    lane_1 = lane_ids((1, 128))
    wanted = jnp.zeros((1, 128), jnp.int32)
    for r in range(rows):
        for s in range(segs):
            for u in range(own_u):
                wanted = jnp.where(lane_1 == (r * segs + s) * own_u + u, labels[s, u, r], wanted)
    wide[:, VOCAB:] = mm(wide[:, :TOK], (row_ids((TOK, 128)) == wanted).astype(BF)).astype(BF)
    roomy = width <= ROOMY
    if roomy:
        back_w[...] = wide[:width, :VOCAB].astype(F32).T.astype(BF)
    hid[:, :, width:] = (lane_ids((rows, span, 128)) == 0).astype(BF)
    lane_t = lane_ids((frames, 128))
    lane_w = lane_ids((frames, TOK))
    group = rows * own_u
    per_vreg = 128 // group

    def row_of(k):
        return owner(k // micro) * micro + k % micro

    def forward(k):
        r = row_of(k)
        ends = scalar_ends(lengths, r, segs)
        seg = seg_of(row_ids((frames, width)), ends)
        enc = enc_all[r].astype(F32)
        for u in range(own_u):
            at = slice(u * frames, (u + 1) * frames)
            per_frame = pick(
                seg, [proj[pl.ds(r * segs * own_u + s * own_u + u, 1), :] for s in range(segs)]
            )
            value = jnp.tanh(enc + per_frame)
            hid[r, at, :width] = value.astype(BF)
            if roomy:
                slope[r, at, :] = (1.0 - value * value).astype(BF)
        logits = mm(hid[r], wide[...])
        seg_l = seg_of(row_ids((frames, 128)), ends)
        for u in range(own_u):
            at = slice(u * frames, (u + 1) * frames)
            logit, last, named = logits[at, :TOK], logits[at, TOK:VOCAB], logits[at, VOCAB:]
            top = jnp.maximum(jnp.max(logit, axis=1, keepdims=True), last[:, 0:1])
            top_dur = jnp.max(
                jnp.where((lane_t >= 1) & (lane_t <= 5), last, -jnp.inf), axis=1, keepdims=True
            )
            is_tok = lane_t == 0
            e_last = jnp.where(
                lane_t < 6, jnp.exp(jnp.where(lane_t < 6, last - jnp.where(is_tok, top, top_dur), 0.0)), 0.0
            )
            e = jnp.exp(logit - top)
            total = jnp.sum(e, axis=1, keepdims=True) + e_last[:, 0:1]
            total_dur = jnp.sum(jnp.where(is_tok, 0.0, e_last), axis=1, keepdims=True)
            prob[r, at, :TOK] = e.astype(BF)
            over = 1.0 / total
            prob_tail[r, at, :] = jnp.where(lane_t == 6, over, e_last * jnp.where(is_tok, over, 1.0 / total_dur))
            norm_tok, norm_dur = top + jnp.log(total), top_dur + jnp.log(total_dur)
            column = r * segs * own_u + seg_l * own_u + u
            at_label = jnp.sum(jnp.where(lane_t == column, named, 0.0), axis=1, keepdims=True) - norm_tok
            lp = last - jnp.where(is_tok, norm_tok, norm_dur)
            for half in range(2):
                cols = slice(half * 128, half * 128 + 128)
                value = mine[:, cols]
                for kind in range(half * per_vreg, min(KINDS, (half + 1) * per_vreg)):
                    column = at_label if kind == 6 else lp[:, kind : kind + 1]
                    value = jnp.where(lane_t == (kind % per_vreg) * group + r * own_u + u, column, value)
                mine[:, cols] = value

    mine[...] = jnp.zeros(mine.shape, F32)

    def forward_step(i, _):
        for j in range(1, labs):
            @pl.when(i * turn == j * micro)
            def _():
                enc_copy(j, owner(j)).wait_recv()
                if j == 2:
                    job.hand_on().start()
        for k in range(turn):
            forward(i * turn + k)
        return 0

    lax.fori_loop(0, rows // turn, forward_step, 0)
    terms[job.w.lab] = mine[...]

    for j in range(1, labs):
        term_copy(j, job.w.lab).start()
    for j in range(1, labs):
        term_copy(j, owner(j)).wait_recv()
    lattice(lengths, counts, terms, skewed, hist, grads, loss, dims)

    def backward(k):
        r = row_of(k)
        ends = scalar_ends(lengths, r, segs)
        shift = (256 - job.w.lab * group - r * own_u) % 128
        rolled = [pltpu.roll(grads[kind], shift, 1) for kind in range(KINDS)]
        seg_l = seg_of(row_ids((frames, TOK)), ends)
        for u in range(own_u):
            at = slice(u * frames, (u + 1) * frames)
            a, b = rolled[6][:, u : u + 1], rolled[0][:, u : u + 1]
            both = a + b
            label = pick(seg_l, [labels[s, u, r] for s in range(segs)])
            tails = prob_tail[r, at, :]
            scaled = both * tails[:, 6:7]
            prob[r, at, :TOK] = (jnp.where(lane_w == label, a, 0.0) - prob[r, at, :TOK].astype(F32) * scaled).astype(BF)
            aim = jnp.zeros((frames, 128), F32)
            for kind in range(6):
                aim = jnp.where(lane_t == kind, rolled[kind][:, u : u + 1], aim)
            prob[r, at, TOK:] = jnp.where(lane_t < 6, aim - tails * both, 0.0).astype(BF)
        if roomy:
            back = mm(prob[r], back_w[...]) * slope[r].astype(F32)
        else:
            value = hid[r, :, :width].astype(F32)
            back = mm_t(prob[r], wide[:width, :VOCAB]) * (1.0 - value * value)
        summed = back[:frames]
        for u in range(1, own_u):
            summed = summed + back[u * frames : (u + 1) * frames]
        part[k // micro, k % micro] = summed.astype(BF)
        shape = (segs * own_u, span)
        lanes = lane_ids(shape)
        seg_t = seg_of(lanes % frames, ends)
        hit = (row_ids(shape) == seg_t * own_u + lanes // frames).astype(BF)
        g_pred[pl.ds(r * segs * own_u, segs * own_u), :] = mm(hit, back.astype(BF)).astype(BF)

    def backward_step(i, _):
        first = rows - (i + 1) * turn
        for k in range(turn - 1, -1, -1):
            backward(first + k)
        for j in range(1, labs):
            @pl.when(first == j * micro)
            def _():
                part_copy(j).start()
        return 0

    lax.fori_loop(0, rows // turn, backward_step, 0)
    gp = g_pred[...]
    g_predictor[:, :512] = mm(gp, rows_of(full[3], n, 0, z.jr))
    g_predictor[:, 512:] = mm(gp, rows_of(full[0], n, 0, z.jr)[:, : features - 512])
    shards, block = n, z.jr
    h_all = hid[...].reshape(rows * span, width + 128)
    g_bias[...] = jnp.zeros(g_bias.shape, F32)
    from_pred = t_mm(gp, pred[...])
    for i in range(2):
        piece = t_mm(h_all, prob[:, :, i * 512 : i * 512 + 512].reshape(rows * span, 512))
        for q in range(2):
            g_bias[2 * i + q : 2 * i + q + 1, :] = piece[width : width + 1, 256 * q : 256 * q + 256]
        for d in range(shards):
            first = d * 3 * block + (i + 1) * block
            g_pack[first : first + block, :] = piece[d * block : (d + 1) * block].astype(BF)
    ends_w = t_mm(h_all, prob[:, :, TOK:].reshape(rows * span, 128))
    g_bias[4:5, :128] = ends_w[width : width + 1]
    ends_w = ends_w[:width] + from_pred[:, 640:768]
    for d in range(shards):
        at = slice(d * block, (d + 1) * block)
        g_pack[d * 3 * block : d * 3 * block + block, :] = from_pred[at, :512].astype(BF)
        g_mix[at, :128] = from_pred[at, 512:640].astype(BF)
        g_mix[at, 128:] = ends_w[at].astype(BF)
    for j in range(1, labs):
        part_copy(j).wait_recv()
    total = part[0].astype(F32)
    for j in range(1, labs):
        total = total + came[j].astype(F32)
    g_enc[...] = total.astype(BF)


VOCAB = TOK + 128
UNROLL = 8
STEP = 2
ROOMY = 768


HEADS = 8
EPS = 1e-05
TAPS = 9
GAIN_ROW = 9
STATE = (
    ("n_ffn", 512, F32), ("n_att", 512, F32), ("n_conv", 512, F32), ("n_depth", 512, F32), ("n_out", 512, F32),
    ("scales", 128, F32), ("act", 2048, BF), ("slope", 2048, BF), ("qkv", 1536, BF), ("context", 512, BF),
    ("value", 512, F32), ("gate", 512, F32),
)


def sigmoid(v):
    return 0.5 * jnp.tanh(0.5 * v) + 0.5


def norm_parts(v):
    c = v - jnp.mean(v, axis=1, keepdims=True)
    r = lax.rsqrt(jnp.mean(c * c, axis=1, keepdims=True) + EPS)
    return c * r, r


def norm_back(gy, n, r, gain):
    gg = gy * gain
    gain_grad = jnp.sum(gy * n, axis=0, keepdims=True)
    inner = gg - jnp.mean(gg, axis=1, keepdims=True) - n * jnp.mean(gg * n, axis=1, keepdims=True)
    return r * inner, gain_grad


def rows_of(ref, n, first, count):
    per = ref.shape[0] // n
    return jnp.concatenate([ref[d * per + first : d * per + first + count, :] for d in range(n)], axis=0)


def put_rows(ref, n, first, count, value):
    per = ref.shape[0] // n
    for d in range(n):
        ref[d * per + first : d * per + first + count, :] = value[d * count : (d + 1) * count].astype(ref.dtype)


def own_ends(ints, micro, segs):
    first = lax.axis_index("lab") * micro
    return [scalar_ends(ints, first + m, segs) for m in range(micro)]


def seg_id(position, ends, frames):
    t, row = position % frames, position // frames
    out = seg_of(t, ends[0])
    for m in range(1, len(ends)):
        out = jnp.where(row == m, seg_of(t, ends[m]), out)
    return out + row * len(ends[0])


def shifted(value, step):
    rows = value.shape[0]
    return pltpu.roll(value, (-step) % rows, 0) if step % rows else value


def assemble_small(target, n, per, ds):
    lane = lane_ids((16, 128))
    columns = [jnp.zeros((16, 128), F32) for _ in range(n * ds // 128)]
    for d in range(n):
        piece = jnp.where(lane < ds, target[d * per : d * per + 16, 256:384].astype(F32), 0.0)
        at = d * ds % 128
        columns[d * ds // 128] = columns[d * ds // 128] + (pltpu.roll(piece, at, 1) if at else piece)
    return jnp.concatenate(columns, axis=1)


def split_small(value, d, ds):
    at = d * ds % 128
    piece = value[:, d * ds // 128 * 128 : d * ds // 128 * 128 + 128]
    piece = pltpu.roll(piece, 128 - at, 1) if at else piece
    return jnp.where(lane_ids((16, 128)) < ds, piece, 0.0)


class Sizes:
    def __init__(self, n, ds, ff, qk, pi, jr):
        self.n, self.ds, self.ff, self.qk, self.pi, self.jr = n, ds, ff, qk, pi, jr
        self.rows = (jr + ff, ff + qk, 2 * ds + pi + jr, 3 * jr)
        self.model = n * ds


def head_pair(ref, block, pair):
    at = block * 512 + pair * 128
    return ref[:, at : at + 128]


def forward_pieces(z, x_ref, ints, dims, full, small_ref, st, probs, encoded, enc_proj):
    frames, rows, segs, own_u, labs = dims
    n, micro = z.n, rows // labs
    count = micro * frames
    ends = own_ends(ints, micro, segs)
    ids_r = seg_id(row_ids((count, 128)), ends, frames)
    ids_c = seg_id(lane_ids((count, count)), ends, frames)
    scale_lane = lane_ids((count, 128))

    def norm(v, name, which):
        nv, r = norm_parts(v)
        st[name][...] = nv
        st["scales"][...] = jnp.where(scale_lane == which, r, st["scales"][...])
        return nv * small_ref[GAIN_ROW + which : GAIN_ROW + which + 1, :]

    small_ref[...] = assemble_small(full[0], n, z.rows[0], z.ds)
    st["scales"][...] = jnp.zeros((count, 128), F32)
    x = x_ref[...].reshape(count, z.model).astype(F32)
    ffn_in = norm(x, "n_ffn", 0).astype(BF)
    half = n // 2
    per = z.rows[0]
    for part in range(2):
        w = jnp.concatenate(
            [full[0][d * per + z.jr : d * per + z.jr + z.ff, :] for d in range(part * half, part * half + half)], axis=0
        )
        pre = mm_t(ffn_in, w)
        sg = sigmoid(pre)
        at = slice(part * half * z.ff, (part + 1) * half * z.ff)
        st["act"][:, at] = (pre * sg).astype(BF)
        st["slope"][:, at] = (sg * (1.0 + pre * (1.0 - sg))).astype(BF)
        yield
    after_ffn = x + 0.5 * mm(st["act"][...], rows_of(full[1], n, 0, z.ff))
    att_in = norm(after_ffn, "n_att", 1).astype(BF)
    st["qkv"][...] = mm_t(att_in, rows_of(full[1], n, z.ff, z.qk)).astype(BF)
    yield
    same = ids_r == ids_c
    low_half = lane_ids((count, 128)) < 64
    for pair in range(HEADS // 2):
        q, k, v = (head_pair(st["qkv"], b, pair) for b in range(3))
        total = None
        for side in range(2):
            keep = low_half if side == 0 else ~low_half
            score = mm_t(jnp.where(keep, q, 0), k) * (64 ** -0.5)
            score = jnp.where(same, score, LOW)
            e = jnp.exp(score - jnp.max(score, axis=1, keepdims=True))
            p = (e * (1.0 / jnp.sum(e, axis=1, keepdims=True))).astype(BF)
            probs[2 * pair + side] = p
            part = mm(p, jnp.where(keep, v, 0))
            total = part if total is None else total + part
        st["context"][:, pair * 128 : pair * 128 + 128] = total.astype(BF)
    yield
    after_att = after_ffn + mm(st["context"][...], rows_of(full[2], n, 0, z.ds))
    conv_in = norm(after_att, "n_conv", 2).astype(BF)
    conv_pre = mm_t(conv_in, rows_of(full[2], n, z.ds, z.pi))
    st["value"][...] = conv_pre[:, : z.model]
    st["gate"][...] = sigmoid(conv_pre[:, z.model :])
    depth = []
    for c in range(z.model // 128):
        at = slice(c * 128, c * 128 + 128)
        gated = st["value"][:, at] * st["gate"][:, at]
        total = jnp.zeros((count, 128), F32)
        for j in range(TAPS):
            ok = shifted(ids_r, j - TAPS // 2) == ids_r
            total = total + jnp.where(ok, shifted(gated, j - TAPS // 2), 0.0) * small_ref[j : j + 1, at]
        depth.append(total)
    dn = norm(jnp.concatenate(depth, axis=1), "n_depth", 3)
    conv_act = (dn * sigmoid(dn)).astype(BF)
    after_conv = after_att + mm(conv_act, rows_of(full[2], n, z.ds + z.pi, z.ds))
    out = norm(after_conv, "n_out", 4).astype(BF)
    encoded[...] = out.reshape(encoded.shape)
    enc_proj[...] = mm_t(out, rows_of(full[2], n, 2 * z.ds + z.pi, z.jr)).astype(BF).reshape(enc_proj.shape)
    yield


def backward_pieces(z, g_enc, ints, dims, full, small_ref, st, probs, grads, small_grad, grad_frames):
    frames, rows, segs, own_u, labs = dims
    n, micro = z.n, rows // labs
    count = micro * frames
    ends = own_ends(ints, micro, segs)
    ids_r = seg_id(row_ids((count, 128)), ends, frames)

    def gain(which):
        return small_ref[GAIN_ROW + which : GAIN_ROW + which + 1, :]

    def back(gy, name, which):
        g, gain_grad = norm_back(gy, st[name][...], st["scales"][:, which : which + 1], gain(which))
        small_grad[GAIN_ROW + which : GAIN_ROW + which + 1, :] = gain_grad
        return g

    def normed(name, which):
        return (st[name][...] * gain(which)).astype(BF)

    small_grad[...] = jnp.zeros(small_grad.shape, F32)
    ge = g_enc[...].reshape(count, -1)
    off = 2 * z.ds + z.pi
    put_rows(grads[2], n, off, z.jr, t_mm(ge, normed("n_out", 4)))
    g_conv_sum = back(mm(ge, rows_of(full[2], n, off, z.jr)), "n_out", 4)
    branch = g_conv_sum.astype(BF)
    dn = st["n_depth"][...] * gain(3)
    sg = sigmoid(dn)
    put_rows(grads[2], n, z.ds + z.pi, z.ds, t_mm((dn * sg).astype(BF), branch))
    g_act = mm_t(branch, rows_of(full[2], n, z.ds + z.pi, z.ds))
    g_depth = back(g_act * (sg * (1.0 + dn * (1.0 - sg))), "n_depth", 3)
    yield
    low_a, low_b = [], []
    for c in range(z.model // 128):
        at = slice(c * 128, c * 128 + 128)
        value, gate = st["value"][:, at], st["gate"][:, at]
        gated, gd = value * gate, g_depth[:, at]
        total = jnp.zeros((count, 128), F32)
        for j in range(TAPS):
            step = j - TAPS // 2
            ok = shifted(ids_r, step) == ids_r
            small_grad[j : j + 1, at] = jnp.sum(jnp.where(ok, shifted(gated, step), 0.0) * gd, axis=0, keepdims=True)
            ok = shifted(ids_r, -step) == ids_r
            total = total + jnp.where(ok, shifted(gd, -step), 0.0) * small_ref[j : j + 1, at]
        low_a.append((total * gate).astype(BF))
        low_b.append((total * value * gate * (1.0 - gate)).astype(BF))
    low = jnp.concatenate(low_a + low_b, axis=1)
    put_rows(grads[2], n, z.ds, z.pi, t_mm(low, normed("n_conv", 2)))
    g_att_sum = g_conv_sum + back(mm(low, rows_of(full[2], n, z.ds, z.pi)), "n_conv", 2)
    branch = g_att_sum.astype(BF)
    put_rows(grads[2], n, 0, z.ds, t_mm(st["context"][...], branch))
    g_context = mm_t(branch, rows_of(full[2], n, 0, z.ds)).astype(BF)
    yield
    low_half = lane_ids((count, 128)) < 64
    columns = [[], [], []]
    for pair in range(HEADS // 2):
        q, k, v = (head_pair(st["qkv"], b, pair) for b in range(3))
        gc = g_context[:, pair * 128 : pair * 128 + 128]
        sums = [None, None, None]
        for side in range(2):
            keep = low_half if side == 0 else ~low_half
            p = probs[2 * pair + side]
            gc_h = jnp.where(keep, gc, 0)
            gp = mm_t(gc_h, v)
            pf = p.astype(F32)
            gs = (pf * (gp - jnp.sum(gp * pf, axis=1, keepdims=True))).astype(BF)
            parts = (
                mm(gs, jnp.where(keep, k, 0)) * (64 ** -0.5),
                t_mm(gs, jnp.where(keep, q, 0)) * (64 ** -0.5),
                t_mm(p, gc_h),
            )
            sums = [b if a is None else a + b for a, b in zip(sums, parts)]
        for b in range(3):
            columns[b].append(sums[b].astype(BF))
    g_qkv = jnp.concatenate(columns[0] + columns[1] + columns[2], axis=1)
    yield
    put_rows(grads[1], n, z.ff, z.qk, t_mm(g_qkv, normed("n_att", 1)))
    g_ffn_sum = g_att_sum + back(mm(g_qkv, rows_of(full[1], n, z.ff, z.qk)), "n_att", 1)
    branch = (0.5 * g_ffn_sum).astype(BF)
    put_rows(grads[1], n, 0, z.ff, t_mm(st["act"][...], branch))
    yield
    g_pre = (mm_t(branch, rows_of(full[1], n, 0, z.ff)) * st["slope"][...].astype(F32)).astype(BF)
    put_rows(grads[0], n, z.jr, z.ff, t_mm(g_pre, normed("n_ffn", 0)))
    gx = g_ffn_sum + back(mm(g_pre, rows_of(full[0], n, z.jr, z.ff)), "n_ffn", 0)
    grad_frames[...] = gx.reshape(grad_frames.shape)
    yield


GATHER_SHARES = (0.4, 0.4, 0.2, 0.4)
ORDER = (
    (0, 0, 0), (0, 1, 0), (0, 2, 0), (0, 3, 0), (1, 0, -1), (1, 0, 1), (1, 1, 1), (2, 0, -1), (1, 1, -1), (2, 0, 1),
    (1, 2, -1), (1, 2, 1), (1, 3, 1), (2, 1, 1), (1, 3, -1), (1, 0, 2), (1, 0, -2), (2, 1, -1), (2, 3, 1),
    (2, 3, -1), (1, 1, -2), (2, 0, 2), (1, 1, 2), (2, 0, -2), (1, 2, -2), (1, 2, 2), (1, 3, -2), (1, 3, 2),
    (2, 1, -2), (2, 2, -1), (2, 2, 1), (1, 0, 3), (2, 1, 2), (2, 2, 2), (2, 2, -2), (2, 3, -2), (1, 1, 3),
    (2, 0, -3), (2, 3, 2), (1, 2, 3), (2, 0, 3), (2, 1, -3), (1, 0, 4), (2, 1, 3), (2, 2, -3), (1, 1, 4), (1, 2, 4),
    (2, 0, 4), (1, 3, 3), (2, 2, 3), (2, 1, 4), (3, 0, 0), (4, 0, 0), (1, 3, 4), (4, 1, 0), (2, 2, 4), (2, 3, -3),
    (2, 3, 3), (3, 1, 0), (4, 2, 0), (2, 3, 4), (3, 2, 0), (4, 3, 0), (4, 4, 0), (3, 3, 0),
)


def pass_kernel(
    z, dims, x_ref, lengths, counts, labels, w_in, w_out, w_qkv, w_att, w_pin, w_pout, w_enc, w_pred, w_joint,
    bias_joint, w_depth, gain0, gain1, gain2, gain3, gain4, predictor, bias_out,
    own0, own1, own2, own3, grad_frames, encoded, loss, g_predictor, *rest,
):
    k = len(STATE)
    st = {name: ref for (name, _, _), ref in zip(STATE, rest[:k])}
    probs, small_in, tail, small_ref, small_grad, g_pack = rest[k : k + 6]
    rest = rest[k + 6 :]
    sources, full, bufs, rest = rest[:4], rest[4:8], rest[8:28], rest[28:]
    shared, (ring_recv, x_recv, sems, send, recv) = rest[:-5], rest[-5:]
    n = z.n
    w = Where(n)
    jr, js, ds = z.jr, w_pred.shape[0], z.ds
    job = Joint(z, w, dims, predictor, lengths, counts, labels, bias_out, g_predictor, g_pack, loss, shared)
    small_in[...] = jnp.zeros(small_in.shape, F32)
    small_in[:TAPS, :ds] = w_depth[...].astype(F32)
    for i, gain in enumerate((gain0, gain1, gain2, gain3, gain4)):
        small_in[GAIN_ROW + i : GAIN_ROW + i + 1, :ds] = gain[...].astype(F32)
    tail[...] = jnp.zeros(tail.shape, F32)
    tail[:1, :js] = bias_joint[...].astype(F32)
    column = tail[:8, :].T[:jr, :1]
    tail[:8, :] = jnp.zeros((8, 128), F32)
    tail[:js, : w_joint.shape[1] - 1024] = w_joint[:, 1024:].astype(F32)
    tail[...] = jnp.where(lane_ids((jr, 128)) == BIAS_LANE, column, tail[...])

    def down(value, count):
        rows = value.shape[0]
        return jnp.concatenate([value, jnp.zeros((count - rows,) + value.shape[1:], value.dtype)], 0) if count > rows else value

    pred_t = down(w_pred[...], jr)

    def fill(g):
        if g == 0:
            sources[0][jr:, :] = w_in[...].astype(F32).T.astype(BF)
            sources[0][:jr, 0:128] = pred_t[:, 512:]
            sources[0][:jr, 128:256] = tail[...].astype(BF)
            sources[0][:jr, 256:] = jnp.zeros((jr, 256), BF)
            sources[0][:16, 256:384] = small_in[...].astype(BF)
        elif g == 1:
            sources[1][: z.ff, :] = w_out[...]
            sources[1][z.ff :, :] = w_qkv[...]
        elif g == 2:
            sources[2][:ds, :] = w_att[...]
            sources[2][ds : ds + z.pi, :] = w_pin[...].astype(F32).T.astype(BF)
            sources[2][ds + z.pi : 2 * ds + z.pi, :] = w_pout[...]
            sources[2][2 * ds + z.pi :, :] = down(w_enc[...], jr)
        elif g == 3:
            sources[3][:jr, :] = pred_t[:, :512]
            sources[3][jr : 2 * jr, :] = down(w_joint[:, :512], jr)
            sources[3][2 * jr :, :] = down(w_joint[:, 512:1024], jr)

    parts = [
        Gather(w, sources[i], full[i], z.rows[i], ring_recv.at[i], x_recv.at[i], sems.at[i], GATHER_SHARES[i])
        for i in range(4)
    ]
    fill(0)
    w.greet()
    compute = forward_pieces(z, x_ref, lengths, dims, full, small_ref, st, probs, encoded, job.enc_own)
    for what, g, distance in ORDER:
        if what == 0:
            if g:
                fill(g)
            parts[g].begin()
            if g == 3:
                job.prepare()
        elif what == 3:
            parts[g].whole()
        elif what == 4:
            next(compute)
            if g == 4:
                job.share()
        else:
            for d in parts[g].distances(distance):
                (parts[g].take if what == 1 else parts[g].crossed)(d)
    pl.run_scoped(lambda *scratch: job.run(full, *scratch), *joint_scratch(dims, n * jr))
    outs = (own0, own1, own2, own3)

    def finish(*grads):
        packs = list(grads) + [g_pack]
        sums = [
            Scatter(w, packs[g], outs[g], z.rows[g], bufs[5 * g : 5 * g + 5], send.at[g], recv.at[g], SHARES[3 - g])
            for g in (3, 2, 1, 0)
        ]
        pieces = backward_pieces(
            z, job.g_enc, lengths, dims, full, small_ref, st, probs, packs, small_grad, grad_frames
        )

        def work(i):
            for _ in range((0, 2, 2, 1)[i]):
                next(pieces)
            if i == 3:
                for d in range(n):
                    at = d * z.rows[0]
                    packs[0][at : at + jr, :256] = job.g_mix[d * jr : (d + 1) * jr, :]
                    if jr > 32:
                        packs[0][at + 32 : at + jr, 256:] = jnp.zeros((jr - 32, 256), BF)
                    packs[0][at : at + 16, 256:384] = split_small(small_grad[...], d, ds).astype(BF)
                    packs[0][at : at + 16, 384:] = jnp.zeros((16, 128), BF)
                    packs[0][at + 16 : at + 32, 256:] = job.g_bias[...].astype(BF)

        sum_up(sums, work, ORDER_SUMS)

    pl.run_scoped(finish, *[pltpu.VMEM((n * z.rows[g], 512), BF) for g in range(3)])
    job.drain()
    for part in parts:
        part.drain()


def pass_call(z, dims, x, ints, params, predictor, bias_out):
    frames, rows, segs, own_u, labs = dims
    n, micro = z.n, rows // labs
    count, width = micro * frames, n * z.jr
    vm, sm = (pl.BlockSpec(memory_space=m) for m in (pltpu.VMEM, pltpu.SMEM))
    shape = jax.ShapeDtypeStruct
    outs = [shape((r, 512), BF) for r in z.rows]
    outs += [shape((micro, frames, z.model), F32), shape((micro, frames, z.model), BF), shape((8, 128), F32)]
    outs += [shape((rows * segs * own_u, predictor.shape[-1]), F32)]
    scratch = [pltpu.VMEM((count, lanes), dtype) for _, lanes, dtype in STATE]
    scratch += [pltpu.VMEM((HEADS, count, count), BF), pltpu.VMEM((16, 128), F32), pltpu.VMEM((z.jr, 128), F32)]
    scratch += [pltpu.VMEM((16, z.model), F32)] * 2 + [pltpu.VMEM((3 * width, 512), BF)]
    scratch += [pltpu.VMEM((r, 512), BF) for r in z.rows] + [pltpu.VMEM((n * r, 512), BF) for r in z.rows]
    for g, r in enumerate(z.rows):
        scratch += scatter_scratch(n, r, 512, SHARES[3 - g])
    scratch += joint_shared(dims, width)
    scratch += [pltpu.SemaphoreType.DMA((4, n - 1))] * 2 + [pltpu.SemaphoreType.DMA((4, 5))] + scatter_sems(n, 4)
    return pl.pallas_call(
        functools.partial(pass_kernel, z, dims),
        out_shape=outs,
        in_specs=[vm] + [sm] * 3 + [vm] * (len(params) + 2),
        out_specs=[vm] * len(outs),
        scratch_shapes=scratch,
        compiler_params=pltpu.CompilerParams(collective_id=0, has_side_effects=True, vmem_limit_bytes=62 * 2**20),
    )(x, *ints, *params, predictor, bias_out)


SHARES = (0.15, 0.35, 0.2, 0.15)
ORDER_SUMS = (
    (0, 0, 0), (0, 1, 0), (0, 2, 0), (1, 0, 0), (3, 0, 0), (2, 0, 1), (0, 3, 0), (1, 1, 0), (3, 1, 0), (2, 1, 1),
    (2, 0, 2), (1, 2, 0), (3, 2, 0), (2, 2, 1), (2, 1, 2), (1, 3, 0), (3, 3, 0), (2, 3, 1), (3, 0, 1), (2, 0, 3),
    (2, 2, 2), (2, 1, 3), (2, 3, 2), (3, 0, 2), (3, 1, 1), (2, 0, 4), (2, 2, 3), (2, 1, 4), (3, 1, 2), (3, 2, 1),
    (2, 3, 3), (3, 0, 3), (2, 0, 5), (3, 3, 1), (2, 2, 4), (2, 1, 5), (3, 2, 2), (3, 1, 3), (2, 0, 6), (3, 3, 2),
    (2, 3, 4), (2, 1, 6), (3, 0, 4), (2, 2, 5), (3, 2, 3), (3, 1, 4), (3, 3, 3), (2, 1, 7), (2, 0, 7), (2, 3, 5),
    (3, 2, 4), (3, 1, 5), (3, 3, 4), (2, 2, 6), (3, 0, 5), (3, 2, 5), (3, 3, 5), (3, 1, 6), (2, 2, 7), (2, 3, 6),
    (3, 0, 6), (3, 2, 6), (3, 3, 6), (3, 1, 7), (2, 3, 7), (3, 0, 7), (3, 2, 7), (3, 3, 7),
)


def unpack_kernel(z, dims, js, own0, own1, own2, own3, grads, encoded, loss, g_predictor, *outs):
    frames, rows, segs, own_u, labs = dims
    ds, ff, pi, jr = z.ds, z.ff, z.pi, z.jr
    (
        loss_o, enc_o, grads_o, pred_o, gg0, g_in, g_out, gg1, g_qkv, g_att, gg2, g_pin, g_depth, gg3, g_pout, gg4,
        g_enc, g_pred, g_bias, g_joint, g_bias_out,
    ) = outs
    hit = (row_ids((128, rows)) == lane_ids((128, rows)) * own_u).astype(F32)
    loss_o[...] = lax.dot_general(
        loss[...], hit, (((1,), (0,)), ((), ())), precision=lax.Precision.HIGHEST, preferred_element_type=F32
    )[:segs]
    enc_o[...] = encoded[...]
    grads_o[...] = grads[...]
    for r in range(rows):
        for s in range(segs):
            first = (r * segs + s) * own_u
            pred_o[r, s] = g_predictor[first : first + own_u, :]
    small = own0[:32, 256:].astype(F32)
    for i, out in enumerate((gg0, gg1, gg2, gg3, gg4)):
        out[...] = small[GAIN_ROW + i : GAIN_ROW + i + 1, :ds]
    g_depth[...] = small[:TAPS, :ds]
    for i in range(4):
        g_bias_out[:, 256 * i : 256 * i + 256] = small[16 + i : 17 + i, :]
    g_bias_out[:, 1024:] = small[20:21, : g_bias_out.shape[1] - 1024]
    g_in[...] = own0[jr:, :].astype(F32).T
    g_out[...] = own1[:ff, :].astype(F32)
    g_qkv[...] = own1[ff:, :].astype(F32)
    g_att[...] = own2[:ds, :].astype(F32)
    g_pin[...] = own2[ds : ds + pi, :].astype(F32).T
    g_pout[...] = own2[ds + pi : 2 * ds + pi, :].astype(F32)
    g_enc[...] = own2[2 * ds + pi :, :].astype(F32)[:js]
    g_pred[:, :512] = own3[:jr, :].astype(F32)[:js]
    g_pred[:, 512:] = own0[:jr, :128].astype(F32)[:js]
    tail = own0[:jr, 128:256].astype(F32)
    wide = jnp.concatenate([tail, jnp.zeros((128 - jr, 128), F32)], axis=0) if jr < 128 else tail
    g_bias[...] = wide.T[BIAS_LANE : BIAS_LANE + 1, :js]
    g_joint[:, :512] = own3[jr : 2 * jr, :].astype(F32)[:js]
    g_joint[:, 512:1024] = own3[2 * jr :, :].astype(F32)[:js]
    g_joint[:, 1024:] = tail[:js, : g_joint.shape[1] - 1024]


def unpack_call(z, dims, js, out_width, own, grads, encoded, loss, g_predictor):
    frames, rows, segs, own_u, labs = dims
    shape = jax.ShapeDtypeStruct
    row = shape((1, z.ds), F32)
    line, features = z.model, g_predictor.shape[1]
    outs = [
        shape((segs, rows), F32), shape(encoded.shape, BF), shape(grads.shape, F32),
        shape((rows, segs, own_u, features), F32), row, shape((line, z.ff), F32), shape((z.ff, line), F32), row,
        shape((z.qk, line), F32), shape((z.ds, line), F32), row, shape((line, z.pi), F32), shape((TAPS, z.ds), F32),
        row, shape((z.ds, line), F32), row, shape((js, line), F32), shape((js, features), F32), shape((1, js), F32),
        shape((js, out_width), F32), shape((1, out_width), F32),
    ]
    vm = pl.BlockSpec(memory_space=pltpu.VMEM)
    return pl.pallas_call(
        functools.partial(unpack_kernel, z, dims, js),
        out_shape=outs,
        in_specs=[vm] * 8,
        out_specs=[vm] * len(outs),
        compiler_params=pltpu.CompilerParams(vmem_limit_bytes=60 * 2**20),
    )(*own, grads, encoded, loss, g_predictor)

def local(
    frames_in, predictor, seg_lengths, label_counts, label_ids, gain_ffn, w_ffn_in, w_ffn_out, gain_att, w_qkv,
    w_att_out, gain_conv, w_point_in, w_depth, gain_depth, w_point_out, gain_out, w_enc, w_pred, bias_joint,
    w_joint_out, bias_out,
):
    n, labs = lax.axis_size("dp"), lax.axis_size("lab")
    micro, frames, model = frames_in.shape
    rows, segs, own_u, joint = predictor.shape
    ds, js = model // n, w_pred.shape[1]
    jr = max(-(-js // TILE), 2) * TILE
    z = Sizes(n, ds, w_ffn_in.shape[1], w_qkv.shape[1], w_point_in.shape[1], jr)
    dims = (frames, rows, segs, own_u, labs)
    lengths, counts, labels = seg_lengths.T, label_counts.T, label_ids.transpose(1, 2, 0)
    gains = [g[None] for g in (gain_ffn, gain_att, gain_conv, gain_depth, gain_out)]
    params = (
        w_ffn_in, w_ffn_out, w_qkv.T, w_att_out, w_point_in, w_point_out, w_enc.T, w_pred.T, w_joint_out,
        bias_joint[None], w_depth, *gains,
    )
    *own, grad_frames, encoded, loss, g_predictor = pass_call(
        z, dims, frames_in, (lengths, counts, labels), params, predictor, bias_out
    )
    (
        loss, encoded, grad_frames, g_predictor, gg0, g_in, g_out, gg1, g_qkv, g_att, gg2, g_pin, g_depth, gg3, g_pout,
        gg4, g_enc, g_pred, g_bias, g_joint, g_bias_out,
    ) = unpack_call(z, dims, js, bias_out.shape[0], own, grad_frames, encoded, loss, g_predictor)
    return (
        loss.T, encoded, grad_frames, g_predictor, gg0[0], g_in, g_out, gg1[0], g_qkv.T, g_att, gg2[0], g_pin, g_depth,
        gg3[0], g_pout, gg4[0], g_enc.T, g_pred.T, g_bias[0], g_joint, g_bias_out[0],
    )


def solution(mesh):
    rows, whole = P(("dp", "lab"), None, None), P()
    predictor, columns, lines, vector = P("dp", None, "lab", None), P(None, "dp"), P("dp", None), P("dp")
    params = (
        vector, columns, lines, vector, columns, lines, vector, columns, columns, vector, lines, vector, columns,
        columns, vector, lines, whole,
    )
    return jax.shard_map(
        local,
        mesh=mesh,
        in_specs=(rows, predictor, lines, lines, P("dp", None, "lab")) + params,
        out_specs=(lines, rows, rows, predictor) + params,
        check_vma=False,
    )
```

```python
import functools

import jax
import jax.numpy as jnp
from jax import lax
from jax.experimental import pallas as pl
from jax.experimental.pallas import tpu as pltpu
from jax.sharding import PartitionSpec as P


MESH = pl.DeviceIdType.MESH
F32 = jnp.float32
BF = jnp.bfloat16
TILE = 16


def ring_place(dp, n):
    odd = dp % 2
    return (1 - odd) * (dp // 2) + odd * (n - 1 - dp // 2)


def ring_device(place, n):
    place = (place + 2 * n) % n
    high = place // (n // 2)
    return (1 - high) * (2 * place) + high * (2 * (n - 1 - place) + 1)


def x_rows(rows, share):
    tiles = rows // TILE
    return min(tiles // 2, int(tiles * share + 0.5)) * TILE


class Where:
    def __init__(self, n):
        self.n = n
        self.dp = lax.axis_index("dp")
        self.lab = lax.axis_index("lab")
        self.core = self.lab % 2
        self.side = self.lab // 2
        self.place = ring_place(self.dp, n)
        self.right = (ring_device(self.place + 1, n), self.lab)
        self.left = (ring_device(self.place - 1, n), self.lab)
        self.twin = (self.dp, self.side * 2 + 1 - self.core)
        self.across = (self.dp, (1 - self.side) * 2 + self.core)
        self.far = (ring_device(self.place + 1 - 2 * self.core, n), self.lab)
        self.far_back = (ring_device(self.place + 2 * self.core - 1, n), self.lab)
        self.corner = (self.dp, (1 - self.side) * 2 + 1 - self.core)

    def at(self, distance):
        return ring_device(self.place + distance, self.n)

    def greet(self, meanwhile):
        barrier = pltpu.get_barrier_semaphore()
        others = (self.right, self.left, self.twin, self.across, self.corner)
        for other in others:
            pl.semaphore_signal(barrier, inc=1, device_id=other, device_id_type=MESH)
        meanwhile()
        pl.semaphore_wait(barrier, len(others))


def remote(src, dst, send_sem, recv_sem, device):
    return pltpu.make_async_remote_copy(
        src_ref=src,
        dst_ref=dst,
        send_sem=send_sem,
        recv_sem=recv_sem,
        device_id=device,
        device_id_type=MESH,
    )


class Gather:
    def __init__(self, where, source, target, rows, ring_recv, x_recv, sems, share):
        self.w, self.source, self.target, self.rows = where, source, target, rows
        self.width = target.shape[1]
        self.half = self.width // 2
        self.cut = x_rows(rows, share)
        self.ring_recv, self.x_recv, self.sems = ring_recv, x_recv, sems
        self.steps = where.n // 2

    def lanes(self):
        return pl.ds(pl.multiple_of(self.w.core * self.half, 128), self.half)

    def rows_at(self, shard, offset, size):
        base = shard * self.rows if shard is not None else 0
        return pl.ds(pl.multiple_of(base + offset, TILE), size)

    def ring_part(self, ref, shard):
        return ref.at[self.rows_at(shard, self.w.side * self.cut, self.rows - self.cut), self.lanes()]

    def x_part(self, ref, shard, side):
        return ref.at[self.rows_at(shard, side * (self.rows - self.cut), self.cut), self.lanes()]

    def slot(self, distance):
        return distance + self.steps - 1 if distance < 0 else distance + self.steps - 2

    def hop(self, distance, first):
        w = self.w
        if distance == self.steps:
            shard = w.at((2 * w.core - 1) * (self.steps - 1))
            device = w.far
        else:
            shard = w.at(distance + 1) if distance < 0 else w.at(distance - 1)
            device = w.right if distance < 0 else w.left
        src = self.ring_part(self.source, None) if first else self.ring_part(self.target, shard)
        slot = 2 * self.steps - 2 if distance == self.steps else self.slot(distance)
        remote(src, self.ring_part(self.target, shard), self.sems.at[1], self.ring_recv.at[slot], device).start()

    def own(self):
        pltpu.make_async_copy(
            self.source, self.target.at[self.rows_at(self.w.dp, 0, self.rows), :], self.sems.at[4]
        ).start()

    def arrived(self, distance):
        w = self.w
        shard = w.at(distance)
        slot = 2 * self.steps - 2 if distance == self.steps else self.slot(distance)
        part = self.ring_part(self.target, shard)
        remote(part, part, self.sems.at[1], self.ring_recv.at[slot], w.right).wait_recv()

    def spread(self, distance):
        w = self.w
        shard = w.at(distance)
        slot = 2 * self.steps - 2 if distance == self.steps else self.slot(distance)
        if self.cut:
            part = self.x_part(self.target, shard, w.side)
            remote(part, part, self.sems.at[2], self.x_recv.at[slot], w.across).start()
        part = self.ring_part(self.target, shard)
        remote(part, part, self.sems.at[3], self.sems.at[0], w.twin).start()

    def crossed(self, distance):
        if not self.cut:
            return
        w = self.w
        shard = w.at(distance)
        slot = 2 * self.steps - 2 if distance == self.steps else self.slot(distance)
        part = self.x_part(self.target, shard, 1 - w.side)
        remote(part, part, self.sems.at[2], self.x_recv.at[slot], w.across).wait_recv()
        remote(part, part, self.sems.at[3], self.sems.at[0], w.twin).start()

    def whole(self):
        part = self.target.at[pl.ds(0, (self.w.n - 1) * self.rows), pl.ds(0, self.half)]
        remote(part, part, self.sems.at[3], self.sems.at[0], self.w.twin).wait_recv()
        pltpu.make_async_copy(
            self.source, self.target.at[self.rows_at(self.w.dp, 0, self.rows), :], self.sems.at[4]
        ).wait()

    def drain(self):
        count = self.w.n - 1
        for sem, rows in ((1, self.rows - self.cut), (2, self.cut), (3, self.rows)):
            if rows:
                part = self.target.at[pl.ds(0, count * rows), pl.ds(0, self.half)]
                remote(part, part, self.sems.at[sem], self.sems.at[sem], self.w.twin).wait_send()

    def begin(self):
        self.own()
        self.hop(-1, True)
        self.hop(1, True)

    def distances(self, named):
        sign, last = (1 if named > 0 else -1), self.steps
        if abs(named) == 2:
            return [sign * d for d in range(2, last - 1)]
        return [sign * (abs(named) if abs(named) < 2 else last + abs(named) - 4)]

    def take(self, distance):
        if distance == self.steps:
            self.arrived(distance)
            self.spread(distance)
        elif distance == self.steps - 1:
            self.arrived(-distance)
            self.arrived(distance)
            self.hop(self.steps, False)
            self.spread(-distance)
            self.spread(distance)
        else:
            self.arrived(distance)
            self.hop(distance + (1 if distance > 0 else -1), False)
            self.spread(distance)


class Pair:
    def __init__(self, where, grads, held, rows, send, recv):
        self.w, self.grads, self.held, self.rows = where, grads, held, rows
        self.half = grads.shape[1] // 2
        self.copy = remote(self.grads.at[:, self.lanes(1 - where.core)], held, send.at[0], recv.at[0], where.twin)

    def lanes(self, core):
        return pl.ds(pl.multiple_of(core * self.half, 128), self.half)

    def give(self):
        self.copy.start()

    def add(self):
        self.copy.wait_recv()

        def body(i, _):
            at = pl.ds(pl.multiple_of(i * self.rows, TILE), self.rows)
            self.held[at, :] = (
                self.held[at, :].astype(F32) + self.grads[at, self.lanes(self.w.core)].astype(F32)
            ).astype(BF)
            return 0

        lax.fori_loop(0, self.w.n, body, 0)

    def drain(self):
        self.copy.wait_send()


class Chain:
    def __init__(self, pair, out, crossed, bufs, send, recv, share):
        self.pair, self.w, self.out, self.crossed = pair, pair.w, out, crossed
        self.cut = x_rows(pair.rows, share)
        self.size = self.cut if crossed else pair.rows - 2 * self.cut
        self.depth = self.w.n // 2 - 1
        self.xbuf, self.rbuf = bufs
        self.send, self.recv = send, recv
        self.stages = self.depth + 5

    def first(self, side):
        return side * (self.pair.rows - self.cut) if self.crossed else self.cut

    def rows_at(self, shard, side=None):
        base = shard * self.pair.rows + self.first(self.w.side if side is None else side)
        return pl.ds(pl.multiple_of(base, TILE), self.size)

    def out_at(self, side=None):
        at = pl.ds(pl.multiple_of(self.first(self.w.side if side is None else side), TILE), self.size)
        return self.out.at[at, self.pair.lanes(self.w.core)]

    def got(self, sem, dst):
        remote(dst, dst, self.send.at[0], self.recv.at[sem], self.w.twin).wait_recv()

    def ring(self, slot, src, device):
        remote(src, self.rbuf.at[slot], self.send.at[1], self.recv.at[slot], device).start()

    def stage(self, s):
        if not self.size:
            return
        w, n, depth, held = self.w, self.w.n, self.depth, self.pair.held
        last = 2 * depth + 1
        if s == 0:
            if self.crossed:
                for i in range(n):
                    remote(
                        held.at[self.rows_at(i, 1 - w.side), :], self.xbuf.at[i], self.send.at[0], self.recv.at[last],
                        w.across,
                    ).start()
        elif s == 1:
            if self.crossed:
                self.got(last, self.xbuf)

                def body(i, _):
                    at = self.rows_at(i)
                    held[at, :] = (held[at, :].astype(F32) + self.xbuf[i].astype(F32)).astype(BF)
                    return 0

                lax.fori_loop(0, n, body, 0)
            dest = w.at((2 * w.core - 1) * (depth + 1))
            self.ring(2 * depth, held.at[self.rows_at(dest), :], w.far_back)
        elif s < 2 + depth:
            hop = s - 2
            for way in (0, 1):
                sign = 1 - 2 * way
                own = held[self.rows_at(w.at(sign * (depth - hop))), :].astype(F32)
                slot = 2 * hop + way
                if hop == 0:
                    if way == 0:
                        self.got(2 * depth, self.rbuf.at[2 * depth])
                    far = self.rbuf[2 * depth].astype(F32)
                    pick = w.core if way == 0 else 1 - w.core
                    own = own + jnp.where(pick == 1, far, 0.0)
                    at = 2 * depth + 1 + way
                else:
                    at = slot - 2
                    self.got(at, self.rbuf.at[at])
                    own = own + self.rbuf[at].astype(F32)
                self.rbuf[at] = own.astype(BF)
                self.ring(slot, self.rbuf.at[at], w.right if way == 0 else w.left)
        elif s == 2 + depth:
            total = held[self.rows_at(w.dp), :].astype(F32)
            for way in (0, 1):
                at = 2 * depth - 2 + way
                self.got(at, self.rbuf.at[at])
                total = total + self.rbuf[at].astype(F32)
            if self.crossed:
                mine = self.out_at()
                mine[...] = total.astype(BF)
                remote(mine, mine, self.send.at[2], self.recv.at[last + 1], w.across).start()
                remote(mine, mine, self.send.at[3], self.recv.at[last + 2], w.twin).start()
            else:
                self.xbuf[0] = total.astype(BF)
                remote(self.xbuf.at[0], self.xbuf.at[1], self.send.at[2], self.recv.at[last + 1], w.across).start()
        elif s == 3 + depth:
            if self.crossed:
                other = self.out_at(1 - w.side)
                self.got(last + 1, other)
                remote(other, other, self.send.at[4], self.recv.at[last + 3], w.twin).start()
            else:
                self.got(last + 1, self.xbuf.at[1])
                mine = self.out_at()
                mine[...] = (self.xbuf[0].astype(F32) + self.xbuf[1].astype(F32)).astype(BF)
                remote(mine, mine, self.send.at[3], self.recv.at[last + 2], w.twin).start()
        elif s == 4 + depth:
            part = self.out_at()
            self.got(last + 2, part)
            if self.crossed:
                self.got(last + 3, part)

    def drain(self):
        if not self.size:
            return
        ring = self.rbuf.at[pl.ds(0, 2 * self.depth + 1)]
        remote(ring, ring, self.send.at[1], self.recv.at[0], self.w.twin).wait_send()
        part = self.out_at()
        remote(part, part, self.send.at[2], self.recv.at[0], self.w.twin).wait_send()
        remote(part, part, self.send.at[3], self.recv.at[0], self.w.twin).wait_send()
        if self.crossed:
            remote(part, part, self.send.at[4], self.recv.at[0], self.w.twin).wait_send()
            remote(self.xbuf, self.xbuf, self.send.at[0], self.recv.at[0], self.w.twin).wait_send()


def scatter_scratch(n, rows, width, share):
    half, cut, depth = width // 2, x_rows(rows, share), n // 2 - 1
    out = [pltpu.VMEM((n * rows, half), BF)]
    for count, size in ((2, rows - 2 * cut), (n, cut)):
        out += [pltpu.VMEM((count, max(size, TILE), half), BF), pltpu.VMEM((2 * depth + 3, max(size, TILE), half), BF)]
    return out


def scatter_sems(n, k):
    return [pltpu.SemaphoreType.DMA((k, 11)), pltpu.SemaphoreType.DMA((k, 2 * n + 8))]


class Scatter:
    def __init__(self, where, grads, out, rows, bufs, send, recv, share):
        n = where.n
        self.pair = Pair(where, grads, bufs[0], rows, send.at[pl.ds(10, 1)], recv.at[pl.ds(2 * n + 7, 1)])
        self.straight = Chain(self.pair, out, False, bufs[1:3], send.at[pl.ds(0, 5)], recv.at[pl.ds(0, n + 2)], share)
        self.crossed = Chain(self.pair, out, True, bufs[3:5], send.at[pl.ds(5, 5)], recv.at[pl.ds(n + 2, n + 3)], share)

    def drain(self):
        for part in (self.pair, self.straight, self.crossed):
            part.drain()


def sum_up(parts, work, order):
    depth = parts[0].straight.depth
    for what, g, stage in order:
        part = parts[g]
        if what == 0:
            work(g)
            part.pair.give()
        elif what == 1:
            part.pair.add()
        else:
            chain = part.straight if what == 2 else part.crossed
            stages = [stage] if stage < 4 else range(4, depth + 2) if stage == 4 else [stage + depth - 3]
            for s in stages:
                chain.stage(s)
    for part in parts:
        part.drain()


LOW = -100000.0
TOK = 1024
KINDS = 7
BIAS_LANE = 6


def mm(a, b):
    return lax.dot_general(a, b, (((1,), (0,)), ((), ())), preferred_element_type=F32)


def mm_t(a, b):
    return lax.dot_general(a, b, (((1,), (1,)), ((), ())), preferred_element_type=F32)


def t_mm(a, b):
    return lax.dot_general(a, b, (((0,), (0,)), ((), ())), preferred_element_type=F32)


def lane_ids(shape):
    return lax.broadcasted_iota(jnp.int32, shape, len(shape) - 1)


def row_ids(shape):
    return lax.broadcasted_iota(jnp.int32, shape, 0)


def seg_of(t, ends):
    return sum((t >= e).astype(jnp.int32) for e in ends[:-1])


def pick(seg, values):
    out = values[0]
    for s in range(1, len(values)):
        out = jnp.where(seg == s, values[s], out)
    return out


def scalar_ends(lengths, r, segs):
    ends, total = [], 0
    for s in range(segs):
        total = total + lengths[s, r]
        ends.append(total)
    return ends


def lse_of(terms):
    top = functools.reduce(jnp.maximum, terms)
    return top, functools.reduce(jnp.add, [jnp.exp(v - top) for v in terms])


def lattice(lengths, counts, terms, skewed, hist, grads, loss, dims):
    frames, rows, segs, own_u, labs = dims
    wide = (frames, 128)
    lane = lane_ids(wide)
    group = rows * own_u
    j, row, u = lane % own_u, (lane % group) // own_u, (lane // group) * own_u + lane % own_u
    t = row_ids(wide)
    all_ends = [scalar_ends(lengths, r, segs) for r in range(rows)]

    def per_lane(values):
        out = jnp.zeros(wide, jnp.int32)
        for r in range(rows):
            out = jnp.where(row == r, values[r], out)
        return out

    ends = [per_lane([all_ends[r][s] for r in range(rows)]) for s in range(segs)]
    labels_in = [per_lane([counts[s, r] for r in range(rows)]) for s in range(segs)]
    seg = seg_of(t, ends)
    stop = pick(seg, ends)
    begin = pick(seg, [jnp.zeros(wide, jnp.int32)] + ends[:-1])
    target = pick(seg, labels_in)
    remain, first = stop - t, t == begin

    kinds = []
    per_vreg = 128 // group
    for k in range(KINDS):
        value = None
        for dev in range(labs):
            part = terms[dev, :, (k // per_vreg) * 128 : (k // per_vreg) * 128 + 128]
            shift = (dev - k % per_vreg) * group % 128
            part = pltpu.roll(part, shift, 1) if shift else part
            value = part if value is None else jnp.where(lane // group == dev, part, value)
        kinds.append(value)
    blank_lp, durs, label_lp = kinds[0], kinds[1:6], kinds[6]
    last_u = own_u * labs - 1
    emit, blank, blank_raw = [], [None], [None]
    for d in range(5):
        ok = (u < last_u) & (d <= remain - 1)
        emit.append(jnp.where(ok, label_lp + durs[d], LOW))
        if d:
            blank_raw.append(blank_lp + durs[d])
            blank.append(jnp.where(d <= remain - 1, blank_raw[d], LOW))
    final = (u == target) & (remain <= 4)
    closing = jnp.zeros(wide, F32)
    for d in range(1, 5):
        closing = jnp.where(remain == d, blank_raw[d], closing)
    closing = jnp.where(final, closing, LOW)
    start = jnp.where(first & (u == 0), 0.0, LOW)

    tall = frames + 16
    tall_u = (lane_ids((tall, 128)) // group) * own_u + lane_ids((tall, 128)) % own_u
    tall_j = lane_ids((tall, 128)) % own_u
    pad = jnp.full((16, 128), LOW, F32)

    def skew(value):
        value = jnp.concatenate([value, pad], axis=0)
        for bit in (1, 2, 4, 8):
            value = jnp.where((tall_u // bit) % 2 == 1, pltpu.roll(value, bit, 0), value)
        return value

    def unskew(value):
        for bit in (1, 2, 4, 8):
            value = jnp.where((tall_u // bit) % 2 == 1, pltpu.roll(value, tall - bit, 0), value)
        return value[:frames]

    up = 128 - (group - own_u + 1)

    def next_up(value, jj):
        return jnp.where(jj == 0, pltpu.roll(value, group - own_u + 1, 1), pltpu.roll(value, 1, 1))

    def next_down(value, jj):
        return jnp.where(jj == own_u - 1, pltpu.roll(value, up, 1), pltpu.roll(value, 127, 1))

    lead = jnp.full((8, 128), LOW, F32)

    def keep(i, value):
        skewed[i, 0:8, :] = lead
        skewed[i, 8 : 8 + tall, :] = value

    for d in range(1, 5):
        keep(d - 1, skew(blank[d]))
    for d in range(5):
        value = skew(emit[d])
        keep(4 + d, value)
        keep(9 + d, next_up(value, tall_j))
    keep(14, skew(start))
    keep(15, skew(closing))
    waves = frames + last_u + 1
    one_j = lane_ids((1, 128)) % own_u
    low_row = skewed[0, 0:1, :]

    def at(i, w):
        return skewed[i, pl.ds(w + 8, 1), :]

    def combine(old, near):
        top_old, sum_old = lse_of(old)
        top = functools.reduce(jnp.maximum, near, top_old)
        total = sum_old * jnp.exp(top_old - top)
        for v in near:
            total = total + jnp.exp(v - top)
        return top + jnp.log(total)

    def wave(i, carry):
        a, ra, b, rb = carry
        old = [at(14, i)]
        for d in range(2, 5):
            old.append(a[d - 1] + at(d - 1, i - d))
        for d in range(2, 6):
            old.append(ra[d - 1] + at(8 + d, i - d))
        new_a = combine(old, [a[0] + at(0, i - 1), ra[0] + at(9, i - 1)])
        back = waves - 1 - i
        old = [at(15, back)]
        for d in range(2, 5):
            old.append(b[d - 1] + at(d - 1, back))
        for d in range(2, 6):
            old.append(rb[d - 1] + at(3 + d, back))
        new_b = combine(old, [b[0] + at(0, back), rb[0] + at(4, back)])
        hist[0, pl.ds(i, 1), :] = new_a
        hist[1, pl.ds(back, 1), :] = new_b
        return (
            (new_a,) + a[:-1],
            (next_up(new_a, one_j),) + ra[:-1],
            (new_b,) + b[:-1],
            (next_down(new_b, one_j),) + rb[:-1],
        )

    hist[...] = jnp.full(hist.shape, LOW, F32)
    lax.fori_loop(
        0, waves, wave, ((low_row,) * 4, (low_row,) * 5, (low_row,) * 4, (low_row,) * 5), unroll=UNROLL
    )
    alpha, beta = unskew(hist[0]), unskew(hist[1])
    ahead = next_down(beta, j)
    norm = jnp.zeros(wide, F32)
    heads = jnp.where(first & (u == 0), beta, 0.0)
    for s in range(segs):
        value = jnp.sum(jnp.where(seg == s, heads, 0.0), axis=0, keepdims=True)
        step = 1
        while step < own_u:
            value = value + pltpu.roll(value, step, 1)
            step *= 2
        step = group
        while step < 128:
            value = value + pltpu.roll(value, step, 1)
            step *= 2
        norm = jnp.where(seg == s, value, norm)
        length = ends[s] - (ends[s - 1] if s else 0)
        loss[pl.ds(s, 1), :] = -value / length[:1].astype(F32)
    base = alpha - norm
    total_a, total_b = None, None
    for d in range(5):
        there = pltpu.roll(ahead, frames - d, 0) if d else ahead
        g = -jnp.exp(base + emit[d] + there)
        total_a = g if d == 0 else total_a + g
        if d:
            gb = -jnp.exp(base + blank[d] + pltpu.roll(beta, frames - d, 0))
            gb = gb - jnp.exp(jnp.where(final & (remain == d), base + blank_raw[d], LOW))
            total_b = gb if d == 1 else total_b + gb
            g = g + gb
        grads[1 + d] = g
    grads[0] = total_b
    grads[6] = total_a


def joint_scratch(dims, width):
    frames, rows, segs, own_u, labs = dims
    span, inner = own_u * frames, rows * segs * own_u
    return [
        pltpu.VMEM((inner, width), F32),
        pltpu.VMEM((rows, span, width + 128), BF),
        pltpu.VMEM((rows, span, width) if width <= ROOMY else (8, 128), BF),
        pltpu.VMEM((width + 128, VOCAB + 128), BF),
        pltpu.VMEM((VOCAB, width) if width <= ROOMY else (8, 128), BF),
        pltpu.VMEM((rows, span, VOCAB), BF),
        pltpu.VMEM((rows, span, 128), F32),
        pltpu.VMEM((16, frames + 24, 128), F32),
        pltpu.VMEM((2, frames + 16, 128), F32),
        pltpu.VMEM((KINDS, frames, 128), F32),
        pltpu.VMEM((inner, width), BF),
    ]


def joint_shared(dims, width):
    frames, rows, segs, own_u, labs = dims
    micro, inner = rows // labs, rows * segs * own_u
    return [
        pltpu.VMEM((micro, frames, width), BF),
        pltpu.VMEM((rows, frames, width), BF),
        pltpu.VMEM((inner, 640), F32),
        pltpu.VMEM((inner, 768), BF),
        pltpu.VMEM((frames, 256), F32),
        pltpu.VMEM((labs, frames, 256), F32),
        pltpu.VMEM((labs, micro, frames, width), BF),
        pltpu.VMEM((labs, micro, frames, width), BF),
        pltpu.VMEM((micro, frames, width), BF),
        pltpu.VMEM((width, 256), BF),
        pltpu.VMEM((16, 256), F32),
        pltpu.SemaphoreType.DMA((3, labs)),
        pltpu.SemaphoreType.DMA((3, labs)),
    ]


class Joint:
    def __init__(self, z, w, dims, predictor, lengths, counts, labels, bias_out, g_predictor, g_pack, loss, shared):
        self.z, self.w, self.dims = z, w, dims
        self.predictor, self.lengths, self.counts, self.labels = predictor, lengths, counts, labels
        self.bias_out, self.g_predictor, self.g_pack, self.loss = bias_out, g_predictor, g_pack, loss
        (
            self.enc_own, self.enc_all, self.pred_wide, self.pred, self.mine, self.terms, self.part, self.came,
            self.g_enc, self.g_mix, self.g_bias, self.send, self.recv,
        ) = shared
        self.micro = dims[1] // dims[4]

    def owner(self, j):
        return ((self.w.side + j // 2) % 2) * 2 + (self.w.core + j % 2) % 2

    def device(self, j):
        return (self.w.dp, self.owner(j))

    def enc_copy(self, j, source):
        to = self.enc_all.at[pl.ds(source * self.micro, self.micro)]
        return remote(self.enc_own, to, self.send.at[0, j], self.recv.at[0, j], self.device(j))

    def term_copy(self, j, source):
        return remote(self.mine, self.terms.at[source], self.send.at[1, j], self.recv.at[1, j], self.device(j))

    def part_copy(self, j):
        return remote(self.part.at[j], self.came.at[j], self.send.at[2, j], self.recv.at[2, j], self.device(j))

    def prepare(self):
        frames, rows, segs, own_u, labs = self.dims
        features = self.predictor.shape[-1]
        for r in range(rows):
            for s in range(segs):
                first = (r * segs + s) * own_u
                self.pred_wide[first : first + own_u, :] = self.predictor[r, s].astype(F32)
        self.pred[:, :features] = self.pred_wide[...].astype(BF)
        self.pred[:, features:] = (lane_ids((self.pred.shape[0], 128)) == BIAS_LANE).astype(BF)

    def hand_on(self):
        rows = self.enc_all.at[pl.ds(self.owner(2) * self.micro, self.micro)]
        return remote(rows, rows, self.send.at[0, 3], self.recv.at[0, 3], self.device(1))

    def share(self):
        for j in (1, 2):
            self.enc_copy(j, self.w.lab).start()
        self.enc_all[pl.ds(self.w.lab * self.micro, self.micro)] = self.enc_own[...]

    def drain(self):
        self.hand_on().wait_send()
        for j in range(1, self.dims[4]):
            if j < 3:
                self.enc_copy(j, self.w.lab).wait_send()
            self.term_copy(j, self.w.lab).wait_send()
            self.part_copy(j).wait_send()

    def run(self, full, *scratch):
        joint_run(self, full, *scratch)


def joint_run(
    job, full, proj, hid, slope, wide, back_w, prob, prob_tail, skewed, hist, grads, g_pred
):
    z, dims, lengths, counts, labels, bias_out = job.z, job.dims, job.lengths, job.counts, job.labels, job.bias_out
    frames, rows, segs, own_u, labs = dims
    micro = rows // labs
    bias_out = bias_out[...].astype(F32).reshape(1, -1)
    n, width, span, features = z.n, z.n * z.jr, own_u * frames, job.predictor.shape[-1]
    pred, mine, terms, enc_all, part, came = job.pred, job.mine, job.terms, job.enc_all, job.part, job.came
    enc_copy, term_copy, part_copy, owner = job.enc_copy, job.term_copy, job.part_copy, job.owner
    g_predictor, g_pack, g_mix, g_bias, g_enc, loss = (
        job.g_predictor, job.g_pack, job.g_mix, job.g_bias, job.g_enc, job.loss
    )
    turn = STEP if width <= ROOMY else 1
    mixes = rows_of(full[0], n, 0, z.jr)
    proj[...] = mm_t(pred[:, :512], rows_of(full[3], n, 0, z.jr)) + mm_t(pred[:, 512:], mixes[:, :256])
    wide[:width, :512] = rows_of(full[3], n, z.jr, z.jr)
    wide[:width, 512:TOK] = rows_of(full[3], n, 2 * z.jr, z.jr)
    wide[:width, TOK:VOCAB] = mixes[:, 128:256]
    top_row = row_ids((128, TOK)) == 0
    wide[width:, :TOK] = jnp.where(top_row, bias_out[:, :TOK].astype(F32), 0.0).astype(BF)
    mine[:, :128] = jnp.zeros((frames, 128), F32)
    mine[:1, : bias_out.shape[1] - TOK] = bias_out[:, TOK:].astype(F32)
    wide[width:, TOK:VOCAB] = jnp.where(row_ids((128, 128)) == 0, mine[:1, :128], 0.0).astype(BF)
    lane_1 = lane_ids((1, 128))
    wanted = jnp.zeros((1, 128), jnp.int32)
    for r in range(rows):
        for s in range(segs):
            for u in range(own_u):
                wanted = jnp.where(lane_1 == (r * segs + s) * own_u + u, labels[s, u, r], wanted)
    wide[:, VOCAB:] = mm(wide[:, :TOK], (row_ids((TOK, 128)) == wanted).astype(BF)).astype(BF)
    roomy = width <= ROOMY
    if roomy:
        back_w[...] = wide[:width, :VOCAB].astype(F32).T.astype(BF)
    hid[:, :, width:] = (lane_ids((rows, span, 128)) == 0).astype(BF)
    lane_t = lane_ids((frames, 128))
    lane_w = lane_ids((frames, TOK))
    group = rows * own_u
    per_vreg = 128 // group

    def row_of(k):
        return owner(k // micro) * micro + k % micro

    def forward(k):
        r = row_of(k)
        ends = scalar_ends(lengths, r, segs)
        seg = seg_of(row_ids((frames, width)), ends)
        enc = enc_all[r].astype(F32)
        for u in range(own_u):
            at = slice(u * frames, (u + 1) * frames)
            per_frame = pick(
                seg, [proj[pl.ds(r * segs * own_u + s * own_u + u, 1), :] for s in range(segs)]
            )
            value = jnp.tanh(enc + per_frame)
            hid[r, at, :width] = value.astype(BF)
            if roomy:
                slope[r, at, :] = (1.0 - value * value).astype(BF)
        logits = mm(hid[r], wide[...])
        seg_l = seg_of(row_ids((frames, 128)), ends)
        for u in range(own_u):
            at = slice(u * frames, (u + 1) * frames)
            logit, last, named = logits[at, :TOK], logits[at, TOK:VOCAB], logits[at, VOCAB:]
            top = jnp.maximum(jnp.max(logit, axis=1, keepdims=True), last[:, 0:1])
            top_dur = jnp.max(
                jnp.where((lane_t >= 1) & (lane_t <= 5), last, -jnp.inf), axis=1, keepdims=True
            )
            is_tok = lane_t == 0
            e_last = jnp.where(
                lane_t < 6, jnp.exp(jnp.where(lane_t < 6, last - jnp.where(is_tok, top, top_dur), 0.0)), 0.0
            )
            e = jnp.exp(logit - top)
            total = jnp.sum(e, axis=1, keepdims=True) + e_last[:, 0:1]
            total_dur = jnp.sum(jnp.where(is_tok, 0.0, e_last), axis=1, keepdims=True)
            prob[r, at, :TOK] = e.astype(BF)
            over = 1.0 / total
            prob_tail[r, at, :] = jnp.where(lane_t == 6, over, e_last * jnp.where(is_tok, over, 1.0 / total_dur))
            norm_tok, norm_dur = top + jnp.log(total), top_dur + jnp.log(total_dur)
            column = r * segs * own_u + seg_l * own_u + u
            at_label = jnp.sum(jnp.where(lane_t == column, named, 0.0), axis=1, keepdims=True) - norm_tok
            lp = last - jnp.where(is_tok, norm_tok, norm_dur)
            for half in range(2):
                cols = slice(half * 128, half * 128 + 128)
                value = mine[:, cols]
                for kind in range(half * per_vreg, min(KINDS, (half + 1) * per_vreg)):
                    column = at_label if kind == 6 else lp[:, kind : kind + 1]
                    value = jnp.where(lane_t == (kind % per_vreg) * group + r * own_u + u, column, value)
                mine[:, cols] = value

    mine[...] = jnp.zeros(mine.shape, F32)

    def forward_step(i, _):
        for j in range(1, labs):
            @pl.when(i * turn == j * micro)
            def _():
                enc_copy(j, owner(j)).wait_recv()
                if j == 2:
                    job.hand_on().start()
        for k in range(turn):
            forward(i * turn + k)
        return 0

    lax.fori_loop(0, rows // turn, forward_step, 0)
    terms[job.w.lab] = mine[...]

    for j in range(1, labs):
        term_copy(j, job.w.lab).start()
    for j in range(1, labs):
        term_copy(j, owner(j)).wait_recv()
    lattice(lengths, counts, terms, skewed, hist, grads, loss, dims)

    def backward(k):
        r = row_of(k)
        ends = scalar_ends(lengths, r, segs)
        shift = (256 - job.w.lab * group - r * own_u) % 128
        rolled = [pltpu.roll(grads[kind], shift, 1) for kind in range(KINDS)]
        seg_l = seg_of(row_ids((frames, TOK)), ends)
        for u in range(own_u):
            at = slice(u * frames, (u + 1) * frames)
            a, b = rolled[6][:, u : u + 1], rolled[0][:, u : u + 1]
            both = a + b
            label = pick(seg_l, [labels[s, u, r] for s in range(segs)])
            tails = prob_tail[r, at, :]
            scaled = both * tails[:, 6:7]
            prob[r, at, :TOK] = (jnp.where(lane_w == label, a, 0.0) - prob[r, at, :TOK].astype(F32) * scaled).astype(BF)
            aim = jnp.zeros((frames, 128), F32)
            for kind in range(6):
                aim = jnp.where(lane_t == kind, rolled[kind][:, u : u + 1], aim)
            prob[r, at, TOK:] = jnp.where(lane_t < 6, aim - tails * both, 0.0).astype(BF)
        if roomy:
            back = mm(prob[r], back_w[...]) * slope[r].astype(F32)
        else:
            value = hid[r, :, :width].astype(F32)
            back = mm_t(prob[r], wide[:width, :VOCAB]) * (1.0 - value * value)
        summed = back[:frames]
        for u in range(1, own_u):
            summed = summed + back[u * frames : (u + 1) * frames]
        part[k // micro, k % micro] = summed.astype(BF)
        shape = (segs * own_u, span)
        lanes = lane_ids(shape)
        seg_t = seg_of(lanes % frames, ends)
        hit = (row_ids(shape) == seg_t * own_u + lanes // frames).astype(BF)
        g_pred[pl.ds(r * segs * own_u, segs * own_u), :] = mm(hit, back.astype(BF)).astype(BF)

    def backward_step(i, _):
        first = rows - (i + 1) * turn
        for k in range(turn - 1, -1, -1):
            backward(first + k)
        for j in range(1, labs):
            @pl.when(first == j * micro)
            def _():
                part_copy(j).start()
        return 0

    lax.fori_loop(0, rows // turn, backward_step, 0)
    gp = g_pred[...]
    g_predictor[:, :512] = mm(gp, rows_of(full[3], n, 0, z.jr))
    g_predictor[:, 512:] = mm(gp, rows_of(full[0], n, 0, z.jr)[:, : features - 512])
    shards, block = n, z.jr
    h_all = hid[...].reshape(rows * span, width + 128)
    g_bias[...] = jnp.zeros(g_bias.shape, F32)
    from_pred = t_mm(gp, pred[...])
    for i in range(2):
        piece = t_mm(h_all, prob[:, :, i * 512 : i * 512 + 512].reshape(rows * span, 512))
        for q in range(2):
            g_bias[2 * i + q : 2 * i + q + 1, :] = piece[width : width + 1, 256 * q : 256 * q + 256]
        for d in range(shards):
            first = d * 3 * block + (i + 1) * block
            g_pack[first : first + block, :] = piece[d * block : (d + 1) * block].astype(BF)
    ends_w = t_mm(h_all, prob[:, :, TOK:].reshape(rows * span, 128))
    g_bias[4:5, :128] = ends_w[width : width + 1]
    ends_w = ends_w[:width] + from_pred[:, 640:768]
    for d in range(shards):
        at = slice(d * block, (d + 1) * block)
        g_pack[d * 3 * block : d * 3 * block + block, :] = from_pred[at, :512].astype(BF)
        g_mix[at, :128] = from_pred[at, 512:640].astype(BF)
        g_mix[at, 128:] = ends_w[at].astype(BF)
    for j in range(1, labs):
        part_copy(j).wait_recv()
    total = part[0].astype(F32)
    for j in range(1, labs):
        total = total + came[j].astype(F32)
    g_enc[...] = total.astype(BF)


VOCAB = TOK + 128
UNROLL = 8
STEP = 2
ROOMY = 768


HEADS = 8
EPS = 1e-05
TAPS = 9
GAIN_ROW = 9
STATE = (
    ("n_ffn", 512, F32), ("n_att", 512, F32), ("n_conv", 512, F32), ("n_depth", 512, F32), ("n_out", 512, F32),
    ("scales", 128, F32), ("act", 2048, BF), ("slope", 2048, BF), ("qkv", 1536, BF), ("context", 512, BF),
    ("value", 512, F32), ("gate", 512, F32),
)


def sigmoid(v):
    return 0.5 * jnp.tanh(0.5 * v) + 0.5


def norm_parts(v):
    c = v - jnp.mean(v, axis=1, keepdims=True)
    r = lax.rsqrt(jnp.mean(c * c, axis=1, keepdims=True) + EPS)
    return c * r, r


def norm_back(gy, n, r, gain):
    gg = gy * gain
    gain_grad = jnp.sum(gy * n, axis=0, keepdims=True)
    inner = gg - jnp.mean(gg, axis=1, keepdims=True) - n * jnp.mean(gg * n, axis=1, keepdims=True)
    return r * inner, gain_grad


def rows_of(ref, n, first, count):
    per = ref.shape[0] // n
    return jnp.concatenate([ref[d * per + first : d * per + first + count, :] for d in range(n)], axis=0)


def put_rows(ref, n, first, count, value):
    per = ref.shape[0] // n
    for d in range(n):
        ref[d * per + first : d * per + first + count, :] = value[d * count : (d + 1) * count].astype(ref.dtype)


def own_ends(ints, micro, segs):
    first = lax.axis_index("lab") * micro
    return [scalar_ends(ints, first + m, segs) for m in range(micro)]


def seg_id(position, ends, frames):
    t, row = position % frames, position // frames
    out = seg_of(t, ends[0])
    for m in range(1, len(ends)):
        out = jnp.where(row == m, seg_of(t, ends[m]), out)
    return out + row * len(ends[0])


def shifted(value, step):
    rows = value.shape[0]
    return pltpu.roll(value, (-step) % rows, 0) if step % rows else value


def assemble_small(target, n, per, ds):
    lane = lane_ids((16, 128))
    columns = [jnp.zeros((16, 128), F32) for _ in range(n * ds // 128)]
    for d in range(n):
        piece = jnp.where(lane < ds, target[d * per : d * per + 16, 256:384].astype(F32), 0.0)
        at = d * ds % 128
        columns[d * ds // 128] = columns[d * ds // 128] + (pltpu.roll(piece, at, 1) if at else piece)
    return jnp.concatenate(columns, axis=1)


def split_small(value, d, ds):
    at = d * ds % 128
    piece = value[:, d * ds // 128 * 128 : d * ds // 128 * 128 + 128]
    piece = pltpu.roll(piece, 128 - at, 1) if at else piece
    return jnp.where(lane_ids((16, 128)) < ds, piece, 0.0)


class Sizes:
    def __init__(self, n, ds, ff, qk, pi, jr):
        self.n, self.ds, self.ff, self.qk, self.pi, self.jr = n, ds, ff, qk, pi, jr
        self.rows = (jr + ff, ff + qk, 2 * ds + pi + jr, 3 * jr)
        self.model = n * ds


def head_pair(ref, block, pair):
    at = block * 512 + pair * 128
    return ref[:, at : at + 128]


def forward_pieces(z, x_ref, ints, dims, full, small_ref, st, probs, encoded, enc_proj):
    frames, rows, segs, own_u, labs = dims
    n, micro = z.n, rows // labs
    count = micro * frames
    ends = own_ends(ints, micro, segs)
    ids_r = seg_id(row_ids((count, 128)), ends, frames)
    ids_c = seg_id(lane_ids((count, count)), ends, frames)
    scale_lane = lane_ids((count, 128))

    def norm(v, name, which):
        nv, r = norm_parts(v)
        st[name][...] = nv
        st["scales"][...] = jnp.where(scale_lane == which, r, st["scales"][...])
        return nv * small_ref[GAIN_ROW + which : GAIN_ROW + which + 1, :]

    small_ref[...] = assemble_small(full[0], n, z.rows[0], z.ds)
    st["scales"][...] = jnp.zeros((count, 128), F32)
    x = x_ref[...].reshape(count, z.model).astype(F32)
    ffn_in = norm(x, "n_ffn", 0).astype(BF)
    half = n // 2
    per = z.rows[0]
    for part in range(2):
        w = jnp.concatenate(
            [full[0][d * per + z.jr : d * per + z.jr + z.ff, :] for d in range(part * half, part * half + half)], axis=0
        )
        pre = mm_t(ffn_in, w)
        sg = sigmoid(pre)
        at = slice(part * half * z.ff, (part + 1) * half * z.ff)
        st["act"][:, at] = (pre * sg).astype(BF)
        st["slope"][:, at] = (sg * (1.0 + pre * (1.0 - sg))).astype(BF)
        yield
    after_ffn = x + 0.5 * mm(st["act"][...], rows_of(full[1], n, 0, z.ff))
    att_in = norm(after_ffn, "n_att", 1).astype(BF)
    st["qkv"][...] = mm_t(att_in, rows_of(full[1], n, z.ff, z.qk)).astype(BF)
    yield
    same = ids_r == ids_c
    low_half = lane_ids((count, 128)) < 64
    for pair in range(HEADS // 2):
        q, k, v = (head_pair(st["qkv"], b, pair) for b in range(3))
        total = None
        for side in range(2):
            keep = low_half if side == 0 else ~low_half
            score = mm_t(jnp.where(keep, q, 0), k) * (64 ** -0.5)
            score = jnp.where(same, score, LOW)
            e = jnp.exp(score - jnp.max(score, axis=1, keepdims=True))
            p = (e * (1.0 / jnp.sum(e, axis=1, keepdims=True))).astype(BF)
            probs[2 * pair + side] = p
            part = mm(p, jnp.where(keep, v, 0))
            total = part if total is None else total + part
        st["context"][:, pair * 128 : pair * 128 + 128] = total.astype(BF)
    yield
    after_att = after_ffn + mm(st["context"][...], rows_of(full[2], n, 0, z.ds))
    conv_in = norm(after_att, "n_conv", 2).astype(BF)
    conv_pre = mm_t(conv_in, rows_of(full[2], n, z.ds, z.pi))
    st["value"][...] = conv_pre[:, : z.model]
    st["gate"][...] = sigmoid(conv_pre[:, z.model :])
    depth = []
    for c in range(z.model // 128):
        at = slice(c * 128, c * 128 + 128)
        gated = st["value"][:, at] * st["gate"][:, at]
        total = jnp.zeros((count, 128), F32)
        for j in range(TAPS):
            ok = shifted(ids_r, j - TAPS // 2) == ids_r
            total = total + jnp.where(ok, shifted(gated, j - TAPS // 2), 0.0) * small_ref[j : j + 1, at]
        depth.append(total)
    dn = norm(jnp.concatenate(depth, axis=1), "n_depth", 3)
    conv_act = (dn * sigmoid(dn)).astype(BF)
    after_conv = after_att + mm(conv_act, rows_of(full[2], n, z.ds + z.pi, z.ds))
    out = norm(after_conv, "n_out", 4).astype(BF)
    encoded[...] = out.reshape(encoded.shape)
    enc_proj[...] = mm_t(out, rows_of(full[2], n, 2 * z.ds + z.pi, z.jr)).astype(BF).reshape(enc_proj.shape)
    yield


def backward_pieces(z, g_enc, ints, dims, full, small_ref, st, probs, grads, small_grad, grad_frames):
    frames, rows, segs, own_u, labs = dims
    n, micro = z.n, rows // labs
    count = micro * frames
    ends = own_ends(ints, micro, segs)
    ids_r = seg_id(row_ids((count, 128)), ends, frames)

    def gain(which):
        return small_ref[GAIN_ROW + which : GAIN_ROW + which + 1, :]

    def back(gy, name, which):
        g, gain_grad = norm_back(gy, st[name][...], st["scales"][:, which : which + 1], gain(which))
        small_grad[GAIN_ROW + which : GAIN_ROW + which + 1, :] = gain_grad
        return g

    def normed(name, which):
        return (st[name][...] * gain(which)).astype(BF)

    small_grad[...] = jnp.zeros(small_grad.shape, F32)
    ge = g_enc[...].reshape(count, -1)
    off = 2 * z.ds + z.pi
    put_rows(grads[2], n, off, z.jr, t_mm(ge, normed("n_out", 4)))
    g_conv_sum = back(mm(ge, rows_of(full[2], n, off, z.jr)), "n_out", 4)
    branch = g_conv_sum.astype(BF)
    dn = st["n_depth"][...] * gain(3)
    sg = sigmoid(dn)
    put_rows(grads[2], n, z.ds + z.pi, z.ds, t_mm((dn * sg).astype(BF), branch))
    g_act = mm_t(branch, rows_of(full[2], n, z.ds + z.pi, z.ds))
    g_depth = back(g_act * (sg * (1.0 + dn * (1.0 - sg))), "n_depth", 3)
    yield
    low_a, low_b = [], []
    for c in range(z.model // 128):
        at = slice(c * 128, c * 128 + 128)
        value, gate = st["value"][:, at], st["gate"][:, at]
        gated, gd = value * gate, g_depth[:, at]
        total = jnp.zeros((count, 128), F32)
        for j in range(TAPS):
            step = j - TAPS // 2
            ok = shifted(ids_r, step) == ids_r
            small_grad[j : j + 1, at] = jnp.sum(jnp.where(ok, shifted(gated, step), 0.0) * gd, axis=0, keepdims=True)
            ok = shifted(ids_r, -step) == ids_r
            total = total + jnp.where(ok, shifted(gd, -step), 0.0) * small_ref[j : j + 1, at]
        low_a.append((total * gate).astype(BF))
        low_b.append((total * value * gate * (1.0 - gate)).astype(BF))
    low = jnp.concatenate(low_a + low_b, axis=1)
    put_rows(grads[2], n, z.ds, z.pi, t_mm(low, normed("n_conv", 2)))
    g_att_sum = g_conv_sum + back(mm(low, rows_of(full[2], n, z.ds, z.pi)), "n_conv", 2)
    branch = g_att_sum.astype(BF)
    put_rows(grads[2], n, 0, z.ds, t_mm(st["context"][...], branch))
    g_context = mm_t(branch, rows_of(full[2], n, 0, z.ds)).astype(BF)
    yield
    low_half = lane_ids((count, 128)) < 64
    columns = [[], [], []]
    for pair in range(HEADS // 2):
        q, k, v = (head_pair(st["qkv"], b, pair) for b in range(3))
        gc = g_context[:, pair * 128 : pair * 128 + 128]
        sums = [None, None, None]
        for side in range(2):
            keep = low_half if side == 0 else ~low_half
            p = probs[2 * pair + side]
            gc_h = jnp.where(keep, gc, 0)
            gp = mm_t(gc_h, v)
            pf = p.astype(F32)
            gs = (pf * (gp - jnp.sum(gp * pf, axis=1, keepdims=True))).astype(BF)
            parts = (
                mm(gs, jnp.where(keep, k, 0)) * (64 ** -0.5),
                t_mm(gs, jnp.where(keep, q, 0)) * (64 ** -0.5),
                t_mm(p, gc_h),
            )
            sums = [b if a is None else a + b for a, b in zip(sums, parts)]
        for b in range(3):
            columns[b].append(sums[b].astype(BF))
    g_qkv = jnp.concatenate(columns[0] + columns[1] + columns[2], axis=1)
    yield
    put_rows(grads[1], n, z.ff, z.qk, t_mm(g_qkv, normed("n_att", 1)))
    g_ffn_sum = g_att_sum + back(mm(g_qkv, rows_of(full[1], n, z.ff, z.qk)), "n_att", 1)
    branch = (0.5 * g_ffn_sum).astype(BF)
    put_rows(grads[1], n, 0, z.ff, t_mm(st["act"][...], branch))
    yield
    g_pre = (mm_t(branch, rows_of(full[1], n, 0, z.ff)) * st["slope"][...].astype(F32)).astype(BF)
    put_rows(grads[0], n, z.jr, z.ff, t_mm(g_pre, normed("n_ffn", 0)))
    gx = g_ffn_sum + back(mm(g_pre, rows_of(full[0], n, z.jr, z.ff)), "n_ffn", 0)
    grad_frames[...] = gx.reshape(grad_frames.shape)
    yield


GATHER_SHARES = (0.4, 0.4, 0.2, 0.4)
ORDER = (
    (0, 0, 0), (0, 1, 0), (0, 2, 0), (0, 3, 0), (1, 0, -1), (1, 0, 1), (1, 1, 1), (2, 0, -1), (1, 1, -1), (2, 0, 1),
    (1, 2, -1), (1, 2, 1), (1, 3, 1), (2, 1, 1), (1, 3, -1), (1, 0, 2), (1, 0, -2), (2, 1, -1), (2, 3, 1),
    (2, 3, -1), (1, 1, -2), (2, 0, 2), (1, 1, 2), (2, 0, -2), (1, 2, -2), (1, 2, 2), (1, 3, -2), (1, 3, 2),
    (2, 1, -2), (2, 2, -1), (2, 2, 1), (1, 0, 3), (2, 1, 2), (2, 2, 2), (2, 2, -2), (2, 3, -2), (1, 1, 3),
    (2, 0, -3), (2, 3, 2), (1, 2, 3), (2, 0, 3), (2, 1, -3), (1, 0, 4), (2, 1, 3), (2, 2, -3), (1, 1, 4), (1, 2, 4),
    (2, 0, 4), (1, 3, 3), (2, 2, 3), (2, 1, 4), (3, 0, 0), (4, 0, 0), (1, 3, 4), (4, 1, 0), (2, 2, 4), (2, 3, -3),
    (2, 3, 3), (3, 1, 0), (4, 2, 0), (2, 3, 4), (3, 2, 0), (4, 3, 0), (4, 4, 0), (3, 3, 0),
)


def pass_kernel(
    z, dims, x_ref, lengths, counts, labels, w_in, w_out, w_qkv, w_att, w_pin, w_pout, w_enc, w_pred, w_joint,
    bias_joint, w_depth, gain0, gain1, gain2, gain3, gain4, predictor, bias_out,
    own0, own1, own2, own3, grad_frames, encoded, loss, g_predictor, *rest,
):
    k = len(STATE)
    st = {name: ref for (name, _, _), ref in zip(STATE, rest[:k])}
    probs, small_in, tail, small_ref, small_grad, g_pack = rest[k : k + 6]
    rest = rest[k + 6 :]
    sources, full, bufs, rest = rest[:4], rest[4:8], rest[8:28], rest[28:]
    shared, (ring_recv, x_recv, sems, send, recv) = rest[:-5], rest[-5:]
    n = z.n
    w = Where(n)
    jr, js, ds = z.jr, w_pred.shape[0], z.ds
    job = Joint(z, w, dims, predictor, lengths, counts, labels, bias_out, g_predictor, g_pack, loss, shared)
    def down(value, count):
        rows = value.shape[0]
        return jnp.concatenate([value, jnp.zeros((count - rows,) + value.shape[1:], value.dtype)], 0) if count > rows else value

    def fill(g):
        pred_t = down(w_pred[...], jr)
        if g == 0:
            small_in[...] = jnp.zeros(small_in.shape, F32)
            small_in[:TAPS, :ds] = w_depth[...].astype(F32)
            for i, gain in enumerate((gain0, gain1, gain2, gain3, gain4)):
                small_in[GAIN_ROW + i : GAIN_ROW + i + 1, :ds] = gain[...].astype(F32)
            tail[...] = jnp.zeros(tail.shape, F32)
            tail[:1, :js] = bias_joint[...].astype(F32)
            column = tail[:8, :].T[:jr, :1]
            tail[:8, :] = jnp.zeros((8, 128), F32)
            tail[:js, : w_joint.shape[1] - 1024] = w_joint[:, 1024:].astype(F32)
            tail[...] = jnp.where(lane_ids((jr, 128)) == BIAS_LANE, column, tail[...])
            sources[0][jr:, :] = w_in[...].astype(F32).T.astype(BF)
            sources[0][:jr, 0:128] = pred_t[:, 512:]
            sources[0][:jr, 128:256] = tail[...].astype(BF)
            sources[0][:jr, 256:] = jnp.zeros((jr, 256), BF)
            sources[0][:16, 256:384] = small_in[...].astype(BF)
        elif g == 1:
            sources[1][: z.ff, :] = w_out[...]
            sources[1][z.ff :, :] = w_qkv[...]
        elif g == 2:
            sources[2][:ds, :] = w_att[...]
            sources[2][ds : ds + z.pi, :] = w_pin[...].astype(F32).T.astype(BF)
            sources[2][ds + z.pi : 2 * ds + z.pi, :] = w_pout[...]
            sources[2][2 * ds + z.pi :, :] = down(w_enc[...], jr)
        elif g == 3:
            sources[3][:jr, :] = pred_t[:, :512]
            sources[3][jr : 2 * jr, :] = down(w_joint[:, :512], jr)
            sources[3][2 * jr :, :] = down(w_joint[:, 512:1024], jr)

    parts = [
        Gather(w, sources[i], full[i], z.rows[i], ring_recv.at[i], x_recv.at[i], sems.at[i], GATHER_SHARES[i])
        for i in range(4)
    ]
    w.greet(lambda: fill(0))
    compute = forward_pieces(z, x_ref, lengths, dims, full, small_ref, st, probs, encoded, job.enc_own)
    for what, g, distance in ORDER:
        if what == 0:
            if g:
                fill(g)
            parts[g].begin()
            if g == 3:
                job.prepare()
        elif what == 3:
            parts[g].whole()
        elif what == 4:
            next(compute)
            if g == 4:
                job.share()
        else:
            for d in parts[g].distances(distance):
                (parts[g].take if what == 1 else parts[g].crossed)(d)
    pl.run_scoped(lambda *scratch: job.run(full, *scratch), *joint_scratch(dims, n * jr))
    outs = (own0, own1, own2, own3)

    def finish(*grads):
        packs = list(grads) + [g_pack]
        sums = [
            Scatter(w, packs[g], outs[g], z.rows[g], bufs[5 * g : 5 * g + 5], send.at[g], recv.at[g], SHARES[3 - g])
            for g in (3, 2, 1, 0)
        ]
        pieces = backward_pieces(
            z, job.g_enc, lengths, dims, full, small_ref, st, probs, packs, small_grad, grad_frames
        )

        def work(i):
            for _ in range((0, 2, 2, 1)[i]):
                next(pieces)
            if i == 3:
                for d in range(n):
                    at = d * z.rows[0]
                    packs[0][at : at + jr, :256] = job.g_mix[d * jr : (d + 1) * jr, :]
                    if jr > 32:
                        packs[0][at + 32 : at + jr, 256:] = jnp.zeros((jr - 32, 256), BF)
                    packs[0][at : at + 16, 256:384] = split_small(small_grad[...], d, ds).astype(BF)
                    packs[0][at : at + 16, 384:] = jnp.zeros((16, 128), BF)
                    packs[0][at + 16 : at + 32, 256:] = job.g_bias[...].astype(BF)

        sum_up(sums, work, ORDER_SUMS)

    pl.run_scoped(finish, *[pltpu.VMEM((n * z.rows[g], 512), BF) for g in range(3)])
    job.drain()
    for part in parts:
        part.drain()


def pass_call(z, dims, x, ints, params, predictor, bias_out):
    frames, rows, segs, own_u, labs = dims
    n, micro = z.n, rows // labs
    count, width = micro * frames, n * z.jr
    vm, sm = (pl.BlockSpec(memory_space=m) for m in (pltpu.VMEM, pltpu.SMEM))
    shape = jax.ShapeDtypeStruct
    outs = [shape((r, 512), BF) for r in z.rows]
    outs += [shape((micro, frames, z.model), F32), shape((micro, frames, z.model), BF), shape((8, 128), F32)]
    outs += [shape((rows * segs * own_u, predictor.shape[-1]), F32)]
    scratch = [pltpu.VMEM((count, lanes), dtype) for _, lanes, dtype in STATE]
    scratch += [pltpu.VMEM((HEADS, count, count), BF), pltpu.VMEM((16, 128), F32), pltpu.VMEM((z.jr, 128), F32)]
    scratch += [pltpu.VMEM((16, z.model), F32)] * 2 + [pltpu.VMEM((3 * width, 512), BF)]
    scratch += [pltpu.VMEM((r, 512), BF) for r in z.rows] + [pltpu.VMEM((n * r, 512), BF) for r in z.rows]
    for g, r in enumerate(z.rows):
        scratch += scatter_scratch(n, r, 512, SHARES[3 - g])
    scratch += joint_shared(dims, width)
    scratch += [pltpu.SemaphoreType.DMA((4, n - 1))] * 2 + [pltpu.SemaphoreType.DMA((4, 5))] + scatter_sems(n, 4)
    return pl.pallas_call(
        functools.partial(pass_kernel, z, dims),
        out_shape=outs,
        in_specs=[vm] + [sm] * 3 + [vm] * (len(params) + 2),
        out_specs=[vm] * len(outs),
        scratch_shapes=scratch,
        compiler_params=pltpu.CompilerParams(collective_id=0, has_side_effects=True, vmem_limit_bytes=62 * 2**20),
    )(x, *ints, *params, predictor, bias_out)


SHARES = (0.15, 0.35, 0.2, 0.15)
ORDER_SUMS = (
    (0, 0, 0), (0, 1, 0), (0, 2, 0), (1, 0, 0), (3, 0, 0), (2, 0, 1), (0, 3, 0), (1, 1, 0), (3, 1, 0), (2, 1, 1),
    (2, 0, 2), (1, 2, 0), (3, 2, 0), (2, 2, 1), (2, 1, 2), (1, 3, 0), (3, 3, 0), (2, 3, 1), (3, 0, 1), (2, 0, 3),
    (2, 2, 2), (2, 1, 3), (2, 3, 2), (3, 0, 2), (3, 1, 1), (2, 0, 4), (2, 2, 3), (2, 1, 4), (3, 1, 2), (3, 2, 1),
    (2, 3, 3), (3, 0, 3), (2, 0, 5), (3, 3, 1), (2, 2, 4), (2, 1, 5), (3, 2, 2), (3, 1, 3), (2, 0, 6), (3, 3, 2),
    (2, 3, 4), (2, 1, 6), (3, 0, 4), (2, 2, 5), (3, 2, 3), (3, 1, 4), (3, 3, 3), (2, 1, 7), (2, 0, 7), (2, 3, 5),
    (3, 2, 4), (3, 1, 5), (3, 3, 4), (2, 2, 6), (3, 0, 5), (3, 2, 5), (3, 3, 5), (3, 1, 6), (2, 2, 7), (2, 3, 6),
    (3, 0, 6), (3, 2, 6), (3, 3, 6), (3, 1, 7), (2, 3, 7), (3, 0, 7), (3, 2, 7), (3, 3, 7),
)


def unpack_kernel(z, dims, js, own0, own1, own2, own3, grads, encoded, loss, g_predictor, *outs):
    frames, rows, segs, own_u, labs = dims
    ds, ff, pi, jr = z.ds, z.ff, z.pi, z.jr
    (
        loss_o, enc_o, grads_o, pred_o, gg0, g_in, g_out, gg1, g_qkv, g_att, gg2, g_pin, g_depth, gg3, g_pout, gg4,
        g_enc, g_pred, g_bias, g_joint, g_bias_out,
    ) = outs
    hit = (row_ids((128, rows)) == lane_ids((128, rows)) * own_u).astype(F32)
    loss_o[...] = lax.dot_general(
        loss[...], hit, (((1,), (0,)), ((), ())), precision=lax.Precision.HIGHEST, preferred_element_type=F32
    )[:segs]
    enc_o[...] = encoded[...]
    grads_o[...] = grads[...]
    for r in range(rows):
        for s in range(segs):
            first = (r * segs + s) * own_u
            pred_o[r, s] = g_predictor[first : first + own_u, :]
    small = own0[:32, 256:].astype(F32)
    for i, out in enumerate((gg0, gg1, gg2, gg3, gg4)):
        out[...] = small[GAIN_ROW + i : GAIN_ROW + i + 1, :ds]
    g_depth[...] = small[:TAPS, :ds]
    for i in range(4):
        g_bias_out[256 * i : 256 * i + 256] = small[16 + i, :]
    g_bias_out[1024:] = small[20, : g_bias_out.shape[0] - 1024]
    g_in[...] = own0[jr:, :].astype(F32).T
    g_out[...] = own1[:ff, :].astype(F32)
    g_qkv[...] = own1[ff:, :].astype(F32)
    g_att[...] = own2[:ds, :].astype(F32)
    g_pin[...] = own2[ds : ds + pi, :].astype(F32).T
    g_pout[...] = own2[ds + pi : 2 * ds + pi, :].astype(F32)
    g_enc[...] = own2[2 * ds + pi :, :].astype(F32)[:js]
    g_pred[:, :512] = own3[:jr, :].astype(F32)[:js]
    g_pred[:, 512:] = own0[:jr, :128].astype(F32)[:js]
    tail = own0[:jr, 128:256].astype(F32)
    wide = jnp.concatenate([tail, jnp.zeros((128 - jr, 128), F32)], axis=0) if jr < 128 else tail
    g_bias[...] = wide.T[BIAS_LANE : BIAS_LANE + 1, :js]
    g_joint[:, :512] = own3[jr : 2 * jr, :].astype(F32)[:js]
    g_joint[:, 512:1024] = own3[2 * jr :, :].astype(F32)[:js]
    g_joint[:, 1024:] = tail[:js, : g_joint.shape[1] - 1024]


def unpack_call(z, dims, js, out_width, own, grads, encoded, loss, g_predictor):
    frames, rows, segs, own_u, labs = dims
    shape = jax.ShapeDtypeStruct
    row = shape((1, z.ds), F32)
    line, features = z.model, g_predictor.shape[1]
    outs = [
        shape((segs, rows), F32), shape(encoded.shape, BF), shape(grads.shape, F32),
        shape((rows, segs, own_u, features), F32), row, shape((line, z.ff), F32), shape((z.ff, line), F32), row,
        shape((z.qk, line), F32), shape((z.ds, line), F32), row, shape((line, z.pi), F32), shape((TAPS, z.ds), F32),
        row, shape((z.ds, line), F32), row, shape((js, line), F32), shape((js, features), F32), shape((1, js), F32),
        shape((js, out_width), F32), shape((out_width,), F32),
    ]
    vm = pl.BlockSpec(memory_space=pltpu.VMEM)
    return pl.pallas_call(
        functools.partial(unpack_kernel, z, dims, js),
        out_shape=outs,
        in_specs=[vm] * 8,
        out_specs=[vm] * len(outs),
        compiler_params=pltpu.CompilerParams(vmem_limit_bytes=60 * 2**20),
    )(*own, grads, encoded, loss, g_predictor)

def local(
    frames_in, predictor, seg_lengths, label_counts, label_ids, gain_ffn, w_ffn_in, w_ffn_out, gain_att, w_qkv,
    w_att_out, gain_conv, w_point_in, w_depth, gain_depth, w_point_out, gain_out, w_enc, w_pred, bias_joint,
    w_joint_out, bias_out,
):
    n, labs = lax.axis_size("dp"), lax.axis_size("lab")
    micro, frames, model = frames_in.shape
    rows, segs, own_u, joint = predictor.shape
    ds, js = model // n, w_pred.shape[1]
    jr = max(-(-js // TILE), 2) * TILE
    z = Sizes(n, ds, w_ffn_in.shape[1], w_qkv.shape[1], w_point_in.shape[1], jr)
    dims = (frames, rows, segs, own_u, labs)
    lengths, counts, labels = seg_lengths.T, label_counts.T, label_ids.transpose(1, 2, 0)
    gains = [g[None] for g in (gain_ffn, gain_att, gain_conv, gain_depth, gain_out)]
    params = (
        w_ffn_in, w_ffn_out, w_qkv.T, w_att_out, w_point_in, w_point_out, w_enc.T, w_pred.T, w_joint_out,
        bias_joint[None], w_depth, *gains,
    )
    *own, grad_frames, encoded, loss, g_predictor = pass_call(
        z, dims, frames_in, (lengths, counts, labels), params, predictor, bias_out
    )
    (
        loss, encoded, grad_frames, g_predictor, gg0, g_in, g_out, gg1, g_qkv, g_att, gg2, g_pin, g_depth, gg3, g_pout,
        gg4, g_enc, g_pred, g_bias, g_joint, g_bias_out,
    ) = unpack_call(z, dims, js, bias_out.shape[0], own, grad_frames, encoded, loss, g_predictor)
    return (
        loss.T, encoded, grad_frames, g_predictor, gg0[0], g_in, g_out, gg1[0], g_qkv.T, g_att, gg2[0], g_pin, g_depth,
        gg3[0], g_pout, gg4[0], g_enc.T, g_pred.T, g_bias[0], g_joint, g_bias_out,
    )


def solution(mesh):
    rows, whole = P(("dp", "lab"), None, None), P()
    predictor, columns, lines, vector = P("dp", None, "lab", None), P(None, "dp"), P("dp", None), P("dp")
    params = (
        vector, columns, lines, vector, columns, lines, vector, columns, columns, vector, lines, vector, columns,
        columns, vector, lines, whole,
    )
    return jax.shard_map(
        local,
        mesh=mesh,
        in_specs=(rows, predictor, lines, lines, P("dp", None, "lab")) + params,
        out_specs=(lines, rows, rows, predictor) + params,
        check_vma=False,
    )
```
